128 devices in a mesh: fsdp: 16 (over x, z), context: 4 (over y), tensor: 2 (over core).
Axes of the slice: x: 4, y: 4, z: 4, core: 2. Of those that a mesh axis runs over, the one named last changes fastest.
Arguments:
- tokens: bfloat16 [32, 1024, 1024], P('fsdp', 'context'), may hold values from -6 to 6
- segments: int32 [32, 1024], P('fsdp'), may hold values from 0 to 6, as said below
- routes: int32 [32, 1024, 8], P('fsdp', 'context'), may hold values from 0 to 31, all different within a row
- attention_gain: bfloat16 [1024], P('fsdp'), may hold values from 0.5 to 1.5
- w_query: bfloat16 [1024, 1024], P('fsdp', 'tensor'), may hold values from -0.1875 to 0.1875
- w_key: bfloat16 [1024, 512], P('fsdp', 'tensor'), may hold values from -0.1875 to 0.1875
- w_value: bfloat16 [1024, 512], P('fsdp', 'tensor'), may hold values from -0.1875 to 0.1875
- w_out: bfloat16 [1024, 1024], P('fsdp', 'tensor'), may hold values from -0.75 to 0.75
- query_gain: bfloat16 [64], P('fsdp'), may hold values from 0.75 to 1.25
- key_gain: bfloat16 [64], P('fsdp'), may hold values from 0.75 to 1.25
- feedforward_gain: bfloat16 [1024], P('fsdp'), may hold values from 0.5 to 1.5
- router: bfloat16 [1024, 32], P('fsdp'), may hold values from -0.09375 to 0.09375
- w_gate: bfloat16 [32, 1024, 512], P('fsdp', None, 'tensor'), may hold values from -0.1875 to 0.1875
- w_up: bfloat16 [32, 1024, 512], P('fsdp', None, 'tensor'), may hold values from -0.1875 to 0.1875
- w_down: bfloat16 [32, 1024, 512], P('fsdp', None, 'tensor'), may hold values from -1 to 1
- cotangent: bfloat16 [32, 1024, 1024], P('fsdp', 'context'), may hold values from -6 to 6
Outputs:
- block_output: bfloat16 [32, 1024, 1024], P('fsdp', 'context')
- grad_tokens: float32 [32, 1024, 1024], P('fsdp', 'context')
- grad_attention_gain: float32 [1024], P('fsdp')
- grad_query: float32 [1024, 1024], P('fsdp', 'tensor')
- grad_key: float32 [1024, 512], P('fsdp', 'tensor')
- grad_value: float32 [1024, 512], P('fsdp', 'tensor')
- grad_out: float32 [1024, 1024], P('fsdp', 'tensor')
- grad_query_gain: float32 [64], P('fsdp')
- grad_key_gain: float32 [64], P('fsdp')
- grad_feedforward_gain: float32 [1024], P('fsdp')
- grad_router: float32 [1024, 32], P('fsdp')
- grad_gate: float32 [32, 1024, 512], P('fsdp', 'context', 'tensor')
- grad_up: float32 [32, 1024, 512], P('fsdp', 'context', 'tensor')
- grad_down: float32 [32, 1024, 512], P('fsdp', 'context', 'tensor')
The draws below stay inside these ranges and needn't reach their ends.
Inputs may be any that keep to these rules, and one draw needn't show every extreme that they name: `segments`: within a sequence the numbers never fall and may skip; each sequence starts with 0 and ends with 6. Of the 2 sequences of one index of fsdp, one has a document that covers every position from 127 to 896.
All inputs are finite; a program needn't handle non-finite values.
Results may differ from the reference program's by a relative error of at most 0.02.
Values may be sent and summed in bfloat16 or wider, within the bound.
No kernel may reach another device: no remote copies, remote signals or barrier semaphores. Data moves between devices by JAX's collectives and lax.ppermute only.
A program may use at most 320 MiB of HBM per device.

```python
import jax
import jax.numpy as jnp
from jax import lax

D = 1024
FF = 512
HQ = 16
HK = 8
HD = 64
EXPERTS = 32
TOPK = 8
SEQ = 1024
SEQ_DEV = 2
SEQS = 32
GROUP = 2
CAP = 160
EDGE = 128
N_FSDP = 16
N_CONTEXT = 4


def draw_segments(key, part):
    key = jax.random.fold_in(key, 7)
    first, second, third, fourth = jax.random.split(key, 4)
    free_cuts = jax.random.randint(first, (SEQS, 6), 1, SEQ)
    early_cuts = jax.random.randint(second, (SEQS, 3), 1, EDGE)
    late_cuts = jax.random.randint(third, (SEQS, 3), SEQ - EDGE + 1, SEQ)
    chosen = jax.random.randint(fourth, (SEQS // SEQ_DEV, 1), 0, SEQ_DEV)
    spanning = (jnp.arange(SEQ_DEV)[None, :] == chosen).reshape(SEQS, 1)
    cuts = jnp.where(spanning, jnp.concatenate([early_cuts, late_cuts], axis=1), free_cuts)
    positions = jnp.arange(SEQ)
    return jnp.sum((cuts[:, None, :] <= positions[None, :, None]).astype(jnp.int32), axis=-1).astype(jnp.int32)


def shard_levels(rng, dims, cuts, smallest, top_value):
    def one(axis_at, blocks):
        heights = jax.random.uniform(jax.random.fold_in(jax.random.fold_in(rng, 6), axis_at), (blocks,), jnp.float32, smallest / len(cuts), top_value / len(cuts))
        return jnp.repeat(jnp.exp(heights), dims[axis_at] // blocks).reshape((-1,) + (1,) * (len(dims) - axis_at - 1))

    factor_of = one(*cuts[0])
    for cut in cuts[1:]:
        factor_of = factor_of * one(*cut)
    return factor_of


def picks_of(stream_key, rows, number_of, top, lift):
    order = jax.random.permutation(jax.random.fold_in(stream_key, 1), number_of)
    favour = order
    for power in range(3):
        favour = favour * favour // number_of
    favour = favour * lift // number_of
    chance = jax.random.randint(jax.random.fold_in(stream_key, 2), (rows, number_of), 0, 4096) + favour
    holders = jax.random.permutation(jax.random.fold_in(stream_key, 3), rows)[jnp.arange(number_of) % rows]
    chance = jnp.where(jnp.arange(rows)[:, None] == holders[None, :], 1 << 14, chance)
    priority = chance * number_of + jnp.arange(number_of)
    return lax.top_k(priority.astype(jnp.int32), top)[1].astype(jnp.int32)


def normal_values(own_key, shape, width, reach, cuts=(), held_as=jnp.bfloat16):
    values = width * jax.random.normal(own_key, shape, jnp.float32)
    if cuts:
        values = values * shard_levels(own_key, shape, cuts, -0.22, 0.18)
    return jnp.clip(values, -reach, reach).astype(held_as)


def setup_inputs(seed: int = 0) -> dict:
    streams_of = jax.random.split(jax.random.key(seed), 17)
    tokens = normal_values(streams_of[0], (SEQS, SEQ, D), 1.0, 6.0, ((0, 16), (1, 4)))
    segments = draw_segments(jax.random.fold_in(streams_of[16], 71), 0)
    routes = picks_of(streams_of[2], SEQS * SEQ, EXPERTS, TOPK, 2048).reshape((SEQS, SEQ, TOPK))
    attention_gain = jnp.clip(1.0 + 0.1 * jax.random.normal(streams_of[3], (D,), jnp.float32), 0.5, 1.5).astype(jnp.bfloat16)
    w_query = normal_values(streams_of[4], (D, HQ * HD), D ** -0.5, 0.1875, ((0, 16), (1, 2)))
    w_key = normal_values(streams_of[5], (D, HK * HD), D ** -0.5, 0.1875, ((0, 16), (1, 2)))
    w_value = normal_values(streams_of[6], (D, HK * HD), D ** -0.5, 0.1875, ((0, 16), (1, 2)))
    w_out = normal_values(streams_of[7], (D, HQ * HD), (HQ * HD // 16) ** -0.5, 0.75, ((0, 16), (1, 2)))
    query_gain = jnp.clip(0.75 + 0.5 * jax.random.uniform(streams_of[8], (HD,), jnp.float32) ** shard_levels(streams_of[8], (HD,), ((0, 16),), -0.2, 0.2), 0.75, 1.25).astype(jnp.bfloat16)
    key_gain = jnp.clip(0.75 + 0.5 * jax.random.uniform(streams_of[9], (HD,), jnp.float32) ** shard_levels(streams_of[9], (HD,), ((0, 16),), -0.2, 0.2), 0.75, 1.25).astype(jnp.bfloat16)
    feedforward_gain = jnp.clip(1.0 + 0.1 * jax.random.normal(streams_of[10], (D,), jnp.float32), 0.5, 1.5).astype(jnp.bfloat16)
    router = normal_values(streams_of[11], (D, EXPERTS), (4 * D) ** -0.5, 0.09375, ((0, 16),))
    w_gate = normal_values(streams_of[12], (EXPERTS, D, FF), D ** -0.5, 0.1875, ((0, 16), (2, 2)))
    w_up = normal_values(streams_of[13], (EXPERTS, D, FF), D ** -0.5, 0.1875, ((0, 16), (2, 2)))
    w_down = normal_values(streams_of[14], (EXPERTS, D, FF), (FF // 16) ** -0.5, 1.0, ((0, 16), (2, 2)))
    cotangent = normal_values(streams_of[15], (SEQS, SEQ, D), 1.0, 6.0, ((0, 16), (1, 4)))
    return dict(tokens=tokens, segments=segments, routes=routes, attention_gain=attention_gain, w_query=w_query, w_key=w_key, w_value=w_value, w_out=w_out, query_gain=query_gain, key_gain=key_gain, feedforward_gain=feedforward_gain, router=router, w_gate=w_gate, w_up=w_up, w_down=w_down, cotangent=cotangent)


@jax.custom_vjp
def low(v):
    return lax.optimization_barrier(v.astype(jnp.bfloat16)).astype(jnp.float32)

@jax.custom_vjp
def low_back(v):
    return v

def low_keep(v):
    return (low(v), None)

def low_pass(kept, grad):
    return (grad,)

def back_keep(v):
    return (v, None)

def back_low(kept, grad):
    return (low(grad),)
low.defvjp(low_keep, low_pass)
low_back.defvjp(back_keep, back_low)
epsilon = 1e-06
negative = -1e+30
highest = lax.Precision.HIGHEST

def rms_scale(values, gain):
    return values * lax.rsqrt(lax.optimization_barrier(jnp.mean(values * values, axis=-1, keepdims=True)) + epsilon) * gain

def rotate_half(values):
    middle = values.shape[-1] // 2
    return jnp.concatenate([-values[..., middle:], values[..., :middle]], axis=-1)

def rotary_tables():
    middle = HD // 2
    inverse = 10000.0 ** (-(2.0 * jnp.arange(middle, dtype=jnp.float32) / HD))
    angles = jnp.arange(SEQ, dtype=jnp.float32)[:, None] * inverse[None, :]
    angles = jnp.concatenate([angles, angles], axis=-1)
    return (jnp.cos(angles)[:, None, :], jnp.sin(angles)[:, None, :])

def rotary(values, cosine, sine):
    return values * cosine + rotate_half(values) * sine

def attend(inputs):
    queries, keys, values, segment_row = inputs
    raw = jnp.einsum('qgjd,kgd->gjqk', queries, keys, precision=highest)
    scores = low_back(raw * HD ** (-0.5))
    same_doc = segment_row[:, None] == segment_row[None, :]
    scores = jnp.where(same_doc[None, None], scores, negative)
    weights = low(jax.nn.softmax(scores, axis=-1))
    mixed = jnp.einsum('gjqk,kgd->qgjd', weights, values, precision=highest)
    return mixed.reshape(SEQ, HQ * HD)

def slot_tables(routes):
    groups = N_FSDP * N_CONTEXT
    local_rows = SEQ // N_CONTEXT
    group_rows = SEQ_DEV * local_rows
    places = jnp.arange(SEQS * SEQ, dtype=jnp.int32).reshape(N_FSDP, SEQ_DEV, N_CONTEXT, local_rows)
    places = places.transpose(0, 2, 1, 3).reshape(groups, group_rows)
    picked = routes.reshape(N_FSDP, SEQ_DEV, N_CONTEXT, local_rows, TOPK).transpose(0, 2, 1, 3, 4)
    picked = picked.reshape(groups, group_rows * TOPK)
    pair_index = (places[:, :, None] * TOPK + jnp.arange(TOPK, dtype=jnp.int32)[None, None, :]).reshape(groups, group_rows * TOPK)
    token_index = jnp.repeat(places, TOPK, axis=1)
    onehot = (picked[:, :, None] == jnp.arange(EXPERTS, dtype=jnp.int32)[None, None, :]).astype(jnp.int32)
    place_in = lax.optimization_barrier(jnp.sum(jnp.cumsum(onehot, axis=1) * onehot, axis=-1)) - 1
    column = jnp.arange(groups, dtype=jnp.int32)[:, None] * CAP + place_in
    target = jnp.where(place_in < CAP, picked * (groups * CAP) + column, EXPERTS * groups * CAP).astype(jnp.int32)
    slot_token = jnp.full((EXPERTS * groups * CAP,), SEQS * SEQ, jnp.int32)
    slot_token = slot_token.at[target.reshape(-1)].set(token_index.reshape(-1).astype(jnp.int32), mode='drop')
    slot_pair = jnp.full((EXPERTS * groups * CAP,), SEQS * SEQ * TOPK, jnp.int32)
    slot_pair = slot_pair.at[target.reshape(-1)].set(pair_index.reshape(-1).astype(jnp.int32), mode='drop')
    return (slot_token.reshape(EXPERTS, groups * CAP), slot_pair.reshape(EXPERTS, groups * CAP))

def expert_rows(padded):

    def apply(inputs):
        gate_weight, up_weight, down_weight, token_row, gate_row = inputs
        rows_in = low_back(padded[token_row])
        gate_value = low_back(jnp.dot(rows_in, gate_weight, precision=highest))
        up_value = low_back(jnp.dot(rows_in, up_weight, precision=highest))
        activation = low(jax.nn.silu(gate_value) * up_value)
        result = low(low_back(jnp.dot(activation, down_weight.T, precision=highest)))
        return result * gate_row[:, None]
    return apply

def forward(tokens, attention_gain, w_query, w_key, w_value, w_out, query_gain, key_gain, feedforward_gain, router, w_gate, w_up, w_down, segments, routes, slot_token, slot_pair):
    cosine, sine = rotary_tables()
    normed1 = low(rms_scale(tokens, attention_gain))
    query_proj = low_back(jnp.dot(normed1, w_query, precision=highest)).reshape(SEQS, SEQ, HQ, HD)
    key_proj = low_back(jnp.dot(normed1, w_key, precision=highest)).reshape(SEQS, SEQ, HK, HD)
    value_b = low(low_back(jnp.dot(normed1, w_value, precision=highest))).reshape(SEQS, SEQ, HK, HD)
    query_b = low(rotary(rms_scale(query_proj, query_gain), cosine, sine)).reshape(SEQS, SEQ, HK, GROUP, HD)
    key_b = low(rotary(rms_scale(key_proj, key_gain), cosine, sine))
    attended = lax.map(jax.checkpoint(attend), (query_b, key_b, value_b, segments))
    attended = low(low_back(attended))
    branch = low_back(jnp.einsum('sqh,dh->sqd', attended, w_out, precision=highest))
    hidden1 = tokens + branch
    normed2 = low(rms_scale(hidden1, feedforward_gain))
    logits = jnp.dot(normed2, router, precision=highest)
    probs = jax.nn.softmax(logits, axis=-1)
    chosen = jnp.take_along_axis(probs, routes, axis=-1)
    gates = chosen / lax.optimization_barrier(jnp.sum(chosen, axis=-1, keepdims=True))
    flat = normed2.reshape(SEQS * SEQ, D)
    padded = jnp.concatenate([flat, jnp.zeros((1, D), flat.dtype)], axis=0)
    gate_pad = jnp.concatenate([gates.reshape(-1), jnp.zeros((1,), gates.dtype)], axis=0)
    slot_gates = gate_pad[slot_pair]
    contrib = lax.map(jax.checkpoint(expert_rows(padded)), (w_gate, w_up, w_down, slot_token, slot_gates))
    mixed = jnp.zeros((SEQS * SEQ + 1, D), flat.dtype).at[slot_token.reshape(-1)].add(contrib.reshape(-1, D))
    return hidden1 + mixed[:SEQS * SEQ].reshape(SEQS, SEQ, D)

def reference(tokens, segments, routes, attention_gain, w_query, w_key, w_value, w_out, query_gain, key_gain, feedforward_gain, router, w_gate, w_up, w_down, cotangent):
    slot_token, slot_pair = slot_tables(routes)
    floats = tuple((item.astype(jnp.float32) for item in (tokens, attention_gain, w_query, w_key, w_value, w_out, query_gain, key_gain, feedforward_gain, router, w_gate, w_up, w_down)))

    def run(*values):
        return forward(*values, segments, routes, slot_token, slot_pair)
    result, pullback = jax.vjp(run, *floats)
    grads = pullback(cotangent.astype(jnp.float32))
    return (result.astype(jnp.bfloat16), grads[0], grads[1], grads[2], grads[3], grads[4], grads[5], grads[6], grads[7], grads[8], grads[9], grads[10], grads[11], grads[12])
```

```python
import functools

import jax
import jax.numpy as jnp
import numpy as np
from jax import lax
from jax.experimental import pallas as pl
from jax.experimental.pallas import tpu as pltpu
from jax.sharding import PartitionSpec as P

HD = 64
EXPERTS = 32
TOPK = 8
SEQ = 1024
D = 1024
ROWS = 512
HALF = 256
CAP = 160
TILE = 384
SLOTS = 768
PAD = 272
N_FSDP = 16
N_CONTEXT = 4
EPS = 1e-06
NEGATIVE = -1e30
VMEM = 60 * 1024 * 1024
BF = jnp.bfloat16
F32 = jnp.float32
NT = (((1,), (1,)), ((), ()))
TN = (((0,), (0,)), ((), ()))


def dot(a, b):
    return jnp.dot(a, b, preferred_element_type=F32)


def dot_nt(a, b):
    return lax.dot_general(a, b, NT, preferred_element_type=F32)


def dot_tn(a, b):
    return lax.dot_general(a, b, TN, preferred_element_type=F32)


def split(v):
    high = v.astype(BF)
    return high, (v - high.astype(F32)).astype(BF)


def params(grid_dims):
    return pltpu.CompilerParams(
        dimension_semantics=("arbitrary",) * grid_dims, vmem_limit_bytes=VMEM
    )


def cost(flops, moved):
    return pl.CostEstimate(flops=flops, bytes_accessed=moved, transcendentals=0)


def head_mean(v):
    rows = lax.broadcasted_iota(jnp.int32, (128, 128), 0) // HD
    cols = lax.broadcasted_iota(jnp.int32, (128, 128), 1) // HD
    block = jnp.where(rows == cols, 1.0, 0.0).astype(BF)
    high, low = split(v)
    return (dot(high, block) + dot(low, block)) * (1.0 / HD)


def swap_halves(v):
    lane = lax.broadcasted_iota(jnp.int32, v.shape, 1) % HD
    return jnp.where(lane < HD // 2, pltpu.roll(v, 96, 1), pltpu.roll(v, 32, 1))


def rot(v, cosine, sine):
    return v * cosine + swap_halves(v) * sine


def rot_back(v, cosine, sine):
    return v * cosine - swap_halves(v) * sine


def rotary_tables():
    middle = HD // 2
    inverse = 10000.0 ** (-(2.0 * np.arange(middle, dtype=np.float64) / HD))
    inverse = inverse.astype(np.float32)
    angles = np.arange(SEQ, dtype=np.float32)[:, None] * inverse[None, :]
    cosine = np.cos(angles.astype(np.float64)).astype(np.float32)
    sine = np.sin(angles.astype(np.float64)).astype(np.float32)
    cosine = np.concatenate([cosine] * 4, axis=1)
    sine = np.concatenate([-sine, sine, -sine, sine], axis=1)
    return jnp.asarray(cosine), jnp.asarray(sine)


def project_kernel(
    place, x, w, gain, q_gain, k_gain, cosine, sine, normed, k_proj, k_b, v_b, q_proj, q_b
):
    values = x[0].astype(F32)
    factor = lax.rsqrt(jnp.mean(values * values, axis=1, keepdims=True) + EPS)
    rows = (values * factor * gain[...]).astype(BF)
    normed[0] = rows
    cos, sin = cosine[...], sine[...]
    keys = dot(rows, w[:, 512:768])
    k_proj[0] = keys
    v_b[0] = dot(rows, w[:, 768:1024]).astype(BF)
    for block in range(2):
        at = slice(block * 128, block * 128 + 128)
        head = keys[:, at]
        scaled = head * lax.rsqrt(head_mean(head * head) + EPS) * k_gain[...]
        k_b[0, :, at] = rot(scaled, cos, sin).astype(BF)

    @pl.when(pl.program_id(1) == place[0])
    def _():
        queries = dot(rows, w[:, 0:512])
        q_proj[0] = queries
        for block in range(4):
            at = slice(block * 128, block * 128 + 128)
            head = queries[:, at]
            scaled = head * lax.rsqrt(head_mean(head * head) + EPS) * q_gain[...]
            q_b[0, :, at] = (rot(scaled, cos, sin).astype(BF).astype(F32) * 0.125).astype(BF)


def project(place, tokens_all, weights, gain, q_gain, k_gain, cosine, sine):
    row = lambda s, c, r: (0, 0)
    whole = lambda s, c, r: (s, c, 0)
    own = lambda s, c, r: (s, 0, 0)
    return pl.pallas_call(
        project_kernel,
        grid_spec=pltpu.PrefetchScalarGridSpec(
            num_scalar_prefetch=1,
            grid=(2, 4),
            in_specs=[
                pl.BlockSpec((1, HALF, D), lambda s, c, r: (c * 2 + s, 0, 0)),
                pl.BlockSpec((D, 1024), row),
                pl.BlockSpec((1, D), row),
                pl.BlockSpec((1, 128), row),
                pl.BlockSpec((1, 128), row),
                pl.BlockSpec((HALF, 128), lambda s, c, r: (c, 0)),
                pl.BlockSpec((HALF, 128), lambda s, c, r: (c, 0)),
            ],
            out_specs=[
                pl.BlockSpec((1, HALF, D), whole),
                pl.BlockSpec((1, HALF, 256), whole),
                pl.BlockSpec((1, HALF, 256), whole),
                pl.BlockSpec((1, HALF, 256), whole),
                pl.BlockSpec((1, HALF, 512), own),
                pl.BlockSpec((1, HALF, 512), own),
            ],
        ),
        out_shape=[
            jax.ShapeDtypeStruct((2, SEQ, D), BF),
            jax.ShapeDtypeStruct((2, SEQ, 256), F32),
            jax.ShapeDtypeStruct((2, SEQ, 256), BF),
            jax.ShapeDtypeStruct((2, SEQ, 256), BF),
            jax.ShapeDtypeStruct((2, HALF, 512), F32),
            jax.ShapeDtypeStruct((2, HALF, 512), BF),
        ],
        compiler_params=params(2),
        cost_estimate=cost(5 * 10**9, 20 * 10**6),
        name="project",
    )(place, tokens_all, weights, gain, q_gain, k_gain, cosine, sine)


def place_head(v, target, source):
    moved = v if target == source else pltpu.roll(v, HD, 1)
    lane = lax.broadcasted_iota(jnp.int32, v.shape, 1) // HD
    return jnp.where(lane == target, moved, jnp.zeros_like(moved))


def attend_kernel(place, q, k, v, seg_q, seg_k, w_out, attended, branch):
    mask = jnp.where(seg_q[0] == seg_k[0], 0.0, NEGATIVE)
    keys = k[0]
    values = jnp.concatenate([v[0], jnp.ones((SEQ, 128), BF)], axis=1)
    for block in range(2):
        heads = q[0, :, block * 128 : block * 128 + 128].astype(F32)
        mixed = jnp.zeros((HALF, 128), F32)
        for j in range(2):
            query = place_head(heads, block, j).astype(BF)
            weights = jnp.exp(dot_nt(query, keys) + mask).astype(BF)
            summed = dot(weights, values)
            mixed = mixed + place_head(summed[:, :128] / summed[:, 128:], j, block)
        attended[:, block * 128 : block * 128 + 128] = mixed.astype(BF)
    part = dot_nt(attended[...], w_out[...])

    @pl.when(pl.program_id(0) == 0)
    def _():
        branch[...] = part

    @pl.when(pl.program_id(0) != 0)
    def _():
        branch[...] += part


def attend(seq, q_b, k_b, v_b, seg_q, seg_k, w_out):
    return pl.pallas_call(
        attend_kernel,
        grid_spec=pltpu.PrefetchScalarGridSpec(
            num_scalar_prefetch=1,
            grid=(2,),
            in_specs=[
                pl.BlockSpec((1, HALF, 256), lambda p, r: (r[0], 0, p)),
                pl.BlockSpec((1, SEQ, 128), lambda p, r: (r[0], 0, p)),
                pl.BlockSpec((1, SEQ, 128), lambda p, r: (r[0], 0, p)),
                pl.BlockSpec((1, HALF, 1), lambda p, r: (r[0], 0, 0)),
                pl.BlockSpec((1, 1, SEQ), lambda p, r: (r[0], 0, 0)),
                pl.BlockSpec((D, 256), lambda p, r: (0, p)),
            ],
            out_specs=[
                pl.BlockSpec((HALF, 256), lambda p, r: (0, p)),
                pl.BlockSpec((HALF, D), lambda p, r: (0, 0)),
            ],
        ),
        out_shape=[
            jax.ShapeDtypeStruct((HALF, 512), BF),
            jax.ShapeDtypeStruct((HALF, D), F32),
        ],
        compiler_params=params(1),
        cost_estimate=cost(8 * 10**9, 4 * 10**6),
        name="attend",
    )(seq, q_b, k_b, v_b, seg_q, seg_k, w_out)


def experts_to_rows(table):
    return jnp.concatenate([table[8 * k : 8 * k + 8] for k in range(4)], axis=1)


def rows_to_experts(rows):
    return jnp.concatenate([rows[:, 256 * k : 256 * k + 256] for k in range(4)], axis=0)


def route_kernel(tokens, mine, other, gain, router, match, kept, hidden, payload, probs, totals):
    values = tokens[...].astype(F32) + mine[...] + other[...]
    hidden[...] = values
    factor = lax.rsqrt(jnp.mean(values * values, axis=1, keepdims=True) + EPS)
    rows = (values * factor * gain[...]).astype(BF)
    payload[0:HALF, :] = rows
    logits = dot_nt(router[...], rows)
    raised = jnp.exp(logits - jnp.max(logits, axis=0, keepdims=True))
    prob = raised / jnp.sum(raised, axis=0, keepdims=True)
    probs[...] = prob
    chosen = prob * match[...]
    total = jnp.sum(chosen, axis=0, keepdims=True)
    totals[...] = total
    high, low = split(experts_to_rows(chosen / total * kept[...]))
    payload[HALF:PAD, :] = jnp.concatenate([high, low], axis=0)


def route(tokens, mine, other, gain, router, match, kept):
    return pl.pallas_call(
        route_kernel,
        out_shape=[
            jax.ShapeDtypeStruct((HALF, D), F32),
            jax.ShapeDtypeStruct((PAD, D), BF),
            jax.ShapeDtypeStruct((EXPERTS, HALF), F32),
            jax.ShapeDtypeStruct((1, HALF), F32),
        ],
        compiler_params=pltpu.CompilerParams(vmem_limit_bytes=VMEM),
        cost_estimate=cost(10**8, 5 * 10**6),
        name="route",
    )(tokens, mine, other, gain, router, match, kept)


def expert_kernel(
    index, counts, where_at, x_low, x_high, c0, c1, c2, c3, slots,
    wg_m, wu_m, wd_m, wg_o, wu_o, wd_o,
    out_y, out_x, kept_x, kept_g, kept_h,
    xs, gs, total, dots,
):
    expert = pl.program_id(0)
    lane_block, row_at = where_at[0], where_at[1]
    halves = (x_low[0], x_low[1], x_high[0], x_high[1])

    @pl.when(expert == 0)
    def _():
        for h in range(4):
            xs[h * HALF : (h + 1) * HALF, :] = halves[h][0:HALF, :]
            gs[h * HALF : (h + 1) * HALF, :] = (c0, c1, c2, c3)[h][0, 0:HALF, :]
        total[...] = jnp.zeros_like(total)
        dots[...] = jnp.zeros_like(dots)

    gate_row = []
    for h in range(4):
        table = halves[h][HALF:PAD, :].astype(F32)
        picked = jnp.zeros((16, 256), F32)
        for k in range(4):
            picked = picked + jnp.where(lane_block == k, table[:, 256 * k : 256 * k + 256], 0.0)
        row = lax.broadcasted_iota(jnp.int32, (16, 256), 0) % 8
        picked = jnp.where(row == row_at + expert, picked, 0.0)
        gate_row.append(jnp.sum(picked, axis=0, keepdims=True))
    gate_row = jnp.concatenate(gate_row, axis=1)
    slot_row = slots[pl.ds(expert, 1), :].astype(jnp.int32)

    def tile(i, carry):
        base = pl.multiple_of(i * TILE, TILE)
        number = lax.broadcasted_iota(jnp.int32, (TILE, 1024), 0)
        here = number == slot_row - base
        pick = jnp.where(here, 1.0, 0.0).astype(BF)
        gate = jnp.sum(jnp.where(here, gate_row, 0.0), axis=1, keepdims=True)
        x = dot(pick, xs[...]).astype(BF)
        g = dot(pick, gs[...]).astype(BF)
        kept_x[0, pl.ds(base, TILE), :] = x
        kept_g[0, pl.ds(base, TILE), :] = g
        gate_dot = jnp.zeros((TILE, 1), F32)
        y = jnp.zeros((TILE, D), F32)
        back = jnp.zeros((TILE, D), F32)
        for part, (wg, wu, wd) in enumerate(((wg_m, wu_m, wd_m), (wg_o, wu_o, wd_o))):
            gate_pre = dot(x, wg[0])
            up_pre = dot(x, wu[0])
            grad = dot(g, wd[0])
            sig = jax.nn.sigmoid(gate_pre)
            swish = gate_pre * sig
            act = (swish * up_pre).astype(BF).astype(F32)
            gate_dot = gate_dot + jnp.sum(act * grad, axis=1, keepdims=True)
            act = (act * gate).astype(BF)
            grad = grad * gate
            grad_gate = (grad * up_pre * sig * (1.0 + gate_pre * (1.0 - sig))).astype(BF)
            grad_up = (grad * swish).astype(BF)
            y = y + dot_nt(act, wd[0])
            back = back + dot_nt(grad_gate, wg[0]) + dot_nt(grad_up, wu[0])
            at = part * 256
            kept_h[0, pl.ds(base, TILE), at : at + 256] = act
            kept_h[0, pl.ds(base, TILE), 512 + at : 768 + at] = grad_gate
            kept_h[0, pl.ds(base, TILE), 1024 + at : 1280 + at] = grad_up
        total[...] += dot_tn(pick, jnp.concatenate([y.astype(BF), back.astype(BF)], axis=1))
        dots[pl.ds(expert, 1), :] += jnp.sum(jnp.where(here, gate_dot, 0.0), axis=0, keepdims=True)
        return carry

    lax.fori_loop(0, (counts[expert] + TILE - 1) // TILE, tile, 0)

    @pl.when(expert == 1)
    def _():
        out_y[...] = total[:, 0:D].astype(BF)
        row = lax.broadcasted_iota(jnp.int32, (8, 256), 0)
        for h in range(4):
            out_x[h, 0:HALF, :] = total[h * HALF : (h + 1) * HALF, D : 2 * D].astype(BF)
            at = slice(h * HALF, h * HALF + HALF)
            spread = jnp.where(row == row_at, dots[0:1, at], 0.0)
            spread = spread + jnp.where(row == row_at + 1, dots[1:2, at], 0.0)
            spread = jnp.concatenate(
                [jnp.where(lane_block == k, spread, 0.0) for k in range(4)], axis=1
            )
            high, low = split(spread)
            out_x[h, HALF:PAD, :] = jnp.concatenate([high, low], axis=0)


def expert_chunk(index, counts, where_at, low, high, high_block, cotangents, slots, mine, other):
    fixed = lambda e, i, n, w: (0, 0)
    by_expert = lambda e, i, n, w: (e, 0, 0)
    cot = lambda h: pl.BlockSpec((1, PAD, D), lambda e, i, n, w: (i[h], 0, 0))
    weight = pl.BlockSpec((1, D, 256), by_expert)
    return pl.pallas_call(
        expert_kernel,
        grid_spec=pltpu.PrefetchScalarGridSpec(
            num_scalar_prefetch=3,
            grid=(2,),
            in_specs=[
                pl.BlockSpec((2, PAD, D), lambda e, i, n, w: (0, 0, 0)),
                pl.BlockSpec((2, PAD, D), lambda e, i, n, w: (high_block, 0, 0)),
                cot(0), cot(1), cot(2), cot(3),
                pl.BlockSpec((2, 1024), fixed),
                weight, weight, weight, weight, weight, weight,
            ],
            out_specs=[
                pl.BlockSpec((1024, D), fixed),
                pl.BlockSpec((4, PAD, D), lambda e, i, n, w: (0, 0, 0)),
                pl.BlockSpec((1, SLOTS, D), by_expert),
                pl.BlockSpec((1, SLOTS, D), by_expert),
                pl.BlockSpec((1, SLOTS, 1536), by_expert),
            ],
            scratch_shapes=[
                pltpu.VMEM((1024, D), BF),
                pltpu.VMEM((1024, D), BF),
                pltpu.VMEM((1024, 2 * D), F32),
                pltpu.VMEM((8, 1024), F32),
            ],
        ),
        out_shape=[
            jax.ShapeDtypeStruct((1024, D), BF),
            jax.ShapeDtypeStruct((4, PAD, D), BF),
            jax.ShapeDtypeStruct((2, SLOTS, D), BF),
            jax.ShapeDtypeStruct((2, SLOTS, D), BF),
            jax.ShapeDtypeStruct((2, SLOTS, 1536), BF),
        ],
        compiler_params=params(1),
        cost_estimate=cost(12 * 10**9, 30 * 10**6),
        name="experts",
    )(index, counts, where_at, low, high, *([cotangents] * 4), slots, *mine, *other)


def expert_weight_kernel(counts, *refs):
    sets, (out_m, out_o), (down, gate_up) = refs[:12], refs[12:14], refs[14:]
    expert, chunk, piece = pl.program_id(0), pl.program_id(1), pl.program_id(2)

    @pl.when((chunk == 0) & (piece == 0))
    def _():
        down[...] = jnp.zeros_like(down)
        gate_up[...] = jnp.zeros_like(gate_up)

    for ch in range(4):

        @pl.when((chunk == ch) & (counts[ch * 2 + expert] > piece * TILE))
        def _(ch=ch):
            x, g, h = sets[3 * ch], sets[3 * ch + 1], sets[3 * ch + 2]
            down[...] += dot_tn(g[0], h[0, :, 0:512])
            gate_up[...] += dot_tn(x[0], h[0, :, 512:1536])

    @pl.when((chunk == 3) & (piece == 1))
    def _():
        for part, out in enumerate((out_m, out_o)):
            at = part * 256
            out[0, :, 0:256] = down[:, at : at + 256].astype(out.dtype)
            out[0, :, 256:512] = gate_up[:, at : at + 256].astype(out.dtype)
            out[0, :, 512:768] = gate_up[:, 512 + at : 768 + at].astype(out.dtype)


def expert_weights(counts, kept):
    def index(ch):
        def at(e, j, i, n):
            more = jnp.where(n[ch * 2 + e] > TILE, 1, 0)
            piece = jnp.where(j == ch, i * more, jnp.where(j > ch, more, 0))
            return (e, piece, 0)

        return at

    specs = []
    for ch in range(4):
        for width in (D, D, 1536):
            specs.append(pl.BlockSpec((1, TILE, width), index(ch)))
    out = pl.BlockSpec((1, D, 768), lambda e, j, i, n: (e, 0, 0))
    return pl.pallas_call(
        expert_weight_kernel,
        grid_spec=pltpu.PrefetchScalarGridSpec(
            num_scalar_prefetch=1,
            grid=(2, 4, 2),
            in_specs=specs,
            out_specs=[out, out],
            scratch_shapes=[pltpu.VMEM((D, 512), F32), pltpu.VMEM((D, 1024), F32)],
        ),
        out_shape=[
            jax.ShapeDtypeStruct((2, D, 768), F32),
            jax.ShapeDtypeStruct((2, D, 768), BF),
        ],
        compiler_params=params(3),
        cost_estimate=cost(10 * 10**9, 30 * 10**6),
        name="expert_weights",
    )(counts, *[item for chunk in kept for item in chunk])


def route_back_kernel(
    own, first, second, cotangent, hidden, gain, router, normed, probs, totals, match,
    grad_hidden, grad_branch, grad_router, grad_gain,
):
    summed = own[...].astype(F32) + first[...].astype(F32) + second[...].astype(F32)
    tables = summed[HALF:PAD, :]
    grad_gates = rows_to_experts(tables[0:8] + tables[8:16])
    prob, total = probs[...], totals[...]
    chosen = prob * match[...]
    shared = jnp.sum(grad_gates * chosen, axis=0, keepdims=True) / (total * total)
    grad_prob = (grad_gates / total - shared) * match[...]
    grad_logits = prob * (grad_prob - jnp.sum(prob * grad_prob, axis=0, keepdims=True))
    high, low = split(grad_logits)
    grad_router[...] = dot(high, normed[0:HALF, :]) + dot(low, normed[0:HALF, :])
    grad_normed = summed[0:HALF, :] + dot_tn(high, router[...]) + dot_tn(low, router[...])
    values = hidden[...]
    factor = lax.rsqrt(jnp.mean(values * values, axis=1, keepdims=True) + EPS)
    grad_gain[...] = jnp.sum(grad_normed * values * factor, axis=0, keepdims=True)
    weighted = grad_normed * gain[...]
    mean = jnp.mean(weighted * values, axis=1, keepdims=True)
    grad = cotangent[...].astype(F32) + factor * weighted - values * (factor * factor * factor * mean)
    grad_hidden[...] = grad
    grad_branch[...] = grad.astype(BF)


def route_back(*args):
    return pl.pallas_call(
        route_back_kernel,
        out_shape=[
            jax.ShapeDtypeStruct((HALF, D), F32),
            jax.ShapeDtypeStruct((HALF, D), BF),
            jax.ShapeDtypeStruct((EXPERTS, D), F32),
            jax.ShapeDtypeStruct((1, D), F32),
        ],
        compiler_params=pltpu.CompilerParams(vmem_limit_bytes=VMEM),
        cost_estimate=cost(10**8, 6 * 10**6),
        name="route_back",
    )(*args)


def norm_back_heads(grad, proj, gain, cosine, sine):
    turned = rot_back(grad, cosine, sine)
    factor = lax.rsqrt(head_mean(proj * proj) + EPS)
    weighted = turned * gain
    mean = head_mean(weighted * proj)
    back = factor * weighted - proj * (factor * factor * factor * mean)
    return back, jnp.sum(turned * proj * factor, axis=0, keepdims=True)


def attend_back_kernel(
    place, q, q_proj, k, k_proj, v, seg_q, seg_k, grad_branch, w_out, attended,
    cos_q, sin_q, cos_k, sin_k, q_gain, k_gain, grad_q, grad_k, grad_v, gains,
):
    mask = jnp.where(seg_q[0] == seg_k[0], 0.0, NEGATIVE)
    keys, values = k[0], v[0]
    grad_mixed = dot(grad_branch[...], w_out[...]).astype(BF).astype(F32)
    sum_k = jnp.zeros((SEQ, 128), F32)
    sum_v = jnp.zeros((SEQ, 128), F32)
    gain_q = jnp.zeros((1, 128), F32)
    pick_lane = lax.broadcasted_iota(jnp.int32, (8, 128), 1) // HD
    for block in range(2):
        at = slice(block * 128, block * 128 + 128)
        heads = q[0, :, at].astype(F32)
        grads = grad_mixed[:, at]
        high, low = split(attended[:, at].astype(F32) * grads)
        sum_q = jnp.zeros((HALF, 128), F32)
        for j in range(2):
            query = place_head(heads, block, j).astype(BF)
            grad = place_head(grads, block, j).astype(BF)
            lanes = jnp.where(pick_lane == j, 1.0, 0.0).astype(BF)
            row_dot = (dot_nt(lanes, high) + dot_nt(lanes, low))[0:1]
            raised = jnp.exp(dot_nt(keys, query) + mask)
            probs = raised * (1.0 / jnp.sum(raised, axis=0, keepdims=True))
            grad_scores = (probs * (dot_nt(values, grad) - row_dot)).astype(BF)
            sum_k = sum_k + dot(grad_scores, query)
            sum_v = sum_v + dot(probs.astype(BF), grad)
            sum_q = sum_q + place_head(dot_tn(grad_scores, keys) * 0.125, j, block)
        back, part = norm_back_heads(sum_q, q_proj[0, :, at], q_gain[...], cos_q[...], sin_q[...])
        grad_q[:, at] = back.astype(BF)
        gain_q = gain_q + part
    back, gain_k = norm_back_heads(sum_k, k_proj[0], k_gain[...], cos_k[...], sin_k[...])
    grad_k[...] = back.astype(BF)
    grad_v[...] = sum_v.astype(BF)
    part = jnp.concatenate([gain_q, gain_k, jnp.zeros((6, 128), F32)], axis=0)

    @pl.when(pl.program_id(0) == 0)
    def _():
        gains[...] = part

    @pl.when(pl.program_id(0) != 0)
    def _():
        gains[...] += part


def attend_back(
    seq, q_b, q_proj, k_b, k_proj, v_b, seg_q, seg_k, grad_branch, w_out, attended,
    cosine, sine, q_gain, k_gain,
):
    queries = pl.BlockSpec((1, HALF, 256), lambda p, r: (r[0], 0, p))
    keys = pl.BlockSpec((1, SEQ, 128), lambda p, r: (r[0], 0, p))
    turn_q = pl.BlockSpec((HALF, 128), lambda p, r: (r[1], 0))
    turn_k = pl.BlockSpec((SEQ, 128), lambda p, r: (0, 0))
    gain = pl.BlockSpec((1, 128), lambda p, r: (0, 0))
    return pl.pallas_call(
        attend_back_kernel,
        grid_spec=pltpu.PrefetchScalarGridSpec(
            num_scalar_prefetch=1,
            grid=(2,),
            in_specs=[
                queries, queries, keys, keys, keys,
                pl.BlockSpec((1, 1, HALF), lambda p, r: (r[0], 0, 0)),
                pl.BlockSpec((1, SEQ, 1), lambda p, r: (r[0], 0, 0)),
                pl.BlockSpec((HALF, D), lambda p, r: (0, 0)),
                pl.BlockSpec((D, 256), lambda p, r: (0, p)),
                pl.BlockSpec((HALF, 256), lambda p, r: (0, p)),
                turn_q, turn_q, turn_k, turn_k, gain, gain,
            ],
            out_specs=[
                pl.BlockSpec((HALF, 256), lambda p, r: (0, p)),
                pl.BlockSpec((SEQ, 128), lambda p, r: (0, p)),
                pl.BlockSpec((SEQ, 128), lambda p, r: (0, p)),
                pl.BlockSpec((8, 128), lambda p, r: (0, 0)),
            ],
        ),
        out_shape=[
            jax.ShapeDtypeStruct((HALF, 512), BF),
            jax.ShapeDtypeStruct((SEQ, 256), BF),
            jax.ShapeDtypeStruct((SEQ, 256), BF),
            jax.ShapeDtypeStruct((8, 128), F32),
        ],
        compiler_params=params(1),
        cost_estimate=cost(16 * 10**9, 8 * 10**6),
        name="attend_back",
    )(
        seq, q_b, q_proj, k_b, k_proj, v_b, seg_q, seg_k, grad_branch, w_out, attended,
        cosine, sine, cosine, sine, q_gain, k_gain,
    )


def weight_grads_kernel(
    place, normed, normed_own, q0, q1, k0, k1, v0, v1, b0, b1, a0, a1, misc, out, total
):
    step = pl.program_id(0)

    def add(first, q, k, v, branch, mixed):
        rows, own = normed[0], normed_own[0]
        parts = (
            (0, 512, dot_tn(own, q[...])),
            (512, 768, dot_tn(rows, k[...])),
            (768, 1024, dot_tn(rows, v[...])),
            (1024, 1536, dot_tn(branch[...], mixed[...])),
        )
        for low, high, value in parts:
            if first:
                total[:, low:high] = value
            else:
                total[:, low:high] += value

    @pl.when(step == 0)
    def _():
        add(True, q0, k0, v0, b0, a0)

    @pl.when(step == 1)
    def _():
        add(False, q1, k1, v1, b1, a1)
        for r in range(N_FSDP):
            at = pl.multiple_of(place[2 + r] * 64, 64)
            out[r, :, 0:1536] = total[pl.ds(at, 64), :].astype(BF)
            out[r, :, 1536:1664] = misc[pl.ds(at, 64), :].astype(BF)


def weight_grads(place, normed, pairs, misc):
    fixed = lambda i, r: (0, 0)
    ordered = lambda i, r: jnp.where(i == 0, r[0], 1 - r[0])
    specs = [
        pl.BlockSpec((1, SEQ, D), lambda i, r: (ordered(i, r), 0, 0)),
        pl.BlockSpec((1, HALF, D), lambda i, r: (ordered(i, r), r[1], 0)),
    ]
    for rows, width in ((HALF, 512), (SEQ, 256), (SEQ, 256), (HALF, D), (HALF, 512)):
        specs += [pl.BlockSpec((rows, width), fixed)] * 2
    specs.append(pl.BlockSpec((D, 128), fixed))
    return pl.pallas_call(
        weight_grads_kernel,
        grid_spec=pltpu.PrefetchScalarGridSpec(
            num_scalar_prefetch=1,
            grid=(2,),
            in_specs=specs,
            out_specs=pl.BlockSpec((N_FSDP, 64, 1664), lambda i, r: (0, 0, 0)),
            scratch_shapes=[pltpu.VMEM((D, 1536), F32)],
        ),
        out_shape=jax.ShapeDtypeStruct((N_FSDP, 64, 1664), BF),
        compiler_params=params(1),
        cost_estimate=cost(4 * 10**9, 16 * 10**6),
        name="weight_grads",
    )(place, normed, normed, *[item for pair in pairs for item in pair], misc)


def input_grads_kernel(place, gq, gk, gv, w, out):
    out[0] = (dot_nt(gk[...], w[:, 512:768]) + dot_nt(gv[...], w[:, 768:1024])).astype(BF)

    @pl.when(pl.program_id(0) == place[0])
    def _():
        part = dot_nt(gk[...], w[:, 512:768]) + dot_nt(gv[...], w[:, 768:1024])
        out[0] = (part + dot_nt(gq[...], w[:, 0:512])).astype(BF)


def input_grads(place, gq, gk, gv, weights):
    return pl.pallas_call(
        input_grads_kernel,
        grid_spec=pltpu.PrefetchScalarGridSpec(
            num_scalar_prefetch=1,
            grid=(4,),
            in_specs=[
                pl.BlockSpec((HALF, 512), lambda i, r: (0, 0)),
                pl.BlockSpec((HALF, 256), lambda i, r: (i, 0)),
                pl.BlockSpec((HALF, 256), lambda i, r: (i, 0)),
                pl.BlockSpec((D, 1024), lambda i, r: (0, 0)),
            ],
            out_specs=pl.BlockSpec((1, HALF, D), lambda i, r: (i, 0, 0)),
        ),
        out_shape=jax.ShapeDtypeStruct((N_CONTEXT, HALF, D), BF),
        compiler_params=params(1),
        cost_estimate=cost(2 * 10**9, 6 * 10**6),
        name="input_grads",
    )(place, gq, gk, gv, weights)


def finish_kernel(grad_normed, tokens, grad_hidden, gain, out):
    values = tokens[...].astype(F32)
    factor = lax.rsqrt(jnp.mean(values * values, axis=1, keepdims=True) + EPS)
    weighted = grad_normed[...].astype(F32) * gain[...]
    mean = jnp.mean(weighted * values, axis=1, keepdims=True)
    out[...] = grad_hidden[...] + factor * weighted - values * (factor * factor * factor * mean)


def finish(*args):
    return pl.pallas_call(
        finish_kernel,
        out_shape=jax.ShapeDtypeStruct((HALF, D), F32),
        compiler_params=pltpu.CompilerParams(vmem_limit_bytes=VMEM),
        cost_estimate=cost(10**7, 4 * 10**6),
        name="finish",
    )(*args)


def ring_pairs(stage, step):
    pairs = []
    for x in range(4):
        for z in range(4):
            for t in range(2):
                if (stage == 0) == (t == 0):
                    far = ((x + step) % 4) * 4 + z
                else:
                    far = x * 4 + (z + step) % 4
                pairs.append(((x * 4 + z) * 2 + t, far * 2 + t))
    return pairs


def ring(value, stage, step):
    return lax.ppermute(value, ("fsdp", "tensor"), ring_pairs(stage, step))


def swap_cores(value):
    return lax.ppermute(value, "tensor", [(0, 1), (1, 0)])


def gather_ring(block, stage, cut):
    behind = ring(block, stage, 1)
    ahead = ring(block, stage, -1)
    first = ring(behind[:cut], stage, 1)
    second = ring(ahead[cut:], stage, -1)
    return ahead, behind, first, second


def scatter_ring(own, ahead, behind, far, stage, cut):
    first = ring(far[:cut], stage, 1)
    second = ring(far[cut:], stage, -1)
    ahead = jnp.concatenate([ahead[:cut] + first, ahead[cut:]], axis=0)
    behind = jnp.concatenate([behind[:cut], behind[cut:] + second], axis=0)
    return own, ring(ahead, stage, 1), ring(behind, stage, -1)


def sum_of(parts):
    return (parts[0].astype(F32) + parts[1].astype(F32) + parts[2].astype(F32)).astype(BF)


def scatter_both(chunks, rows, cut_far, cut_near):
    column = sum_of(scatter_ring(*chunks, 1, cut_far))
    blocks = [column[i * rows : (i + 1) * rows] for i in range(4)]
    return scatter_ring(*blocks, 0, cut_near)


def local(
    tokens, segments, routes, attention_gain, w_query, w_key, w_value, w_out, query_gain,
    key_gain, feedforward_gain, router, w_gate, w_up, w_down, cotangent,
):
    f, c, t = lax.axis_index("fsdp"), lax.axis_index("context"), lax.axis_index("tensor")
    x_at, z_at = f // 4, f % 4
    shifts = jnp.array([0, 1, 3, 2], jnp.int32)
    a_at, b_at = jnp.where(t == 0, x_at, z_at), jnp.where(t == 0, z_at, x_at)
    a_all, b_all = (a_at + shifts) % 4, (b_at + shifts) % 4
    order = jnp.where(
        t == 0,
        a_all[None, :] * 4 + b_all[:, None],
        b_all[:, None] * 4 + a_all[None, :],
    ).astype(jnp.int32)
    as_row = lambda *v: jnp.stack([jnp.asarray(i, jnp.int32) for i in v])

    tokens_half = lax.dynamic_index_in_dim(tokens, t, 0, keepdims=False)
    cot_half = lax.dynamic_index_in_dim(cotangent, t, 0, keepdims=False)
    small = jnp.concatenate(
        [
            router,
            attention_gain[:, None],
            feedforward_gain[:, None],
            jnp.pad(query_gain, (0, 60))[:, None],
            jnp.pad(key_gain, (0, 60))[:, None],
            jnp.zeros((64, 92), BF),
        ],
        axis=1,
    )
    packed = jnp.concatenate([w_query, w_key, w_value, small], axis=1)
    weights = lax.all_gather(packed, "fsdp", axis=0, tiled=True)
    tokens_all = lax.all_gather(tokens_half, ("context", "tensor"), axis=0)
    out_whole = lax.all_gather(w_out, "fsdp", axis=0, tiled=True)
    other = tuple(swap_cores(w) for w in (w_gate, w_up, w_down))

    picked = routes.reshape(ROWS, TOPK).T
    experts = jnp.arange(EXPERTS, dtype=jnp.int32)
    match = jnp.any(picked[:, None, :] == experts[None, :, None], axis=0)
    earlier = jnp.arange(ROWS)[:, None] < jnp.arange(ROWS)[None, :]
    place = dot(match.astype(BF), earlier.astype(BF))
    kept = match & (place < CAP)
    half = lambda v: lax.dynamic_slice_in_dim(v, t * HALF, HALF, 1)
    start = jnp.where(t == 0, 0.0, place[:, HALF : HALF + 1])
    match_half = half(match).astype(F32)
    kept_half = half(kept)
    local_place = jnp.where(kept_half, half(place) - start, -1.0).astype(BF)
    kept_half = kept_half.astype(F32)
    table = experts_to_rows(local_place)
    cot_payload = jnp.concatenate([cot_half, table, jnp.zeros((8, D), BF)], axis=0)
    cot_all = lax.all_gather(cot_payload, "fsdp", axis=0)

    mine = cot_all[:, HALF : HALF + 8, :].reshape(N_FSDP, 8, 4, HALF)
    mine = lax.dynamic_slice(mine, (0, 2 * (f % 4), f // 4, 0), (N_FSDP, 2, 1, HALF))
    mine = jnp.take(mine.reshape(N_FSDP, 2, HALF), order.reshape(-1), axis=0).astype(F32)
    mine = mine.reshape(4, 4, 2, HALF)
    number = jnp.max(mine, axis=-1) + 1.0
    offset = jnp.cumsum(number, axis=1) - number
    slots = jnp.where(mine >= 0, mine + offset[..., None], -1.0)
    slots = slots.transpose(0, 2, 1, 3).reshape(4, 2, 1024)
    counts = jnp.sum(number, axis=1).astype(jnp.int32)

    gain1 = weights[:, 1056].astype(F32)[None, :]
    gain2 = weights[:, 1057].astype(F32)[None, :]
    head_gain = lambda at: jnp.tile(
        weights.reshape(N_FSDP, 64, 1152)[:, 0:4, at].reshape(1, HD).astype(F32), (1, 2)
    )
    q_gain, k_gain = head_gain(1058), head_gain(1059)
    router_t = weights[:, 1024:1056].T
    cosine, sine = rotary_tables()
    normed1, k_proj, k_b, v_b, q_proj, q_b = project(
        as_row(c), tokens_all, weights, gain1, q_gain, k_gain, cosine, sine
    )
    seg_own = lax.dynamic_slice_in_dim(segments, c * HALF, HALF, 1)
    att_other, branch_other = attend(
        as_row(1 - t), q_b, k_b, v_b, seg_own[:, :, None], segments[:, None, :], out_whole
    )
    received = swap_cores(branch_other)
    att_own, branch_own = attend(
        as_row(t), q_b, k_b, v_b, seg_own[:, :, None], segments[:, None, :], out_whole
    )
    hidden1, payload, probs, totals = route(
        tokens_half, branch_own, received, gain2, router_t, match_half, kept_half
    )

    ahead, behind, first, second = gather_ring(payload, 0, 144)
    column = jnp.concatenate([payload, ahead, behind, first, second], axis=0)
    ahead, behind, first, second = gather_ring(column, 1, 2 * PAD)
    as_pairs = lambda v: v.reshape(-1, PAD, D)
    where_at = as_row(f // 4, 2 * (f % 4))
    results = []
    for chunk, (low, high, high_block) in enumerate(
        ((column, column, 1), (ahead, ahead, 1), (behind, behind, 1), (first, second, 0))
    ):
        results.append(
            expert_chunk(
                order[chunk], counts[chunk], where_at, as_pairs(low), as_pairs(high), high_block,
                cot_all, slots[chunk], (w_gate, w_up, w_down), other,
            )
        )
    back = scatter_both([r[1].reshape(4 * PAD, D) for r in results], PAD, 2 * PAD, 144)
    mixed = scatter_both([r[0] for r in results], HALF, 512, 128)
    grads_m, grads_o = expert_weights(counts.reshape(-1), [r[2:] for r in results])
    grads_e = (grads_m + swap_cores(grads_o).astype(F32)).astype(BF)
    grads_e = lax.psum_scatter(grads_e, "context", scatter_dimension=1, tiled=True)

    grad_hidden, grad_branch, grad_router, grad_gain2 = route_back(
        *back, cot_half, hidden1, gain2, router_t, payload, probs, totals, match_half
    )
    branch_far = swap_cores(grad_branch)
    attention_back = lambda seq, grad, att: attend_back(
        as_row(seq, c), q_b, q_proj, k_b, k_proj, v_b, seg_own[:, None, :], segments[:, :, None],
        grad, out_whole, att, cosine, sine, q_gain, k_gain,
    )
    gq_own, gk_own, gv_own, gains_own = attention_back(t, grad_branch, att_own)
    gq_far, gk_far, gv_far, gains_far = attention_back(1 - t, branch_far, att_other)
    head_grads = gains_own + gains_far
    head_grads = head_grads[0:2, 0:64] + head_grads[0:2, 64:128]
    by_owner = lambda v: jnp.pad(v.reshape(N_FSDP, 4), ((0, 0), (0, 60))).reshape(D, 1)
    misc = jnp.concatenate(
        [
            grad_router.T,
            grad_gain2.reshape(D, 1),
            by_owner(head_grads[0]),
            by_owner(head_grads[1]),
            jnp.zeros((D, 93), F32),
        ],
        axis=1,
    )
    grads_w = weight_grads(
        jnp.concatenate([as_row(t, c), order.reshape(-1)]),
        normed1,
        (
            (gq_own, gq_far),
            (gk_own, gk_far),
            (gv_own, gv_far),
            (grad_branch, branch_far),
            (att_own, att_other),
        ),
        misc,
    )
    grads_w = grads_w.reshape(4, 256, 1664)
    grads_w = sum_of(scatter_both([grads_w[i] for i in range(4)], 64, 128, 32))
    shift = lambda v, n: lax.ppermute(v, "context", [(i, (i + n) % 4) for i in range(4)])
    grads_w = (
        grads_w.astype(F32)
        + shift(grads_w, 1).astype(F32)
        + shift(grads_w, 2).astype(F32)
        + shift(grads_w, 3).astype(F32)
    )
    sums = grads_w[:, 1536:1664]
    shards = jnp.concatenate([w_query, w_key, w_value], axis=1).astype(F32)
    grad_gain1 = jnp.sum(shards * grads_w[:, 0:1024], axis=1) / attention_gain.astype(F32)
    sums = jnp.concatenate([sums[:, 0:35], grad_gain1[:, None], sums[:, 36:]], axis=1)
    sums = sums + swap_cores(sums)

    far_in = input_grads(as_row(c), gq_far, gk_far, gv_far, weights)
    own_in = input_grads(as_row(c), gq_own, gk_own, gv_own, weights)
    near = (own_in.astype(F32) + swap_cores(far_in).astype(F32)).astype(BF)
    grad_normed1 = lax.psum_scatter(near, "context", scatter_dimension=0, tiled=True)[0]
    grad_tokens = finish(grad_normed1, tokens_half, grad_hidden, gain1)

    def both(v):
        far = swap_cores(v)
        return jnp.where(t == 0, jnp.stack([v, far]), jnp.stack([far, v]))

    block_half = hidden1 + mixed[0].astype(F32) + mixed[1].astype(F32) + mixed[2].astype(F32)
    grads_e = grads_e.astype(F32)
    return (
        both(block_half.astype(BF)),
        both(grad_tokens),
        sums[:, 35],
        grads_w[:, 0:512],
        grads_w[:, 512:768],
        grads_w[:, 768:1024],
        grads_w[:, 1024:1536],
        sums[0:4, 33],
        sums[0:4, 34],
        sums[:, 32],
        sums[:, 0:32],
        grads_e[:, :, 256:512],
        grads_e[:, :, 512:768],
        grads_e[:, :, 0:256],
    )


def solution(mesh):
    in_specs = (
        P("fsdp", "context", None),
        P("fsdp", None),
        P("fsdp", "context", None),
        P("fsdp"),
        P("fsdp", "tensor"),
        P("fsdp", "tensor"),
        P("fsdp", "tensor"),
        P("fsdp", "tensor"),
        P("fsdp"),
        P("fsdp"),
        P("fsdp"),
        P("fsdp", None),
        P("fsdp", None, "tensor"),
        P("fsdp", None, "tensor"),
        P("fsdp", None, "tensor"),
        P("fsdp", "context", None),
    )
    out_specs = (
        P("fsdp", "context", None),
        P("fsdp", "context", None),
        P("fsdp"),
        P("fsdp", "tensor"),
        P("fsdp", "tensor"),
        P("fsdp", "tensor"),
        P("fsdp", "tensor"),
        P("fsdp"),
        P("fsdp"),
        P("fsdp"),
        P("fsdp", None),
        P("fsdp", "context", "tensor"),
        P("fsdp", "context", "tensor"),
        P("fsdp", "context", "tensor"),
    )
    return jax.shard_map(local, mesh=mesh, in_specs=in_specs, out_specs=out_specs, check_vma=False)
```

```python
import functools

import jax
import jax.numpy as jnp
import numpy as np
from jax import lax
from jax.experimental import pallas as pl
from jax.experimental.pallas import tpu as pltpu
from jax.sharding import PartitionSpec as P

HD = 64
EXPERTS = 32
TOPK = 8
SEQ = 1024
D = 1024
ROWS = 512
HALF = 256
CAP = 160
MAIN = 96
MORE = 32
PIECES = 2
PAD = 272
N_FSDP = 16
N_CONTEXT = 4
EPS = 1e-06
NEGATIVE = -1e30
VMEM = 62 * 1024 * 1024
BF = jnp.bfloat16
F32 = jnp.float32
NT = (((1,), (1,)), ((), ()))
TN = (((0,), (0,)), ((), ()))


def dot(a, b):
    return jnp.dot(a, b, preferred_element_type=F32)


def dot_nt(a, b):
    return lax.dot_general(a, b, NT, preferred_element_type=F32)


def dot_tn(a, b):
    return lax.dot_general(a, b, TN, preferred_element_type=F32)


def split(v):
    high = v.astype(BF)
    return high, (v - high.astype(F32)).astype(BF)


def params(grid_dims):
    return pltpu.CompilerParams(
        dimension_semantics=("arbitrary",) * grid_dims, vmem_limit_bytes=VMEM
    )


def cost(flops, moved):
    return pl.CostEstimate(flops=flops, bytes_accessed=moved, transcendentals=0)


HBM = pl.BlockSpec(memory_space=pltpu.HBM)


def past(kernel, inputs, others):
    return lambda *refs: kernel(*refs[:inputs], *refs[inputs + others :])


def head_mean(v):
    rows = lax.broadcasted_iota(jnp.int32, (512, 256), 0) % 256 // HD
    cols = lax.broadcasted_iota(jnp.int32, (512, 256), 1) // HD
    block = jnp.where(rows == cols, 1.0, 0.0).astype(BF)
    return dot(jnp.concatenate(split(v), axis=1), block) * (1.0 / HD)


def swap_halves(v):
    lane = lax.broadcasted_iota(jnp.int32, v.shape, 1) % HD
    width = v.shape[1]
    return jnp.where(lane < HD // 2, pltpu.roll(v, width - 32, 1), pltpu.roll(v, 32, 1))


def twice(v):
    return jnp.concatenate([v, v], axis=1)


def rotary_tables():
    middle = HD // 2
    inverse = 10000.0 ** (-(2.0 * np.arange(middle, dtype=np.float64) / HD))
    inverse = inverse.astype(np.float32)
    angles = np.arange(SEQ, dtype=np.float32)[:, None] * inverse[None, :]
    angles = angles.astype(np.float64)
    cosine, sine = np.cos(angles).astype(np.float32), np.sin(angles).astype(np.float32)
    cosine = np.concatenate([cosine] * 4, axis=1)
    sine = np.concatenate([-sine, sine, -sine, sine], axis=1)
    order = lambda v: v.reshape(4, 4, 2, 32, 128).transpose(0, 2, 1, 3, 4).reshape(8, 128, 128)
    return order(cosine), order(sine)


def pack_kernel(where, w_query, w_key, w_value, w_out, router, gain1, gain2, q_gain, k_gain, out):
    out[:, 0:512] = w_query[...]
    out[:, 512:768] = w_key[...]
    out[:, 768:1024] = w_value[...]
    out[:, 1024:1536] = w_out[...]
    diagonal = lax.broadcasted_iota(jnp.int32, (64, 64), 0) == lax.broadcasted_iota(
        jnp.int32, (64, 64), 1
    )
    column = lambda v: jnp.sum(
        jnp.where(diagonal, v[...].astype(F32), 0.0), axis=1, keepdims=True
    )
    row = lax.broadcasted_iota(jnp.int32, (64, 128), 0)
    lane = lax.broadcasted_iota(jnp.int32, (64, 128), 1)
    small = jnp.where(lane == 32, column(gain1), 0.0) + jnp.where(lane == 33, column(gain2), 0.0)
    for i in range(4):
        here = lane == HD + 4 * where[0] + i
        for r, v in enumerate((q_gain, k_gain)):
            small = small + jnp.where(here & (row == r), v[0:1, i : i + 1].astype(F32), 0.0)
    out[:, 1536:1664] = small.astype(BF)
    out[:, 1536:1568] = router[...]


def pack(where, *arrays):
    whole = lambda v: pl.BlockSpec(v.shape, lambda i, r: (0, 0))
    return pl.pallas_call(
        pack_kernel,
        grid_spec=pltpu.PrefetchScalarGridSpec(
            num_scalar_prefetch=1,
            grid=(1,),
            in_specs=[whole(v) for v in arrays],
            out_specs=pl.BlockSpec((64, 1664), lambda i, r: (0, 0)),
        ),
        out_shape=jax.ShapeDtypeStruct((64, 1664), BF),
        compiler_params=params(1),
        cost_estimate=cost(10**6, 10**6),
        name="pack",
    )(where, *arrays)


def stack_pairs(blocks, *others):
    rows, width = blocks[0].shape

    def kernel(a, b, c, d, low, high):
        low[0], low[1] = a[...], b[...]
        high[0], high[1] = c[...], d[...]

    return pl.pallas_call(
        past(kernel, 4, len(others)),
        in_specs=[pl.BlockSpec(memory_space=pltpu.VMEM)] * 4 + [HBM] * len(others),
        out_shape=[jax.ShapeDtypeStruct((2, rows, width), BF)] * 2,
        compiler_params=pltpu.CompilerParams(vmem_limit_bytes=VMEM),
        cost_estimate=cost(10**6, 10**6),
        name="stack_pairs",
    )(*blocks, *others)


def add_blocks(arrays, handed=(), *others):
    blocks, n, k = arrays[0].shape[0], len(arrays), len(handed)

    def kernel(*refs):
        for i, out in enumerate(refs[n + k + len(others) :][:blocks]):
            total = refs[0][i].astype(F32)
            for ref in refs[1:n]:
                total = total + ref[i].astype(F32)
            out[...] = total.astype(BF)

    vmem = pl.BlockSpec(memory_space=pltpu.VMEM)
    out = pl.pallas_call(
        kernel,
        in_specs=[vmem] * n + [HBM] * (k + len(others)),
        out_specs=[vmem] * blocks + [HBM] * k,
        out_shape=[jax.ShapeDtypeStruct(arrays[0].shape[1:], BF)] * blocks
        + [jax.ShapeDtypeStruct(v.shape, v.dtype) for v in handed],
        input_output_aliases={n + i: blocks + i for i in range(k)},
        compiler_params=pltpu.CompilerParams(vmem_limit_bytes=VMEM),
        cost_estimate=cost(10**9, 10**7),
        name="add_blocks",
    )(*arrays, *handed, *others)
    return out[:blocks], *out[blocks:]


def pack_cotangent(where, cotangent, table, *others):
    def kernel(where, rows, table, out):
        out[0:HALF, :] = rows[...].reshape(HALF, D)
        out[HALF:PAD, :] = jnp.concatenate([table[...], jnp.zeros((8, D), BF)], axis=0)

    return pl.pallas_call(
        past(kernel, 3, len(others)),
        grid_spec=pltpu.PrefetchScalarGridSpec(
            num_scalar_prefetch=1,
            grid=(1,),
            in_specs=[
                pl.BlockSpec((2, 4, 1, 32, D), lambda i, r: (0, 0, r[0], 0, 0)),
                pl.BlockSpec((8, D), lambda i, r: (0, 0)),
            ]
            + [HBM] * len(others),
            out_specs=pl.BlockSpec((PAD, D), lambda i, r: (0, 0)),
        ),
        out_shape=jax.ShapeDtypeStruct((PAD, D), BF),
        compiler_params=params(1),
        cost_estimate=cost(10**6, 10**6),
        name="pack_cotangent",
    )(where, cotangent.reshape(2, 4, 2, 32, D), table, *others)


def project_kernel(
    order, near, x0, x1, x2, x3, x4, x5, x6, x7, w0, w1, w2, w3, cos_all, sin_all,
    w, small, heads, cosine, sine, normed, k_proj, k_b, v_b, q_proj, q_b,
):
    @pl.when(pl.program_id(0) == 0)
    def _():
        for i, shards in enumerate((w0, w1, w2, w3)):
            for j in range(4):
                to = pl.ds(pl.multiple_of(order[4 * i + j] * 64, 64), 64)
                w[to, :] = shards[j]
        for i in range(8):
            cosine[i * 128 : i * 128 + 128, :] = cos_all[near[i]]
            sine[i * 128 : i * 128 + 128, :] = sin_all[near[i]]
        last = w[:, 1536:1664].astype(F32)
        small[...] = last.T
        summed = last[0:64]
        for i in range(1, N_FSDP):
            summed = summed + last[i * 64 : i * 64 + 64]
        lane = lax.broadcasted_iota(jnp.int32, (8, 128), 1)
        gains = jnp.where(lane >= HD, summed[0:8], 0.0)
        heads[...] = gains + pltpu.roll(gains, HD, 1)

    gain = small[32:33, :]
    for i, x in enumerate((x0, x1, x2, x3, x4, x5, x6, x7)):
        values = x[0].astype(F32)
        factor = lax.rsqrt(jnp.mean(values * values, axis=1, keepdims=True) + EPS)
        normed[0, i * 128 : i * 128 + 128, :] = (values * factor * gain).astype(BF)
    both = dot(normed[0], w[:, 512:1024])
    keys = both[:, 0:256]
    k_proj[0] = keys
    v_b[0] = both[:, 256:512].astype(BF)
    cos, sin = twice(cosine[...]), twice(sine[...])
    scaled = keys * lax.rsqrt(head_mean(keys * keys) + EPS) * twice(heads[1:2, :])
    k_b[0] = (scaled * cos + swap_halves(scaled) * sin).astype(BF)
    queries = dot(normed[0, 0:256, :], w[:, 0:512])
    q_proj[0] = queries
    for block in range(2):
        at = slice(block * 256, block * 256 + 256)
        head = queries[:, at]
        scaled = head * lax.rsqrt(head_mean(head * head) + EPS) * twice(heads[0:1, :])
        turned = scaled * cos[0:256] + swap_halves(scaled) * sin[0:256]
        q_b[0, :, at] = (turned.astype(BF).astype(F32) * 0.125).astype(BF)


def project(order, near, tokens, shards, cosine, sine, *others):
    row = lambda s, r, n: (0, 0)
    of = lambda s, r, n: (s, 0, 0)
    block = lambda i: pl.BlockSpec((1, 128, D), lambda s, r, n: (n[i], s, 0))
    fixed = ((D, 1664, BF), (128, D, F32), (8, 128, F32), (SEQ, 128, F32), (SEQ, 128, F32))
    shapes = ((SEQ, D, BF), (SEQ, 256, F32), (SEQ, 256, BF), (SEQ, 256, BF), (256, 512, F32), (256, 512, BF))
    return pl.pallas_call(
        past(project_kernel, 16, len(others)),
        grid_spec=pltpu.PrefetchScalarGridSpec(
            num_scalar_prefetch=2,
            grid=(2,),
            in_specs=[block(i) for i in range(8)]
            + [pl.BlockSpec((4, 64, 1664), lambda s, r, n: (0, 0, 0))] * 4
            + [pl.BlockSpec((8, 128, 128), lambda s, r, n: (0, 0, 0))] * 2
            + [HBM] * len(others),
            out_specs=[pl.BlockSpec((r, n), row) for r, n, _ in fixed]
            + [pl.BlockSpec((1, r, n), of) for r, n, _ in shapes],
        ),
        out_shape=[jax.ShapeDtypeStruct((r, n), dt) for r, n, dt in fixed]
        + [jax.ShapeDtypeStruct((2, r, n), dt) for r, n, dt in shapes],
        compiler_params=params(1),
        cost_estimate=cost(10 * 10**9, 20 * 10**6),
        name="project",
    )(order, near, *([tokens] * 8), *shards, cosine, sine, *others)


def as_column(row):
    return jnp.broadcast_to(row, (8, row.shape[1])).T[:, 0:1]


def place_head(v, target, source):
    moved = v if target == source else pltpu.roll(v, HD, 1)
    lane = lax.broadcasted_iota(jnp.int32, v.shape, 1) // HD
    return jnp.where(lane == target, moved, jnp.zeros_like(moved))


def stack_heads(v):
    parts = []
    for block in range(2):
        for j in range(2):
            parts.append(place_head(v[:, block * 128 : block * 128 + 128], block, j))
    return jnp.concatenate(parts, axis=0)


def unstack_heads(v):
    blocks = []
    for block in range(2):
        pair = [v[(2 * block + j) * 256 : (2 * block + j + 1) * 256] for j in range(2)]
        blocks.append(place_head(pair[0], 0, block) + place_head(pair[1], 1, block))
    return jnp.concatenate(blocks, axis=1)


def attend_kernel(q, k, v, seg, w_out, attended, mine, other):
    row = seg[0]
    mask = jnp.where(as_column(row[:, 0:HALF]) == row, 0.0, NEGATIVE)
    queries = stack_heads(q[0].astype(F32)).astype(BF)
    scores = dot_nt(queries, k[0])
    weights = jnp.concatenate(
        [jnp.exp(scores[i * 256 : i * 256 + 256] + mask).astype(BF) for i in range(4)], axis=0
    )
    summed = dot(weights, jnp.concatenate([v[0], jnp.ones((SEQ, 128), BF)], axis=1))
    mixed = unstack_heads(summed[:, :128] / summed[:, 128:]).astype(BF)
    attended[0] = mixed
    part = dot_nt(mixed, w_out[...])

    @pl.when(pl.program_id(1) == 0)
    def _():
        mine[...] = part[0:128]
        other[...] = part[128:256]

    @pl.when(pl.program_id(1) != 0)
    def _():
        mine[...] += part[0:128]
        other[...] += part[128:256]


def attend(q_b, k_b, v_b, seg, w_out, *others):
    half = pl.BlockSpec((128, D), lambda s, p: (s, 0))
    return pl.pallas_call(
        past(attend_kernel, 5, len(others)),
        grid=(2, 2),
        in_specs=[
            pl.BlockSpec((1, HALF, 256), lambda s, p: (s, 0, p)),
            pl.BlockSpec((1, SEQ, 128), lambda s, p: (s, 0, p)),
            pl.BlockSpec((1, SEQ, 128), lambda s, p: (s, 0, p)),
            pl.BlockSpec((1, 1, SEQ), lambda s, p: (s, 0, 0)),
            pl.BlockSpec((D, 256), lambda s, p: (0, 4 + p)),
        ]
        + [HBM] * len(others),
        out_specs=[pl.BlockSpec((1, HALF, 256), lambda s, p: (s, 0, p)), half, half],
        out_shape=[
            jax.ShapeDtypeStruct((2, HALF, 512), BF),
            jax.ShapeDtypeStruct((HALF, D), F32),
            jax.ShapeDtypeStruct((HALF, D), F32),
        ],
        compiler_params=params(2),
        cost_estimate=cost(10 * 10**9, 8 * 10**6),
        name="attend",
    )(q_b, k_b, v_b, seg, w_out, *others)


def experts_to_rows(table):
    return jnp.concatenate([table[8 * k : 8 * k + 8] for k in range(4)], axis=1)


def rows_to_experts(rows):
    return jnp.concatenate([rows[:, 256 * k : 256 * k + 256] for k in range(4)], axis=0)


def route_kernel(tokens, mine, other, small, match, kept, hidden, payload, probs, totals):
    values = tokens[...].astype(F32) + mine[...] + other[...]
    hidden[...] = values
    factor = lax.rsqrt(jnp.mean(values * values, axis=1, keepdims=True) + EPS)
    rows = (values * factor * small[33:34, :]).astype(BF)
    payload[0:HALF, :] = rows
    logits = dot_nt(small[0:32, :].astype(BF), rows)
    raised = jnp.exp(logits - jnp.max(logits, axis=0, keepdims=True))
    prob = raised / jnp.sum(raised, axis=0, keepdims=True)
    probs[...] = prob
    chosen = prob * match[...]
    total = jnp.sum(chosen, axis=0, keepdims=True)
    totals[...] = total
    high, low = split(experts_to_rows(chosen / total * kept[...]))
    payload[HALF:PAD, :] = jnp.concatenate([high, low], axis=0)


def route(*args):
    return pl.pallas_call(
        past(route_kernel, 6, len(args) - 6),
        in_specs=[pl.BlockSpec(memory_space=pltpu.VMEM)] * 6 + [HBM] * (len(args) - 6),
        out_shape=[
            jax.ShapeDtypeStruct((HALF, D), F32),
            jax.ShapeDtypeStruct((PAD, D), BF),
            jax.ShapeDtypeStruct((EXPERTS, HALF), F32),
            jax.ShapeDtypeStruct((1, HALF), F32),
        ],
        compiler_params=pltpu.CompilerParams(vmem_limit_bytes=VMEM),
        cost_estimate=cost(10**8, 5 * 10**6),
        name="route",
    )(*args)


def own_row(table, lane_block, row):
    picked = jnp.zeros((8, 256), F32)
    for k in range(4):
        picked = picked + jnp.where(lane_block == k, table[:, 256 * k : 256 * k + 256], 0.0)
    number = lax.broadcasted_iota(jnp.int32, (8, 256), 0)
    return jnp.sum(jnp.where(number == row, picked, 0.0), axis=0, keepdims=True)


def expert_math(x, g, gate, w):
    pre = dot(x, w[:, 0:1024])
    grad_all = dot(g, w[:, 1024:1536])
    acts, grads, gate_dot = [], [], 0.0
    for part in range(2):
        gate_pre = pre[:, part * 512 : part * 512 + 256]
        up_pre = pre[:, part * 512 + 256 : part * 512 + 512]
        grad = grad_all[:, part * 256 : part * 256 + 256]
        sig = jax.nn.sigmoid(gate_pre)
        swish = gate_pre * sig
        act = (swish * up_pre).astype(BF).astype(F32)
        gate_dot = gate_dot + jnp.sum(act * grad, axis=1, keepdims=True)
        acts.append((act * gate).astype(BF))
        grad = grad * gate
        grads.append((grad * up_pre * sig * (1.0 + gate_pre * (1.0 - sig))).astype(BF))
        grads.append((grad * swish).astype(BF))
    act = jnp.concatenate(acts, axis=1)
    grad = jnp.concatenate(grads, axis=1)
    y = dot_nt(act, w[:, 1024:1536]).astype(BF)
    back = dot_nt(grad, w[:, 0:1024]).astype(BF)
    return y, back, act, grad, gate_dot


def pick_rows(places, first, rows):
    number = lax.broadcasted_iota(jnp.int32, (rows, 256), 0) + first
    return number == places.astype(jnp.int32)


def expert_kernel(order, where_at, x_low, x_high, c_low, c_high, w_m, w_o, *refs):
    refs = refs[len(refs) - 29 :]
    out_y, out_x, kept_x, kept_g, kept_h, more_x, more_g, more_h, pieces = refs[:9]
    x_all, c_all, wv, xs, gs, hs, picks, sums, ys, bs, total, places, gate_rows, dots = refs[9:23]
    mx, mg, mh = refs[23:26]
    in_sem, out_sem, more_sem = refs[26:]
    chunk = where_at[2]
    lane_block, row_at = where_at[0], where_at[1]
    copy = pltpu.make_async_copy
    loads = [
        copy(x_low, x_all.at[0:2], in_sem.at[0]),
        copy(c_low, c_all.at[0:2], in_sem.at[1]),
        copy(x_high, x_all.at[2:4], in_sem.at[2]),
        copy(c_high, c_all.at[2:4], in_sem.at[3]),
    ]

    def load_w(e):
        return [
            copy(w_m.at[e, :, 0:512], wv.at[e, :, 0:512], in_sem.at[4 + e]),
            copy(w_o.at[e, :, 0:512], wv.at[e, :, 512:1024], in_sem.at[6 + e]),
            copy(w_m.at[e, :, 512:768], wv.at[e, :, 1024:1280], in_sem.at[8 + e]),
            copy(w_o.at[e, :, 512:768], wv.at[e, :, 1280:1536], in_sem.at[10 + e]),
        ]

    for load in loads + load_w(0) + load_w(1):
        load.start()
    for load in loads:
        load.wait()

    def gather(h, carry):
        table = c_all[h, HALF : HALF + 8, :].astype(F32)
        gate_table = x_all[h, HALF:PAD, :].astype(F32)
        gate_table = gate_table[0:8] + gate_table[8:16]
        pick = []
        for e in range(2):
            row = own_row(table, lane_block, row_at + e)
            places[pl.ds(4 * e + h, 1), :] = row
            gate_rows[pl.ds(4 * e + h, 1), :] = own_row(gate_table, lane_block, row_at + e)
            pick.append(jnp.where(pick_rows(row, 0, MAIN), 1.0, 0.0))
        pick = jnp.concatenate(pick, axis=0).astype(BF)
        picks[h] = pick
        x = dot(pick, x_all[h, 0:HALF, :]).astype(BF)
        g = dot(pick, c_all[h, 0:HALF, :]).astype(BF)
        to = pl.ds(pl.multiple_of(h * MAIN, MAIN), MAIN)
        for e in range(2):
            xs[e, to, :] = x[e * MAIN : e * MAIN + MAIN]
            gs[e, to, :] = g[e * MAIN : e * MAIN + MAIN]
        return carry

    lax.fori_loop(0, 4, gather, 0)
    rows = pl.ds(pl.multiple_of(chunk * (4 * MAIN), 4 * MAIN), 4 * MAIN)
    sends = [copy(xs.at[e], kept_x.at[e, rows], out_sem.at[e]) for e in range(2)]
    sends += [copy(gs.at[e], kept_g.at[e, rows], out_sem.at[2 + e]) for e in range(2)]
    for send in sends:
        send.start()
    send_h = lambda e: copy(hs.at[e], kept_h.at[e, rows], out_sem.at[4 + e])
    send_x = lambda h: copy(bs.at[h], out_x.at[h], out_sem.at[6 + h])
    send_y = lambda h: copy(ys.at[h], out_y.at[order[h]], out_sem.at[10 + h])

    def gates(e, first, count):
        here = [pick_rows(places[pl.ds(4 * e + h, 1), :], first, count) for h in range(4)]
        columns = [
            jnp.sum(
                jnp.where(here[h], gate_rows[pl.ds(4 * e + h, 1), :], 0.0), axis=1, keepdims=True
            )
            for h in range(4)
        ]
        return here, jnp.concatenate(columns, axis=0)

    def spread(here, gate_dot, count, h):
        part = gate_dot[h * count : h * count + count]
        return jnp.sum(jnp.where(here[h], part, 0.0), axis=0, keepdims=True)

    def math(e, carry):
        here, gate = gates(e, 0, MAIN)
        for load in load_w(e):
            load.wait()
        y, back, act, grad, gate_dot = expert_math(xs[e], gs[e], gate, wv.at[e])
        hs[e, :, 0:512] = act
        hs[e, :, 512:1536] = grad
        send_h(e).start()
        to = pl.ds(pl.multiple_of(e * MAIN, MAIN), MAIN)
        for h in range(4):
            sums[h, to, 0:D] = y[h * MAIN : h * MAIN + MAIN]
            sums[h, to, D : 2 * D] = back[h * MAIN : h * MAIN + MAIN]
            dots[pl.ds(4 * e + h, 1), :] = spread(here, gate_dot, MAIN, h)
        return carry

    lax.fori_loop(0, 2, math, 0)

    counts = []
    for e in range(2):
        most = jnp.max(places[4 * e : 4 * e + 4, :]).astype(jnp.int32) + 1
        counts.append((jnp.maximum(most - MAIN, 0) + MORE - 1) // MORE)
        pieces[e] = jnp.zeros((8, 128), F32) + counts[e].astype(F32)

    @pl.when(counts[0] + counts[1] > 0)
    def _():
        total[...] = jnp.zeros_like(total)

        def piece(n, carry):
            e = jnp.where(n < counts[0], 0, 1)
            i = n - e * counts[0]
            here, gate = gates(e, MAIN + i * MORE, MORE)
            pick = [jnp.where(v, 1.0, 0.0).astype(BF) for v in here]
            for h in range(4):
                to = slice(h * MORE, h * MORE + MORE)
                mx[to, :] = dot(pick[h], x_all[h, 0:HALF, :]).astype(BF)
                mg[to, :] = dot(pick[h], c_all[h, 0:HALF, :]).astype(BF)
            y, back, act, grad, gate_dot = expert_math(mx[...], mg[...], gate, wv.at[e])
            mh[:, 0:512] = act
            mh[:, 512:1536] = grad
            to = pl.ds(pl.multiple_of(i * 4 * MORE, 4 * MORE), 4 * MORE)
            extra = [
                copy(v, far.at[e, to], more_sem.at[k])
                for k, (v, far) in enumerate(((mx, more_x), (mg, more_g), (mh, more_h)))
            ]
            for send in extra:
                send.start()
            both = jnp.concatenate([y, back], axis=1)
            for h in range(4):
                part = both[h * MORE : h * MORE + MORE]
                total[h * HALF : h * HALF + HALF, :] += dot_tn(pick[h], part)
                dots[pl.ds(4 * e + h, 1), :] += spread(here, gate_dot, MORE, h)
            for send in extra:
                send.wait()
            return carry

        lax.fori_loop(0, counts[0] + counts[1], piece, 0)

    def scatter(h, carry):
        out = dot_tn(picks[h], sums[h])
        ys[h] = out[:, 0:D].astype(BF)
        bs[h, 0:HALF, :] = out[:, D : 2 * D].astype(BF)
        row = lax.broadcasted_iota(jnp.int32, (8, 256), 0)
        table = jnp.where(row == row_at, dots[pl.ds(h, 1), :], 0.0)
        table = table + jnp.where(row == row_at + 1, dots[pl.ds(4 + h, 1), :], 0.0)
        table = [jnp.where(lane_block == k, table, 0.0) for k in range(4)]
        high, low = split(jnp.concatenate(table, axis=1))
        bs[h, HALF:PAD, :] = jnp.concatenate([high, low], axis=0)

        @pl.when(counts[0] + counts[1] > 0)
        def _():
            at = pl.ds(pl.multiple_of(h * HALF, HALF), HALF)
            ys[h] = (ys[h].astype(F32) + total[at, 0:D]).astype(BF)
            bs[h, 0:HALF, :] = (bs[h, 0:HALF, :].astype(F32) + total[at, D : 2 * D]).astype(BF)

        send_x(h).start()
        send_y(h).start()
        return carry

    lax.fori_loop(0, 4, scatter, 0)
    for send in sends:
        send.wait()
    for e in range(2):
        send_h(e).wait()
    for h in range(4):
        send_x(h).wait()
        send_y(h).wait()


def expert_chunk(order, where_at, x, cotangents, mine, other, kept, *others):
    rows, more = 4 * MAIN, 4 * MORE * PIECES
    widths = (D, D, 1536)
    shape = lambda *v: jax.ShapeDtypeStruct(v, BF)
    vmem = lambda *v: pltpu.VMEM(v, BF)
    aliases = {8: 0, 9: 2, 10: 3, 11: 4} if kept else {}
    return pl.pallas_call(
        expert_kernel,
        grid_spec=pltpu.PrefetchScalarGridSpec(
            num_scalar_prefetch=2,
            grid=(1,),
            in_specs=[HBM] * (6 + len(kept) + len(others)),
            out_specs=[HBM] * 8 + [pl.BlockSpec((2, 8, 128), lambda i, r, w: (0, 0, 0))],
            scratch_shapes=[
                vmem(4, PAD, D),
                vmem(4, PAD, D),
                vmem(2, D, 1536),
                vmem(2, rows, D),
                vmem(2, rows, D),
                vmem(2, rows, 1536),
                vmem(4, 2 * MAIN, 256),
                vmem(4, 2 * MAIN, 2 * D),
                vmem(4, HALF, D),
                vmem(4, PAD, D),
                pltpu.VMEM((1024, 2 * D), F32),
                pltpu.VMEM((8, 256), F32),
                pltpu.VMEM((8, 256), F32),
                pltpu.VMEM((8, 256), F32),
                vmem(4 * MORE, D),
                vmem(4 * MORE, D),
                vmem(4 * MORE, 1536),
                pltpu.SemaphoreType.DMA((12,)),
                pltpu.SemaphoreType.DMA((14,)),
                pltpu.SemaphoreType.DMA((3,)),
            ],
        ),
        out_shape=[shape(N_FSDP, HALF, D), shape(4, PAD, D)]
        + [shape(2, 4 * rows, n) for n in widths]
        + [shape(2, more, n) for n in widths]
        + [jax.ShapeDtypeStruct((2, 8, 128), F32)],
        input_output_aliases=aliases,
        compiler_params=params(1),
        cost_estimate=cost(14 * 10**9, 30 * 10**6),
        name="experts",
    )(order, where_at, *x, *cotangents, mine, other, *kept, *others)


def expert_weight_kernel(place, x, g, act, grad, *refs):
    more, counts, (down, gate_up), (mx, mg, mh) = refs[:12], refs[12:16], refs[-5:-3], refs[-3:]
    out = refs[-6]
    expert, part = pl.program_id(0), pl.program_id(1)
    down[...] = dot_tn(g[0], act[0])
    gate_up[...] = dot_tn(x[0], grad[0])
    for chunk in range(4):
        count = jnp.max(counts[chunk][0]).astype(jnp.int32)

        @pl.when(count > 0)
        def _(chunk=chunk, count=count):
            def piece(i, carry):
                rows = pl.ds(pl.multiple_of(i * 4 * MORE, 4 * MORE), 4 * MORE)
                for ref, to in zip(more[3 * chunk : 3 * chunk + 3], (mx, mg, mh)):
                    pltpu.sync_copy(ref.at[expert, rows], to)
                for p in range(2):

                    @pl.when(part == p)
                    def _(p=p):
                        at = p * 256
                        down[...] += dot_tn(mg[...], mh[:, at : at + 256])
                        at = 512 + p * 512
                        gate_up[...] += dot_tn(mx[...], mh[:, at : at + 512])

                return carry

            lax.fori_loop(0, count, piece, 0)

    for c in range(4):
        at = slice(c * 256, c * 256 + 256)
        out[c, 0, 0, :, 0:512] = gate_up[at, :].astype(BF)
        out[c, 0, 0, :, 512:768] = down[at, :].astype(BF)


def expert_weights(place, kept, more, counts, *others):
    rows = 16 * MAIN
    by_expert = lambda e, p, r: (e, 0, 0)
    return pl.pallas_call(
        expert_weight_kernel,
        grid_spec=pltpu.PrefetchScalarGridSpec(
            num_scalar_prefetch=1,
            grid=(2, 2),
            in_specs=[
                pl.BlockSpec((1, rows, D), by_expert),
                pl.BlockSpec((1, rows, D), by_expert),
                pl.BlockSpec((1, rows, 256), lambda e, p, r: (e, 0, p)),
                pl.BlockSpec((1, rows, 512), lambda e, p, r: (e, 0, 1 + p)),
            ]
            + [HBM] * 12
            + [pl.BlockSpec((1, 8, 128), by_expert)] * 4
            + [HBM] * len(others),
            out_specs=pl.BlockSpec(
                (4, 1, 1, 256, 768),
                lambda e, p, r: (0, jnp.where(p == 0, r[0], 1 - r[0]), e, 0, 0),
            ),
            scratch_shapes=[
                pltpu.VMEM((D, 256), F32),
                pltpu.VMEM((D, 512), F32),
                pltpu.VMEM((4 * MORE, D), BF),
                pltpu.VMEM((4 * MORE, D), BF),
                pltpu.VMEM((4 * MORE, 1536), BF),
            ],
        ),
        out_shape=jax.ShapeDtypeStruct((4, 2, 2, 256, 768), BF),
        compiler_params=params(2),
        cost_estimate=cost(20 * 10**9, 30 * 10**6),
        name="expert_weights",
    )(place, kept[0], kept[1], kept[2], kept[2], *more, *counts, *others)


def route_back_kernel(
    own, first, second, third, cotangent, hidden, small, normed, probs, totals, match,
    grad_hidden, grad_branch, grad_router, grad_gain,
):
    summed = own[...].astype(F32) + first[...].astype(F32)
    summed = summed + (second[...].astype(F32) + third[...].astype(F32))
    tables = summed[HALF:PAD, :]
    grad_gates = rows_to_experts(tables[0:8] + tables[8:16])
    prob, total = probs[...], totals[...]
    chosen = prob * match[...]
    shared = jnp.sum(grad_gates * chosen, axis=0, keepdims=True) / (total * total)
    grad_prob = (grad_gates / total - shared) * match[...]
    grad_logits = prob * (grad_prob - jnp.sum(prob * grad_prob, axis=0, keepdims=True))
    high, low = split(grad_logits)
    grad_router[...] = dot(high, normed[0:HALF, :]) + dot(low, normed[0:HALF, :])
    router = small[0:32, :].astype(BF)
    grad_normed = summed[0:HALF, :] + dot_tn(high, router) + dot_tn(low, router)
    values = hidden[...]
    factor = lax.rsqrt(jnp.mean(values * values, axis=1, keepdims=True) + EPS)
    grad_gain[...] = jnp.sum(grad_normed * values * factor, axis=0, keepdims=True)
    weighted = grad_normed * small[33:34, :]
    mean = jnp.mean(weighted * values, axis=1, keepdims=True)
    grad = cotangent[0:HALF, :].astype(F32) + factor * weighted - values * (factor * factor * factor * mean)
    grad_hidden[...] = grad
    grad_branch[...] = grad.astype(BF)


def route_back(handed, *args):
    n, others, shapes = len(handed), len(args) - 11, [jax.ShapeDtypeStruct(v.shape, v.dtype) for v in handed]
    vmem = pl.BlockSpec(memory_space=pltpu.VMEM)
    kernel = past(route_back_kernel, 11, others + n)
    return pl.pallas_call(
        lambda *refs: kernel(*refs[n:]),
        in_specs=[HBM] * n + [vmem] * 11 + [HBM] * others,
        out_specs=[HBM] * n + [vmem] * 4,
        input_output_aliases={i: i for i in range(n)},
        out_shape=shapes
        + [
            jax.ShapeDtypeStruct((HALF, D), F32),
            jax.ShapeDtypeStruct((HALF, D), BF),
            jax.ShapeDtypeStruct((EXPERTS, D), F32),
            jax.ShapeDtypeStruct((1, D), F32),
        ],
        compiler_params=pltpu.CompilerParams(vmem_limit_bytes=VMEM),
        cost_estimate=cost(4 * 10**9, 6 * 10**6),
        name="route_back",
    )(*handed, *args)


def norm_back_heads(grad, proj, gain, cosine, sine):
    turned = grad * cosine - swap_halves(grad) * sine
    factor = lax.rsqrt(head_mean(proj * proj) + EPS)
    weighted = turned * gain
    mean = head_mean(weighted * proj)
    back = factor * weighted - proj * (factor * factor * factor * mean)
    return back, jnp.sum(turned * proj * factor, axis=0, keepdims=True)


def attend_back_kernel(
    q, q_proj, k, k_proj, v, seg, branch_m, branch_o, w_out, attended,
    cosine, sine, heads, grad_q, grad_k, grad_v, gains,
):
    row = seg[0]
    mask = jnp.where(as_column(row) == row[:, 0:HALF], 0.0, NEGATIVE)
    keys, values = k[0], v[0]
    grad_branch = jnp.concatenate([branch_m[...], branch_o[...]], axis=0)
    grad_mixed = dot(grad_branch, w_out[...]).astype(BF).astype(F32)
    queries = stack_heads(q[0].astype(F32)).astype(BF)
    grads = stack_heads(grad_mixed).astype(BF)
    high, low = split(stack_heads(attended[0].astype(F32) * grad_mixed))
    ones = jnp.ones((8, 256), BF)
    row_dot = dot_nt(ones, jnp.concatenate([high, low], axis=1))[0:1]
    scores = dot_nt(keys, queries)
    grad_probs = dot_nt(values, grads)
    probs_b, grad_scores = [], []
    for i in range(4):
        at = slice(i * 256, i * 256 + 256)
        raised = jnp.exp(scores[:, at] + mask)
        probs = raised * (1.0 / jnp.sum(raised, axis=0, keepdims=True))
        probs_b.append(probs.astype(BF))
        grad_scores.append((probs * (grad_probs[:, at] - row_dot[:, at])).astype(BF))
    probs_b = jnp.concatenate(probs_b, axis=1)
    grad_scores = jnp.concatenate(grad_scores, axis=1)
    grad_v[0] = dot(probs_b, grads).astype(BF)
    sum_k = dot(grad_scores, queries)
    sum_q = unstack_heads(dot_tn(grad_scores, keys) * 0.125)
    cos, sin = cosine[...], sine[...]
    back, gain_q = norm_back_heads(
        sum_q, q_proj[0], twice(heads[0:1, :]), twice(cos[0:256]), twice(sin[0:256])
    )
    grad_q[0] = back.astype(BF)
    wide = lambda value: jnp.concatenate([value[0:512], value[512:1024]], axis=1)
    back, gain_k = norm_back_heads(
        wide(sum_k), wide(k_proj[0]), twice(heads[1:2, :]), wide(cos), wide(sin)
    )
    grad_k[0, 0:512, :] = back[:, 0:128].astype(BF)
    grad_k[0, 512:1024, :] = back[:, 128:256].astype(BF)
    part = jnp.concatenate([gain_q, gain_k, jnp.zeros((6, 256), F32)], axis=0)

    @pl.when((pl.program_id(0) == 0) & (pl.program_id(1) == 0))
    def _():
        gains[...] = part

    @pl.when((pl.program_id(0) != 0) | (pl.program_id(1) != 0))
    def _():
        gains[...] += part


def attend_back(
    q_b, q_proj, k_b, k_proj, v_b, seg, branch_m, branch_o, w_out, attended,
    cosine, sine, heads,
):
    queries = pl.BlockSpec((1, HALF, 256), lambda s, p: (s, 0, p))
    keys = pl.BlockSpec((1, SEQ, 128), lambda s, p: (s, 0, p))
    table = pl.BlockSpec((SEQ, 128), lambda s, p: (0, 0))
    gain = pl.BlockSpec((8, 128), lambda s, p: (0, 0))
    half = pl.BlockSpec((128, D), lambda s, p: (s, 0))
    return pl.pallas_call(
        attend_back_kernel,
        grid=(2, 2),
        in_specs=[
            queries, queries, keys, keys, keys,
            pl.BlockSpec((1, 1, SEQ), lambda s, p: (s, 0, 0)),
            half, half,
            pl.BlockSpec((D, 256), lambda s, p: (0, 4 + p)),
            queries, table, table, gain,
        ],
        out_specs=[queries, keys, keys, pl.BlockSpec((8, 256), lambda s, p: (0, 0))],
        out_shape=[
            jax.ShapeDtypeStruct((2, HALF, 512), BF),
            jax.ShapeDtypeStruct((2, SEQ, 256), BF),
            jax.ShapeDtypeStruct((2, SEQ, 256), BF),
            jax.ShapeDtypeStruct((8, 256), F32),
        ],
        compiler_params=params(2),
        cost_estimate=cost(18 * 10**9, 16 * 10**6),
        name="attend_back",
    )(
        q_b, q_proj, k_b, k_proj, v_b, seg, branch_m, branch_o, w_out, attended,
        cosine, sine, heads,
    )


def weight_grads_kernel(
    place, normed, gq, gk, gv, branch_m, branch_o, mixed, router, gain, head_gains,
    out_0, out_1, out_2, out_3, out, sem,
):
    step = pl.program_id(0)
    rows = jnp.concatenate([normed[0], normed[1]], axis=0)
    own = jnp.concatenate([normed[0, 0:256, :], normed[1, 0:256, :]], axis=0)
    keys = jnp.concatenate(
        [
            jnp.concatenate([gk[0], gk[1]], axis=0),
            jnp.concatenate([gv[0], gv[1]], axis=0),
        ],
        axis=1,
    )
    queries = jnp.concatenate([gq[0], gq[1]], axis=0)
    branch = jnp.concatenate(
        [branch_m[0:128], branch_o[0:128], branch_m[128:256], branch_o[128:256]], axis=0
    )
    heads = jnp.concatenate([mixed[0], mixed[1]], axis=0)
    at = lax.broadcasted_iota(jnp.int32, (256, 256), 1)
    share = 4 * (at // HD + 4 * step) + at % HD
    spread = (lax.broadcasted_iota(jnp.int32, (256, 256), 0) % HD == share) & (at % HD < 4)
    spread = jnp.where(spread, 1.0, 0.0).astype(BF)
    high, low = split(head_gains[...])
    spread = dot(high, spread) + dot(low, spread)
    row = lax.broadcasted_iota(jnp.int32, (8, 256), 0)
    last = jnp.where(row == 0, gain[...], 0.0)
    last = last + jnp.where(row == 1, spread[0:1], 0.0) + jnp.where(row == 2, spread[1:2], 0.0)
    small = jnp.concatenate([router[...], last, jnp.zeros((88, 256), F32)], axis=0)
    parts = (
        (0, 512, dot_tn(own, queries).astype(BF)),
        (512, 1024, dot_tn(rows, keys).astype(BF)),
        (1024, 1536, dot_tn(branch, heads).astype(BF)),
        (1536, 1664, small.T.astype(BF)),
    )
    for i in range(4):
        to = place[4 * step + i]
        for low, high, value in parts:
            out[to, :, low:high] = value[i * 64 : i * 64 + 64]

    @pl.when(step == 3)
    def _():
        sends = [
            pltpu.make_async_copy(out.at[4 * i : 4 * i + 4], to, sem.at[i])
            for i, to in enumerate((out_0, out_1, out_2, out_3))
        ]
        for send in sends:
            send.start()
        for send in sends:
            send.wait()


def weight_grads(place, *args):
    fixed = lambda i, r: (0, 0, 0)
    column = pl.BlockSpec((HALF, 256), lambda i, r: (0, i))
    return pl.pallas_call(
        past(weight_grads_kernel, 11, len(args) - 10),
        grid_spec=pltpu.PrefetchScalarGridSpec(
            num_scalar_prefetch=1,
            grid=(4,),
            in_specs=[
                pl.BlockSpec((2, SEQ, 256), lambda i, r: (0, 0, i)),
                pl.BlockSpec((2, HALF, 512), fixed),
                pl.BlockSpec((2, SEQ, 256), fixed),
                pl.BlockSpec((2, SEQ, 256), fixed),
                column,
                column,
                pl.BlockSpec((2, HALF, 512), fixed),
                pl.BlockSpec((EXPERTS, 256), lambda i, r: (0, i)),
                pl.BlockSpec((1, 256), lambda i, r: (0, i)),
                pl.BlockSpec((8, 256), lambda i, r: (0, 0)),
            ]
            + [HBM] * (len(args) - 10),
            out_specs=[HBM] * 4,
            scratch_shapes=[pltpu.VMEM((N_FSDP, 64, 1664), BF), pltpu.SemaphoreType.DMA((4,))],
        ),
        out_shape=[jax.ShapeDtypeStruct((4, 64, 1664), BF)] * 4,
        compiler_params=params(1),
        cost_estimate=cost(9 * 10**9, 16 * 10**6),
        name="weight_grads",
    )(place, *args)


def input_grads_kernel(gq, gk, gv, w, mine, other):
    part = dot_nt(jnp.concatenate([gk[0], gv[0]], axis=1), w[:, 512:1024])
    own = dot_nt(gq[0], w[:, 0:512])
    for c in range(4):
        for parity, out in enumerate((mine, other)):
            at = slice(c * 256 + parity * 128, c * 256 + parity * 128 + 128)
            value = part[at] + own[at] if c == 0 else part[at]
            out[c] = value.astype(BF)


def input_grads(gq, gk, gv, weights, *others):
    by = lambda s: (s, 0, 0)
    half = pl.BlockSpec((4, 128, D), lambda s: (0, s, 0))
    return pl.pallas_call(
        past(input_grads_kernel, 4, len(others)),
        grid=(2,),
        in_specs=[
            pl.BlockSpec((1, HALF, 512), by),
            pl.BlockSpec((1, SEQ, 256), by),
            pl.BlockSpec((1, SEQ, 256), by),
            pl.BlockSpec((D, 1024), lambda s: (0, 0)),
        ]
        + [HBM] * len(others),
        out_specs=[half, half],
        out_shape=[jax.ShapeDtypeStruct((4, HALF, D), BF)] * 2,
        compiler_params=params(1),
        cost_estimate=cost(6 * 10**9, 12 * 10**6),
        name="input_grads",
    )(gq, gk, gv, weights, *others)


def finish_kernel(own, first, second, third, tokens, grad_hidden, small, out):
    values = tokens[...].astype(F32)
    factor = lax.rsqrt(jnp.mean(values * values, axis=1, keepdims=True) + EPS)
    summed = own[...].astype(F32) + first[...].astype(F32)
    summed = summed + (second[...].astype(F32) + third[...].astype(F32))
    weighted = summed * small[32:33, :]
    mean = jnp.mean(weighted * values, axis=1, keepdims=True)
    out[...] = grad_hidden[...] + factor * weighted - values * (factor * factor * factor * mean)


def finish(*args):
    return pl.pallas_call(
        past(finish_kernel, 7, len(args) - 7),
        in_specs=[pl.BlockSpec(memory_space=pltpu.VMEM)] * 7 + [HBM] * (len(args) - 7),
        out_shape=jax.ShapeDtypeStruct((HALF, D), F32),
        compiler_params=pltpu.CompilerParams(vmem_limit_bytes=VMEM),
        cost_estimate=cost(10**7, 6 * 10**6),
        name="finish",
    )(*args)


def settle_kernel(
    own, first, second, third, w_query, w_key, w_value, gain, g_query, g_key, g_value, g_out, sums
):
    summed = own[...].astype(F32) + first[...].astype(F32)
    summed = summed + (second[...].astype(F32) + third[...].astype(F32))
    g_query[...] = summed[:, 0:512]
    g_key[...] = summed[:, 512:768]
    g_value[...] = summed[:, 768:1024]
    g_out[...] = summed[:, 1024:1536]
    part = jnp.sum(w_query[...].astype(F32) * summed[:, 0:512], axis=1, keepdims=True)
    part = part + jnp.sum(w_key[...].astype(F32) * summed[:, 512:768], axis=1, keepdims=True)
    part = part + jnp.sum(w_value[...].astype(F32) * summed[:, 768:1024], axis=1, keepdims=True)
    diagonal = lax.broadcasted_iota(jnp.int32, (64, 64), 0) == lax.broadcasted_iota(
        jnp.int32, (64, 64), 1
    )
    column = jnp.sum(jnp.where(diagonal, gain[...].astype(F32), 0.0), axis=1, keepdims=True)
    lane = lax.broadcasted_iota(jnp.int32, (64, 128), 1)
    sums[...] = jnp.where(lane == 35, part / column, summed[:, 1536:1664])


def settle(*args):
    return pl.pallas_call(
        past(settle_kernel, 8, len(args) - 8),
        in_specs=[pl.BlockSpec(memory_space=pltpu.VMEM)] * 8 + [HBM] * (len(args) - 8),
        out_shape=[jax.ShapeDtypeStruct((64, n), F32) for n in (512, 256, 256, 512, 128)],
        compiler_params=pltpu.CompilerParams(vmem_limit_bytes=VMEM),
        cost_estimate=cost(10**6, 2 * 10**6),
        name="settle",
    )(*args)


def join_kernel(where, mine, far, out):
    @pl.when(pl.program_id(0) == 0)
    def _():
        out[...] = mine[...].reshape(2, 4, 1, 32, D)

    @pl.when(pl.program_id(0) == 1)
    def _():
        out[...] = far[...].reshape(2, 4, 1, 32, D)


def join(where, mine, far, *others):
    whole = pl.BlockSpec((HALF, D), lambda i, r: (0, 0))
    return pl.pallas_call(
        past(join_kernel, 3, len(others)),
        grid_spec=pltpu.PrefetchScalarGridSpec(
            num_scalar_prefetch=1,
            grid=(2,),
            in_specs=[whole, whole] + [HBM] * len(others),
            out_specs=pl.BlockSpec(
                (2, 4, 1, 32, D), lambda i, r: (0, 0, jnp.where(i == 0, r[0], 1 - r[0]), 0, 0)
            ),
        ),
        out_shape=jax.ShapeDtypeStruct((2, 4, 2, 32, D), mine.dtype),
        compiler_params=params(1),
        cost_estimate=cost(10**6, 4 * 10**6),
        name="join",
    )(where, mine, far, *others).reshape(2, 256, D)


def ring_pairs(stage, step):
    pairs = []
    for x in range(4):
        for z in range(4):
            for t in range(2):
                if (stage == 0) == (t == 0):
                    far = ((x + step) % 4) * 4 + z
                else:
                    far = x * 4 + (z + step) % 4
                pairs.append(((x * 4 + z) * 2 + t, far * 2 + t))
    return pairs


def ring(value, stage, step):
    return lax.ppermute(value, ("fsdp", "tensor"), ring_pairs(stage, step))


def shift(value, step):
    return lax.ppermute(value, "context", [(i, (i + step) % 4) for i in range(4)])


def swap_cores(value):
    return lax.ppermute(value, "tensor", [(0, 1), (1, 0)])


def gather_row(block, stage=0):
    return block, ring(block, stage, -1), ring(block, stage, 1), ring(block, stage, 2)


def gather_chunks(low, high):
    behind_low, ahead_high = ring(low, 1, 1), ring(high, 1, -1)
    behind_high, ahead_low = ring(high, 1, 1), ring(low, 1, -1)
    far = ring(behind_low, 1, 1), ring(ahead_high, 1, -1)
    return (low, high), (ahead_low, ahead_high), (behind_low, behind_high), far


def scatter_parts(parts, move):
    own, ahead, behind, far = parts
    return own, move(ahead, 1), move(behind, -1), move(far, 2)


def total_of(parts):
    first, second, third, fourth = (p.astype(F32) for p in parts)
    return (first + second) + (third + fourth)


def along(stage):
    return lambda v, n: ring(v, stage, n)


def local(
    tokens, segments, routes, attention_gain, w_query, w_key, w_value, w_out, query_gain,
    key_gain, feedforward_gain, router, w_gate, w_up, w_down, cotangent,
):
    f, c, t = lax.axis_index("fsdp"), lax.axis_index("context"), lax.axis_index("tensor")
    x_at, z_at = f // 4, f % 4
    steps = jnp.array([0, 1, 3, 2], jnp.int32)
    as_row = lambda *v: jnp.stack([jnp.asarray(i, jnp.int32) for i in v])
    all_x, all_z = (x_at + steps) % 4, (z_at + steps) % 4
    order = jnp.where(
        t == 0, all_x[None, :] * 4 + all_z[:, None], all_x[:, None] * 4 + all_z[None, :]
    ).astype(jnp.int32)
    far_x, far_z = steps[(jnp.arange(4) - x_at) % 4], steps[(jnp.arange(4) - z_at) % 4]
    place = jnp.where(
        t == 0, far_x[:, None] + 4 * far_z[None, :], 4 * far_x[:, None] + far_z[None, :]
    )
    place = place.reshape(-1).astype(jnp.int32)
    near = ((c + steps) % 4)[:, None] * 2 + jnp.stack([t, 1 - t])[None, :]
    near = near.reshape(8)

    shard = pack(
        as_row(f), w_query, w_key, w_value, w_out, router, attention_gain[None, :],
        feedforward_gain[None, :], query_gain[None, :], key_gain[None, :],
    )
    shards = jnp.stack(gather_row(shard))
    shards = gather_row(shards, 1)

    parity = lambda v, p: lax.dynamic_index_in_dim(
        v.reshape(2, 4, 2, 32, D), p, 2, keepdims=False
    ).reshape(HALF, D)
    tokens_m = parity(tokens, t)
    tokens_all = lax.all_gather(tokens_m, ("context", "tensor"), axis=0)
    picked = routes.reshape(ROWS, TOPK).T
    experts = jnp.arange(EXPERTS, dtype=jnp.int32)
    match = jnp.any(picked[:, None, :] == experts[None, :, None], axis=0)
    before = lambda n: (jnp.arange(n)[:, None] < jnp.arange(n)[None, :]).astype(BF)
    kept = match & (dot(match.astype(BF), before(ROWS)) < CAP)
    half = lambda v: lax.dynamic_index_in_dim(
        v.astype(F32).reshape(EXPERTS, 2, 4, 2, 32), t, 3, keepdims=False
    ).reshape(EXPERTS, HALF)
    match_half, kept_half = half(match), half(kept)
    local_place = dot(kept_half.astype(BF), before(HALF))
    table = experts_to_rows(jnp.where(kept_half > 0, local_place, -1.0).astype(BF))
    cot_payload = pack_cotangent(as_row(t), cotangent, table, *shards[1:])
    cot_row = gather_row(cot_payload)

    packed = jnp.concatenate([w_gate, w_up, w_down], axis=2)
    packed_o = swap_cores(packed)
    seg = segments.reshape(2, 4, 4, 2, 32).transpose(0, 1, 3, 2, 4).reshape(2, 8, 128)
    seg = jnp.take(seg, near, axis=1).reshape(2, 1, SEQ).astype(F32)

    cosine, sine = (jnp.asarray(v) for v in rotary_tables())
    weights, small, heads, cosine, sine, normed1, k_proj, k_b, v_b, q_proj, q_b = project(
        order.reshape(-1), near.astype(jnp.int32), tokens_all, shards, cosine, sine, packed_o, seg
    )
    cot_chunks = gather_chunks(*stack_pairs(cot_row, small))
    attended, branch_m, branch_o = attend(q_b, k_b, v_b, seg, weights, cot_chunks[0][0])
    hidden1, payload, probs, totals = route(
        tokens_m, branch_m, swap_cores(branch_o), small, match_half, kept_half,
        *cot_chunks[1], *cot_chunks[2],
    )

    chunks = gather_chunks(*stack_pairs(gather_row(payload), *cot_chunks[3]))
    outs_x, more, counts, carried = {}, [], [], ()
    for slot, i in enumerate((0, 1, 3, 2)):
        where_at = as_row(f // 4, 2 * (f % 4), slot)
        result = expert_chunk(
            order[i], where_at, chunks[i], cot_chunks[i], packed, packed_o, carried
        )
        carried = result[0], *result[2:5]
        outs_x[i] = result[1]
        more += result[5:8]
        counts.append(result[8])
    parts = scatter_parts([outs_x[i] for i in range(4)], along(1))
    grads_e = expert_weights(as_row(t), carried[1:], more, counts, parts[1], parts[3])
    back, grads_e = add_blocks(parts, (grads_e,))
    back = scatter_parts(back, along(0))

    grads_e = lax.psum_scatter(
        grads_e.reshape(8, 2, 256, 768), ("context", "tensor"), scatter_dimension=0
    )
    mixed, grad_hidden, grad_branch, grad_router, grad_gain2 = route_back(
        [carried[0]], *back, cot_payload, hidden1, small, payload, probs, totals, match_half
    )
    mixed = lax.psum_scatter(mixed, "fsdp", scatter_dimension=0)
    branch_far = swap_cores(grad_branch)
    gq, gk, gv, gains = attend_back(
        q_b, q_proj, k_b, k_proj, v_b, seg,
        grad_branch, branch_far, weights, attended, cosine, sine, heads,
    )
    grads_w = weight_grads(
        place, normed1, gq, gk, gv, grad_branch, branch_far, attended, grad_router, grad_gain2, gains,
    )
    gin_m, gin_o = input_grads(gq, gk, gv, weights, grads_w[0])
    (sent,) = add_blocks((gin_m, swap_cores(gin_o)))
    gin = scatter_parts(sent, shift)
    grad_tokens = finish(*gin, tokens_m, grad_hidden, small, grads_e)

    grads_w = scatter_parts(grads_w, along(1))
    (grads_w,) = add_blocks(grads_w, (), *sent[1:])
    grads_w = [v[None] for v in scatter_parts(grads_w, along(0))]
    ((grads_w,),) = add_blocks(grads_w, (), *gin[1:])
    g_query, g_key, g_value, g_out, sums = settle(
        *scatter_parts([grads_w] * 4, shift), w_query, w_key, w_value, attention_gain[None, :],
        grad_tokens,
    )
    sums = sums + swap_cores(sums)

    both = lambda v, *others: join(as_row(t), v, swap_cores(v), *others)
    block_half = (hidden1 + mixed.astype(F32)).astype(BF)
    grads_e = grads_e.astype(F32)
    return (
        both(block_half, sums),
        both(grad_tokens),
        sums[:, 35],
        g_query,
        g_key,
        g_value,
        g_out,
        sums[0:4, 33],
        sums[0:4, 34],
        sums[:, 32],
        sums[:, 0:32],
        grads_e[:, :, 0:256],
        grads_e[:, :, 256:512],
        grads_e[:, :, 512:768],
    )


def solution(mesh):
    in_specs = (
        P("fsdp", "context", None),
        P("fsdp", None),
        P("fsdp", "context", None),
        P("fsdp"),
        P("fsdp", "tensor"),
        P("fsdp", "tensor"),
        P("fsdp", "tensor"),
        P("fsdp", "tensor"),
        P("fsdp"),
        P("fsdp"),
        P("fsdp"),
        P("fsdp", None),
        P("fsdp", None, "tensor"),
        P("fsdp", None, "tensor"),
        P("fsdp", None, "tensor"),
        P("fsdp", "context", None),
    )
    out_specs = (
        P("fsdp", "context", None),
        P("fsdp", "context", None),
        P("fsdp"),
        P("fsdp", "tensor"),
        P("fsdp", "tensor"),
        P("fsdp", "tensor"),
        P("fsdp", "tensor"),
        P("fsdp"),
        P("fsdp"),
        P("fsdp"),
        P("fsdp", None),
        P("fsdp", "context", "tensor"),
        P("fsdp", "context", "tensor"),
        P("fsdp", "context", "tensor"),
    )
    return jax.shard_map(local, mesh=mesh, in_specs=in_specs, out_specs=out_specs, check_vma=False)
```

```python
import functools

import jax
import jax.numpy as jnp
import numpy as np
from jax import lax
from jax.experimental import pallas as pl
from jax.experimental.pallas import tpu as pltpu
from jax.sharding import PartitionSpec as P

HD = 64
EXPERTS = 32
TOPK = 8
SEQ = 1024
D = 1024
ROWS = 512
HALF = 256
CAP = 160
MAIN = 96
TILES = -(-CAP // MAIN)
PAD = 272
N_FSDP = 16
N_CONTEXT = 4
EPS = 1e-06
NEGATIVE = -1e30
VMEM = 62 * 1024 * 1024
BF = jnp.bfloat16
F32 = jnp.float32
NT = (((1,), (1,)), ((), ()))
TN = (((0,), (0,)), ((), ()))


def dot(a, b):
    return jnp.dot(a, b, preferred_element_type=F32)


def dot_nt(a, b):
    return lax.dot_general(a, b, NT, preferred_element_type=F32)


def dot_tn(a, b):
    return lax.dot_general(a, b, TN, preferred_element_type=F32)


def split(v):
    high = v.astype(BF)
    return high, (v - high.astype(F32)).astype(BF)


def params(grid_dims):
    return pltpu.CompilerParams(
        dimension_semantics=("arbitrary",) * grid_dims, vmem_limit_bytes=VMEM
    )


def cost(flops, moved):
    return pl.CostEstimate(flops=flops, bytes_accessed=moved, transcendentals=0)


HBM = pl.BlockSpec(memory_space=pltpu.HBM)


def past(kernel, inputs, others):
    return lambda *refs: kernel(*refs[:inputs], *refs[inputs + others :])


def head_mean(v):
    rows = lax.broadcasted_iota(jnp.int32, (512, 256), 0) % 256 // HD
    cols = lax.broadcasted_iota(jnp.int32, (512, 256), 1) // HD
    block = jnp.where(rows == cols, 1.0, 0.0).astype(BF)
    return dot(jnp.concatenate(split(v), axis=1), block) * (1.0 / HD)


def swap_halves(v):
    lane = lax.broadcasted_iota(jnp.int32, v.shape, 1) % HD
    width = v.shape[1]
    return jnp.where(lane < HD // 2, pltpu.roll(v, width - 32, 1), pltpu.roll(v, 32, 1))


def twice(v):
    return jnp.concatenate([v, v], axis=1)


def rotary_tables():
    middle = HD // 2
    inverse = 10000.0 ** (-(2.0 * np.arange(middle, dtype=np.float64) / HD))
    inverse = inverse.astype(np.float32)
    angles = np.arange(SEQ, dtype=np.float32)[:, None] * inverse[None, :]
    angles = angles.astype(np.float64)
    cosine, sine = np.cos(angles).astype(np.float32), np.sin(angles).astype(np.float32)
    cosine = np.concatenate([cosine] * 4, axis=1)
    sine = np.concatenate([-sine, sine, -sine, sine], axis=1)
    order = lambda v: v.reshape(4, 4, 2, 32, 128).transpose(0, 2, 1, 3, 4).reshape(8, 128, 128)
    return order(cosine), order(sine)


def pack_kernel(where, w_query, w_key, w_value, w_out, router, gain1, gain2, q_gain, k_gain, out):
    out[:, 0:512] = w_query[...]
    out[:, 512:768] = w_key[...]
    out[:, 768:1024] = w_value[...]
    out[:, 1024:1536] = w_out[...]
    diagonal = lax.broadcasted_iota(jnp.int32, (64, 64), 0) == lax.broadcasted_iota(
        jnp.int32, (64, 64), 1
    )
    column = lambda v: jnp.sum(
        jnp.where(diagonal, v[...].astype(F32), 0.0), axis=1, keepdims=True
    )
    row = lax.broadcasted_iota(jnp.int32, (64, 128), 0)
    lane = lax.broadcasted_iota(jnp.int32, (64, 128), 1)
    small = jnp.where(lane == 32, column(gain1), 0.0) + jnp.where(lane == 33, column(gain2), 0.0)
    for i in range(4):
        here = lane == HD + 4 * where[0] + i
        for r, v in enumerate((q_gain, k_gain)):
            small = small + jnp.where(here & (row == r), v[0:1, i : i + 1].astype(F32), 0.0)
    out[:, 1536:1664] = small.astype(BF)
    out[:, 1536:1568] = router[...]


def pack(where, *arrays):
    whole = lambda v: pl.BlockSpec(v.shape, lambda i, r: (0, 0))
    return pl.pallas_call(
        pack_kernel,
        grid_spec=pltpu.PrefetchScalarGridSpec(
            num_scalar_prefetch=1,
            grid=(1,),
            in_specs=[whole(v) for v in arrays],
            out_specs=pl.BlockSpec((64, 1664), lambda i, r: (0, 0)),
        ),
        out_shape=jax.ShapeDtypeStruct((64, 1664), BF),
        compiler_params=params(1),
        cost_estimate=cost(10**6, 10**6),
        name="pack",
    )(where, *arrays)


def stack_pairs(blocks, *others):
    rows, width = blocks[0].shape

    def kernel(a, b, c, d, low, high):
        low[0], low[1] = a[...], b[...]
        high[0], high[1] = c[...], d[...]

    return pl.pallas_call(
        past(kernel, 4, len(others)),
        in_specs=[pl.BlockSpec(memory_space=pltpu.VMEM)] * 4 + [HBM] * len(others),
        out_shape=[jax.ShapeDtypeStruct((2, rows, width), BF)] * 2,
        compiler_params=pltpu.CompilerParams(vmem_limit_bytes=VMEM),
        cost_estimate=cost(10**6, 10**6),
        name="stack_pairs",
    )(*blocks, *others)


def add_blocks(arrays, handed=(), *others):
    blocks, n, k = arrays[0].shape[0], len(arrays), len(handed)

    def kernel(*refs):
        for i, out in enumerate(refs[n + k + len(others) :][:blocks]):
            total = refs[0][i].astype(F32)
            for ref in refs[1:n]:
                total = total + ref[i].astype(F32)
            out[...] = total.astype(BF)

    vmem = pl.BlockSpec(memory_space=pltpu.VMEM)
    out = pl.pallas_call(
        kernel,
        in_specs=[vmem] * n + [HBM] * (k + len(others)),
        out_specs=[vmem] * blocks + [HBM] * k,
        out_shape=[jax.ShapeDtypeStruct(arrays[0].shape[1:], BF)] * blocks
        + [jax.ShapeDtypeStruct(v.shape, v.dtype) for v in handed],
        input_output_aliases={n + i: blocks + i for i in range(k)},
        compiler_params=pltpu.CompilerParams(vmem_limit_bytes=VMEM),
        cost_estimate=cost(10**9, 10**7),
        name="add_blocks",
    )(*arrays, *handed, *others)
    return out[:blocks], *out[blocks:]


def pack_cotangent(where, cotangent, table, *others):
    def kernel(where, rows, table, out):
        out[0:HALF, :] = rows[...].reshape(HALF, D)
        out[HALF:PAD, :] = jnp.concatenate([table[...], jnp.zeros((8, D), BF)], axis=0)

    return pl.pallas_call(
        past(kernel, 3, len(others)),
        grid_spec=pltpu.PrefetchScalarGridSpec(
            num_scalar_prefetch=1,
            grid=(1,),
            in_specs=[
                pl.BlockSpec((2, 4, 1, 32, D), lambda i, r: (0, 0, r[0], 0, 0)),
                pl.BlockSpec((8, D), lambda i, r: (0, 0)),
            ]
            + [HBM] * len(others),
            out_specs=pl.BlockSpec((PAD, D), lambda i, r: (0, 0)),
        ),
        out_shape=jax.ShapeDtypeStruct((PAD, D), BF),
        compiler_params=params(1),
        cost_estimate=cost(10**6, 10**6),
        name="pack_cotangent",
    )(where, cotangent.reshape(2, 4, 2, 32, D), table, *others)


def project_kernel(
    order, near, x0, x1, x2, x3, x4, x5, x6, x7, w0, w1, w2, w3, cos_all, sin_all,
    w, small, heads, cosine, sine, normed, k_proj, k_b, v_b, q_proj, q_b,
):
    @pl.when(pl.program_id(0) == 0)
    def _():
        for i, shards in enumerate((w0, w1, w2, w3)):
            for j in range(4):
                to = pl.ds(pl.multiple_of(order[4 * i + j] * 64, 64), 64)
                w[to, :] = shards[j]
        for i in range(8):
            cosine[i * 128 : i * 128 + 128, :] = cos_all[near[i]]
            sine[i * 128 : i * 128 + 128, :] = sin_all[near[i]]
        last = w[:, 1536:1664].astype(F32)
        small[...] = last.T
        summed = last[0:64]
        for i in range(1, N_FSDP):
            summed = summed + last[i * 64 : i * 64 + 64]
        lane = lax.broadcasted_iota(jnp.int32, (8, 128), 1)
        gains = jnp.where(lane >= HD, summed[0:8], 0.0)
        heads[...] = gains + pltpu.roll(gains, HD, 1)

    gain = small[32:33, :]
    for i, x in enumerate((x0, x1, x2, x3, x4, x5, x6, x7)):
        values = x[0].astype(F32)
        factor = lax.rsqrt(jnp.mean(values * values, axis=1, keepdims=True) + EPS)
        normed[0, i * 128 : i * 128 + 128, :] = (values * factor * gain).astype(BF)
    both = dot(normed[0], w[:, 512:1024])
    keys = both[:, 0:256]
    k_proj[0] = keys
    v_b[0] = both[:, 256:512].astype(BF)
    cos, sin = twice(cosine[...]), twice(sine[...])
    scaled = keys * lax.rsqrt(head_mean(keys * keys) + EPS) * twice(heads[1:2, :])
    k_b[0] = (scaled * cos + swap_halves(scaled) * sin).astype(BF)
    queries = dot(normed[0, 0:256, :], w[:, 0:512])
    q_proj[0] = queries
    for block in range(2):
        at = slice(block * 256, block * 256 + 256)
        head = queries[:, at]
        scaled = head * lax.rsqrt(head_mean(head * head) + EPS) * twice(heads[0:1, :])
        turned = scaled * cos[0:256] + swap_halves(scaled) * sin[0:256]
        q_b[0, :, at] = (turned.astype(BF).astype(F32) * 0.125).astype(BF)


def project(order, near, tokens, shards, cosine, sine, *others):
    row = lambda s, r, n: (0, 0)
    of = lambda s, r, n: (s, 0, 0)
    block = lambda i: pl.BlockSpec((1, 128, D), lambda s, r, n: (n[i], s, 0))
    fixed = ((D, 1664, BF), (128, D, F32), (8, 128, F32), (SEQ, 128, F32), (SEQ, 128, F32))
    shapes = ((SEQ, D, BF), (SEQ, 256, F32), (SEQ, 256, BF), (SEQ, 256, BF), (256, 512, F32), (256, 512, BF))
    return pl.pallas_call(
        past(project_kernel, 16, len(others)),
        grid_spec=pltpu.PrefetchScalarGridSpec(
            num_scalar_prefetch=2,
            grid=(2,),
            in_specs=[block(i) for i in range(8)]
            + [pl.BlockSpec((4, 64, 1664), lambda s, r, n: (0, 0, 0))] * 4
            + [pl.BlockSpec((8, 128, 128), lambda s, r, n: (0, 0, 0))] * 2
            + [HBM] * len(others),
            out_specs=[pl.BlockSpec((r, n), row) for r, n, _ in fixed]
            + [pl.BlockSpec((1, r, n), of) for r, n, _ in shapes],
        ),
        out_shape=[jax.ShapeDtypeStruct((r, n), dt) for r, n, dt in fixed]
        + [jax.ShapeDtypeStruct((2, r, n), dt) for r, n, dt in shapes],
        compiler_params=params(1),
        cost_estimate=cost(10 * 10**9, 20 * 10**6),
        name="project",
    )(order, near, *([tokens] * 8), *shards, cosine, sine, *others)


def as_column(row):
    return jnp.broadcast_to(row, (8, row.shape[1])).T[:, 0:1]


def place_head(v, target, source):
    moved = v if target == source else pltpu.roll(v, HD, 1)
    lane = lax.broadcasted_iota(jnp.int32, v.shape, 1) // HD
    return jnp.where(lane == target, moved, jnp.zeros_like(moved))


def stack_heads(v):
    parts = []
    for block in range(2):
        for j in range(2):
            parts.append(place_head(v[:, block * 128 : block * 128 + 128], block, j))
    return jnp.concatenate(parts, axis=0)


def unstack_heads(v):
    blocks = []
    for block in range(2):
        pair = [v[(2 * block + j) * 256 : (2 * block + j + 1) * 256] for j in range(2)]
        blocks.append(place_head(pair[0], 0, block) + place_head(pair[1], 1, block))
    return jnp.concatenate(blocks, axis=1)


def attend_kernel(q, k, v, seg, w_out, attended, mine, other):
    row = seg[0]
    mask = jnp.where(as_column(row[:, 0:HALF]) == row, 0.0, NEGATIVE)
    queries = stack_heads(q[0].astype(F32)).astype(BF)
    scores = dot_nt(queries, k[0])
    weights = jnp.concatenate(
        [jnp.exp(scores[i * 256 : i * 256 + 256] + mask).astype(BF) for i in range(4)], axis=0
    )
    summed = dot(weights, jnp.concatenate([v[0], jnp.ones((SEQ, 128), BF)], axis=1))
    mixed = unstack_heads(summed[:, :128] / summed[:, 128:]).astype(BF)
    attended[0] = mixed
    part = dot_nt(mixed, w_out[...])

    @pl.when(pl.program_id(1) == 0)
    def _():
        mine[...] = part[0:128]
        other[...] = part[128:256]

    @pl.when(pl.program_id(1) != 0)
    def _():
        mine[...] += part[0:128]
        other[...] += part[128:256]


def attend(q_b, k_b, v_b, seg, w_out, *others):
    half = pl.BlockSpec((128, D), lambda s, p: (s, 0))
    return pl.pallas_call(
        past(attend_kernel, 5, len(others)),
        grid=(2, 2),
        in_specs=[
            pl.BlockSpec((1, HALF, 256), lambda s, p: (s, 0, p)),
            pl.BlockSpec((1, SEQ, 128), lambda s, p: (s, 0, p)),
            pl.BlockSpec((1, SEQ, 128), lambda s, p: (s, 0, p)),
            pl.BlockSpec((1, 1, SEQ), lambda s, p: (s, 0, 0)),
            pl.BlockSpec((D, 256), lambda s, p: (0, 4 + p)),
        ]
        + [HBM] * len(others),
        out_specs=[pl.BlockSpec((1, HALF, 256), lambda s, p: (s, 0, p)), half, half],
        out_shape=[
            jax.ShapeDtypeStruct((2, HALF, 512), BF),
            jax.ShapeDtypeStruct((HALF, D), F32),
            jax.ShapeDtypeStruct((HALF, D), F32),
        ],
        compiler_params=params(2),
        cost_estimate=cost(10 * 10**9, 8 * 10**6),
        name="attend",
    )(q_b, k_b, v_b, seg, w_out, *others)


def experts_to_rows(table):
    return jnp.concatenate([table[8 * k : 8 * k + 8] for k in range(4)], axis=1)


def rows_to_experts(rows):
    return jnp.concatenate([rows[:, 256 * k : 256 * k + 256] for k in range(4)], axis=0)


def route_kernel(tokens, mine, other, small, match, kept, hidden, payload, probs, totals):
    values = tokens[...].astype(F32) + mine[...] + other[...]
    hidden[...] = values
    factor = lax.rsqrt(jnp.mean(values * values, axis=1, keepdims=True) + EPS)
    rows = (values * factor * small[33:34, :]).astype(BF)
    payload[0:HALF, :] = rows
    logits = dot_nt(small[0:32, :].astype(BF), rows)
    raised = jnp.exp(logits - jnp.max(logits, axis=0, keepdims=True))
    prob = raised / jnp.sum(raised, axis=0, keepdims=True)
    probs[...] = prob
    chosen = prob * match[...]
    total = jnp.sum(chosen, axis=0, keepdims=True)
    totals[...] = total
    high, low = split(experts_to_rows(chosen / total * kept[...]))
    payload[HALF:PAD, :] = jnp.concatenate([high, low], axis=0)


def route(*args):
    return pl.pallas_call(
        past(route_kernel, 6, len(args) - 6),
        in_specs=[pl.BlockSpec(memory_space=pltpu.VMEM)] * 6 + [HBM] * (len(args) - 6),
        out_shape=[
            jax.ShapeDtypeStruct((HALF, D), F32),
            jax.ShapeDtypeStruct((PAD, D), BF),
            jax.ShapeDtypeStruct((EXPERTS, HALF), F32),
            jax.ShapeDtypeStruct((1, HALF), F32),
        ],
        compiler_params=pltpu.CompilerParams(vmem_limit_bytes=VMEM),
        cost_estimate=cost(10**8, 5 * 10**6),
        name="route",
    )(*args)


def own_row(table, lane_block, row):
    picked = jnp.zeros((8, 256), F32)
    for k in range(4):
        picked = picked + jnp.where(lane_block == k, table[:, 256 * k : 256 * k + 256], 0.0)
    number = lax.broadcasted_iota(jnp.int32, (8, 256), 0)
    return jnp.sum(jnp.where(number == row, picked, 0.0), axis=0, keepdims=True)


def expert_math(x, g, gate, w):
    pre = dot(x, w[:, 0:1024])
    grad_all = dot(g, w[:, 1024:1536])
    acts, grads, gate_dot = [], [], 0.0
    for part in range(2):
        gate_pre = pre[:, part * 512 : part * 512 + 256]
        up_pre = pre[:, part * 512 + 256 : part * 512 + 512]
        grad = grad_all[:, part * 256 : part * 256 + 256]
        sig = jax.nn.sigmoid(gate_pre)
        swish = gate_pre * sig
        act = (swish * up_pre).astype(BF).astype(F32)
        gate_dot = gate_dot + jnp.sum(act * grad, axis=1, keepdims=True)
        acts.append((act * gate).astype(BF))
        grad = grad * gate
        grads.append((grad * up_pre * sig * (1.0 + gate_pre * (1.0 - sig))).astype(BF))
        grads.append((grad * swish).astype(BF))
    act = jnp.concatenate(acts, axis=1)
    grad = jnp.concatenate(grads, axis=1)
    y = dot_nt(act, w[:, 1024:1536]).astype(BF)
    back = dot_nt(grad, w[:, 0:1024]).astype(BF)
    return y, back, act, grad, gate_dot


def pick_rows(places, first, rows):
    number = lax.broadcasted_iota(jnp.int32, (rows, 256), 0) + first
    return number == places.astype(jnp.int32)


def expert_kernel(order, where_at, x_low, x_high, c_low, c_high, w_gate, w_up, w_down, *refs):
    refs = refs[len(refs) - 25 :]
    out_y, out_x, kept_x, kept_g, kept_h, more_x, more_g, more_h, tiles = refs[:9]
    x_all, c_all, wv, xs, gs, hs, picks, sums, ys, bs, total, places, gate_rows, dots = refs[9:23]
    in_sem, out_sem = refs[23:]
    slot = where_at[2]
    lane_block, row_at = where_at[0], where_at[1]
    copy = pltpu.make_async_copy
    loads = [
        copy(x_low, x_all.at[0:2], in_sem.at[0]),
        copy(c_low, c_all.at[0:2], in_sem.at[1]),
        copy(x_high, x_all.at[2:4], in_sem.at[2]),
        copy(c_high, c_all.at[2:4], in_sem.at[3]),
    ]

    def load_w(e):
        copies = []
        for part in range(2):
            for w, at in ((w_gate, 512 * part), (w_up, 512 * part + 256), (w_down, 1024 + 256 * part)):
                sem = in_sem.at[4 + 2 * len(copies) + e]
                copies.append(copy(w.at[part, e], wv.at[e, :, at : at + 256], sem))
        return copies

    for load in loads + load_w(0) + load_w(1):
        load.start()
    for load in loads:
        load.wait()

    def read(h, carry):
        table = c_all[h, HALF : HALF + 8, :].astype(F32)
        gate_table = x_all[h, HALF:PAD, :].astype(F32)
        gate_table = gate_table[0:8] + gate_table[8:16]
        for e in range(2):
            places[pl.ds(4 * e + h, 1), :] = own_row(table, lane_block, row_at + e)
            gate_rows[pl.ds(4 * e + h, 1), :] = own_row(gate_table, lane_block, row_at + e)
        return carry

    lax.fori_loop(0, 4, read, 0)
    most = jnp.max(places[...]).astype(jnp.int32)
    count = jnp.maximum(most, 0) // MAIN + 1
    tiles[...] = jnp.zeros((8, 128), F32) + count.astype(F32)

    rows = pl.ds(pl.multiple_of(slot * (4 * MAIN), 4 * MAIN), 4 * MAIN)

    def tile(i, carry):
        first = i * MAIN
        more = pl.ds(pl.multiple_of(jnp.maximum(i - 1, 0) * (4 * MAIN), 4 * MAIN), 4 * MAIN)
        sends = lambda e: (
            (xs, kept_x, more_x, e),
            (gs, kept_g, more_g, 2 + e),
            (hs, kept_h, more_h, 4 + e),
        )

        def start(v, kept, other, e, n):
            @pl.when(i == 0)
            def _():
                copy(v.at[e], kept.at[e, rows], out_sem.at[n]).start()

            @pl.when(i > 0)
            def _():
                copy(v.at[e], other.at[e, more], out_sem.at[n]).start()

        def gather(h, carry):
            pick = [
                jnp.where(pick_rows(places[pl.ds(4 * e + h, 1), :], first, MAIN), 1.0, 0.0)
                for e in range(2)
            ]
            pick = jnp.concatenate(pick, axis=0).astype(BF)
            picks[h] = pick
            x = dot(pick, x_all[h, 0:HALF, :]).astype(BF)
            g = dot(pick, c_all[h, 0:HALF, :]).astype(BF)
            to = pl.ds(pl.multiple_of(h * MAIN, MAIN), MAIN)
            for e in range(2):
                xs[e, to, :] = x[e * MAIN : e * MAIN + MAIN]
                gs[e, to, :] = g[e * MAIN : e * MAIN + MAIN]
            return carry

        lax.fori_loop(0, 4, gather, 0)
        for e in range(2):
            start(xs, kept_x, more_x, e, e)
            start(gs, kept_g, more_g, e, 2 + e)

        def math(e, carry):
            here = [pick_rows(places[pl.ds(4 * e + h, 1), :], first, MAIN) for h in range(4)]
            gate = [
                jnp.sum(
                    jnp.where(here[h], gate_rows[pl.ds(4 * e + h, 1), :], 0.0),
                    axis=1,
                    keepdims=True,
                )
                for h in range(4)
            ]

            @pl.when(i == 0)
            def _():
                for load in load_w(e):
                    load.wait()

            y, back, act, grad, gate_dot = expert_math(
                xs[e], gs[e], jnp.concatenate(gate, axis=0), wv.at[e]
            )
            hs[e, :, 0:512] = act
            hs[e, :, 512:1536] = grad
            start(hs, kept_h, more_h, e, 4 + e)
            to = pl.ds(pl.multiple_of(e * MAIN, MAIN), MAIN)
            for h in range(4):
                at = slice(h * MAIN, h * MAIN + MAIN)
                sums[h, to, 0:D] = y[at]
                sums[h, to, D : 2 * D] = back[at]
                spread = jnp.sum(jnp.where(here[h], gate_dot[at], 0.0), axis=0, keepdims=True)
                row = pl.ds(4 * e + h, 1)
                dots[row, :] = jnp.where(i == 0, 0.0, dots[row, :]) + spread
            return carry

        lax.fori_loop(0, 2, math, 0)
        last = i == count - 1

        def scatter(h, carry):
            out = dot_tn(picks[h], sums[h])
            at = pl.ds(pl.multiple_of(h * HALF, HALF), HALF)

            @pl.when(i > 0)
            def _():
                total[at, :] += out

            @pl.when((i == 0) & jnp.logical_not(last))
            def _():
                total[at, :] = out

            @pl.when(last)
            def _():
                @pl.when(i == 0)
                def _():
                    ys[h] = out[:, 0:D].astype(BF)
                    bs[h, 0:HALF, :] = out[:, D : 2 * D].astype(BF)

                @pl.when(i > 0)
                def _():
                    ys[h] = total[at, 0:D].astype(BF)
                    bs[h, 0:HALF, :] = total[at, D : 2 * D].astype(BF)

                row = lax.broadcasted_iota(jnp.int32, (8, 256), 0)
                table = jnp.where(row == row_at, dots[pl.ds(h, 1), :], 0.0)
                table = table + jnp.where(row == row_at + 1, dots[pl.ds(4 + h, 1), :], 0.0)
                table = [jnp.where(lane_block == k, table, 0.0) for k in range(4)]
                high, low = split(jnp.concatenate(table, axis=1))
                bs[h, HALF:PAD, :] = jnp.concatenate([high, low], axis=0)
                copy(bs.at[h], out_x.at[h], out_sem.at[6 + h]).start()
                copy(ys.at[h], out_y.at[order[h]], out_sem.at[10 + h]).start()

            return carry

        lax.fori_loop(0, 4, scatter, 0)
        for e in range(2):
            for v, kept, _, n in sends(e):
                copy(v.at[e], kept.at[e, rows], out_sem.at[n]).wait()
        return carry

    lax.fori_loop(0, count, tile, 0)
    for h in range(4):
        copy(bs.at[h], out_x.at[h], out_sem.at[6 + h]).wait()
        copy(ys.at[h], out_y.at[order[h]], out_sem.at[10 + h]).wait()


def expert_chunk(order, where_at, x, cotangents, weights, kept):
    rows = 4 * MAIN
    widths = (D, D, 1536)
    shape = lambda *v: jax.ShapeDtypeStruct(v, BF)
    vmem = lambda *v: pltpu.VMEM(v, BF)
    aliases = {9: 0, 10: 2, 11: 3, 12: 4} if kept else {}
    return pl.pallas_call(
        expert_kernel,
        grid_spec=pltpu.PrefetchScalarGridSpec(
            num_scalar_prefetch=2,
            grid=(1,),
            in_specs=[HBM] * (7 + len(kept)),
            out_specs=[HBM] * 8 + [pl.BlockSpec((8, 128), lambda i, r, w: (0, 0))],
            scratch_shapes=[
                vmem(4, PAD, D),
                vmem(4, PAD, D),
                vmem(2, D, 1536),
                vmem(2, rows, D),
                vmem(2, rows, D),
                vmem(2, rows, 1536),
                vmem(4, 2 * MAIN, 256),
                vmem(4, 2 * MAIN, 2 * D),
                vmem(4, HALF, D),
                vmem(4, PAD, D),
                pltpu.VMEM((1024, 2 * D), F32),
                pltpu.VMEM((8, 256), F32),
                pltpu.VMEM((8, 256), F32),
                pltpu.VMEM((8, 256), F32),
                pltpu.SemaphoreType.DMA((16,)),
                pltpu.SemaphoreType.DMA((14,)),
            ],
        ),
        out_shape=[shape(N_FSDP, HALF, D), shape(4, PAD, D)]
        + [shape(2, 4 * rows, n) for n in widths]
        + [shape(2, (TILES - 1) * rows, n) for n in widths]
        + [jax.ShapeDtypeStruct((8, 128), F32)],
        input_output_aliases=aliases,
        compiler_params=params(1),
        cost_estimate=cost(14 * 10**9, 30 * 10**6),
        name="experts",
    )(order, where_at, *x, *cotangents, *weights, *kept)


def expert_weight_kernel(place, x, g, act, grad, *refs):
    more, counts, (down, gate_up), (mx, mg, mh) = refs[:12], refs[12:16], refs[-5:-3], refs[-3:]
    out = refs[-6]
    expert, part = pl.program_id(0), pl.program_id(1)
    down[...] = dot_tn(g[0], act[0])
    gate_up[...] = dot_tn(x[0], grad[0])
    for chunk in range(4):
        count = jnp.max(counts[chunk][...]).astype(jnp.int32) - 1

        @pl.when(count > 0)
        def _(chunk=chunk, count=count):
            def piece(i, carry):
                rows = pl.ds(pl.multiple_of(i * 4 * MAIN, 4 * MAIN), 4 * MAIN)
                for ref, to in zip(more[3 * chunk : 3 * chunk + 3], (mx, mg, mh)):
                    pltpu.sync_copy(ref.at[expert, rows], to)
                for p in range(2):

                    @pl.when(part == p)
                    def _(p=p):
                        at = p * 256
                        down[...] += dot_tn(mg[...], mh[:, at : at + 256])
                        at = 512 + p * 512
                        gate_up[...] += dot_tn(mx[...], mh[:, at : at + 512])

                return carry

            lax.fori_loop(0, count, piece, 0)

    for c in range(4):
        at = slice(c * 256, c * 256 + 256)
        out[c, 0, 0, :, 0:512] = gate_up[at, :].astype(BF)
        out[c, 0, 0, :, 512:768] = down[at, :].astype(BF)


def expert_weights(place, kept, more, counts, *others):
    rows = 16 * MAIN
    by_expert = lambda e, p, r: (e, 0, 0)
    return pl.pallas_call(
        expert_weight_kernel,
        grid_spec=pltpu.PrefetchScalarGridSpec(
            num_scalar_prefetch=1,
            grid=(2, 2),
            in_specs=[
                pl.BlockSpec((1, rows, D), by_expert),
                pl.BlockSpec((1, rows, D), by_expert),
                pl.BlockSpec((1, rows, 256), lambda e, p, r: (e, 0, p)),
                pl.BlockSpec((1, rows, 512), lambda e, p, r: (e, 0, 1 + p)),
            ]
            + [HBM] * 12
            + [pl.BlockSpec((8, 128), lambda e, p, r: (0, 0))] * 4
            + [HBM] * len(others),
            out_specs=pl.BlockSpec(
                (4, 1, 1, 256, 768),
                lambda e, p, r: (0, p, e, 0, 0),
            ),
            scratch_shapes=[
                pltpu.VMEM((D, 256), F32),
                pltpu.VMEM((D, 512), F32),
                pltpu.VMEM((4 * MAIN, D), BF),
                pltpu.VMEM((4 * MAIN, D), BF),
                pltpu.VMEM((4 * MAIN, 1536), BF),
            ],
        ),
        out_shape=jax.ShapeDtypeStruct((4, 2, 2, 256, 768), BF),
        compiler_params=params(2),
        cost_estimate=cost(20 * 10**9, 30 * 10**6),
        name="expert_weights",
    )(place, kept[0], kept[1], kept[2], kept[2], *more, *counts, *others)


def route_back_kernel(
    own, first, second, third, cotangent, hidden, small, normed, probs, totals, match,
    grad_hidden, grad_branch, grad_router, grad_gain,
):
    summed = own[...].astype(F32) + first[...].astype(F32)
    summed = summed + (second[...].astype(F32) + third[...].astype(F32))
    tables = summed[HALF:PAD, :]
    grad_gates = rows_to_experts(tables[0:8] + tables[8:16])
    prob, total = probs[...], totals[...]
    chosen = prob * match[...]
    shared = jnp.sum(grad_gates * chosen, axis=0, keepdims=True) / (total * total)
    grad_prob = (grad_gates / total - shared) * match[...]
    grad_logits = prob * (grad_prob - jnp.sum(prob * grad_prob, axis=0, keepdims=True))
    high, low = split(grad_logits)
    grad_router[...] = dot(high, normed[0:HALF, :]) + dot(low, normed[0:HALF, :])
    router = small[0:32, :].astype(BF)
    grad_normed = summed[0:HALF, :] + dot_tn(high, router) + dot_tn(low, router)
    values = hidden[...]
    factor = lax.rsqrt(jnp.mean(values * values, axis=1, keepdims=True) + EPS)
    grad_gain[...] = jnp.sum(grad_normed * values * factor, axis=0, keepdims=True)
    weighted = grad_normed * small[33:34, :]
    mean = jnp.mean(weighted * values, axis=1, keepdims=True)
    grad = cotangent[0:HALF, :].astype(F32) + factor * weighted - values * (factor * factor * factor * mean)
    grad_hidden[...] = grad
    grad_branch[...] = grad.astype(BF)


def route_back(handed, *args):
    n, others, shapes = len(handed), len(args) - 11, [jax.ShapeDtypeStruct(v.shape, v.dtype) for v in handed]
    vmem = pl.BlockSpec(memory_space=pltpu.VMEM)
    kernel = past(route_back_kernel, 11, others + n)
    return pl.pallas_call(
        lambda *refs: kernel(*refs[n:]),
        in_specs=[HBM] * n + [vmem] * 11 + [HBM] * others,
        out_specs=[HBM] * n + [vmem] * 4,
        input_output_aliases={i: i for i in range(n)},
        out_shape=shapes
        + [
            jax.ShapeDtypeStruct((HALF, D), F32),
            jax.ShapeDtypeStruct((HALF, D), BF),
            jax.ShapeDtypeStruct((EXPERTS, D), F32),
            jax.ShapeDtypeStruct((1, D), F32),
        ],
        compiler_params=pltpu.CompilerParams(vmem_limit_bytes=VMEM),
        cost_estimate=cost(4 * 10**9, 6 * 10**6),
        name="route_back",
    )(*handed, *args)


def norm_back_heads(grad, proj, gain, cosine, sine):
    turned = grad * cosine - swap_halves(grad) * sine
    factor = lax.rsqrt(head_mean(proj * proj) + EPS)
    weighted = turned * gain
    mean = head_mean(weighted * proj)
    back = factor * weighted - proj * (factor * factor * factor * mean)
    return back, jnp.sum(turned * proj * factor, axis=0, keepdims=True)


def attend_back_kernel(
    q, q_proj, k, k_proj, v, seg, branch_m, branch_o, w_out, attended,
    cosine, sine, heads, grad_q, grad_k, grad_v, gains,
):
    row = seg[0]
    mask = jnp.where(as_column(row) == row[:, 0:HALF], 0.0, NEGATIVE)
    keys, values = k[0], v[0]
    grad_branch = jnp.concatenate([branch_m[...], branch_o[...]], axis=0)
    grad_mixed = dot(grad_branch, w_out[...]).astype(BF).astype(F32)
    queries = stack_heads(q[0].astype(F32)).astype(BF)
    grads = stack_heads(grad_mixed).astype(BF)
    high, low = split(stack_heads(attended[0].astype(F32) * grad_mixed))
    ones = jnp.ones((8, 256), BF)
    row_dot = dot_nt(ones, jnp.concatenate([high, low], axis=1))[0:1]
    scores = dot_nt(keys, queries)
    grad_probs = dot_nt(values, grads)
    probs_b, grad_scores = [], []
    for i in range(4):
        at = slice(i * 256, i * 256 + 256)
        raised = jnp.exp(scores[:, at] + mask)
        probs = raised * (1.0 / jnp.sum(raised, axis=0, keepdims=True))
        probs_b.append(probs.astype(BF))
        grad_scores.append((probs * (grad_probs[:, at] - row_dot[:, at])).astype(BF))
    probs_b = jnp.concatenate(probs_b, axis=1)
    grad_scores = jnp.concatenate(grad_scores, axis=1)
    grad_v[0] = dot(probs_b, grads).astype(BF)
    sum_k = dot(grad_scores, queries)
    sum_q = unstack_heads(dot_tn(grad_scores, keys) * 0.125)
    cos, sin = cosine[...], sine[...]
    back, gain_q = norm_back_heads(
        sum_q, q_proj[0], twice(heads[0:1, :]), twice(cos[0:256]), twice(sin[0:256])
    )
    grad_q[0] = back.astype(BF)
    wide = lambda value: jnp.concatenate([value[0:512], value[512:1024]], axis=1)
    back, gain_k = norm_back_heads(
        wide(sum_k), wide(k_proj[0]), twice(heads[1:2, :]), wide(cos), wide(sin)
    )
    grad_k[0, 0:512, :] = back[:, 0:128].astype(BF)
    grad_k[0, 512:1024, :] = back[:, 128:256].astype(BF)
    part = jnp.concatenate([gain_q, gain_k, jnp.zeros((6, 256), F32)], axis=0)

    @pl.when((pl.program_id(0) == 0) & (pl.program_id(1) == 0))
    def _():
        gains[...] = part

    @pl.when((pl.program_id(0) != 0) | (pl.program_id(1) != 0))
    def _():
        gains[...] += part


def attend_back(
    q_b, q_proj, k_b, k_proj, v_b, seg, branch_m, branch_o, w_out, attended,
    cosine, sine, heads,
):
    queries = pl.BlockSpec((1, HALF, 256), lambda s, p: (s, 0, p))
    keys = pl.BlockSpec((1, SEQ, 128), lambda s, p: (s, 0, p))
    table = pl.BlockSpec((SEQ, 128), lambda s, p: (0, 0))
    gain = pl.BlockSpec((8, 128), lambda s, p: (0, 0))
    half = pl.BlockSpec((128, D), lambda s, p: (s, 0))
    return pl.pallas_call(
        attend_back_kernel,
        grid=(2, 2),
        in_specs=[
            queries, queries, keys, keys, keys,
            pl.BlockSpec((1, 1, SEQ), lambda s, p: (s, 0, 0)),
            half, half,
            pl.BlockSpec((D, 256), lambda s, p: (0, 4 + p)),
            queries, table, table, gain,
        ],
        out_specs=[queries, keys, keys, pl.BlockSpec((8, 256), lambda s, p: (0, 0))],
        out_shape=[
            jax.ShapeDtypeStruct((2, HALF, 512), BF),
            jax.ShapeDtypeStruct((2, SEQ, 256), BF),
            jax.ShapeDtypeStruct((2, SEQ, 256), BF),
            jax.ShapeDtypeStruct((8, 256), F32),
        ],
        compiler_params=params(2),
        cost_estimate=cost(18 * 10**9, 16 * 10**6),
        name="attend_back",
    )(
        q_b, q_proj, k_b, k_proj, v_b, seg, branch_m, branch_o, w_out, attended,
        cosine, sine, heads,
    )


def weight_grads_kernel(
    place, normed, gq, gk, gv, branch_m, branch_o, mixed, router, gain, head_gains,
    out_0, out_1, out_2, out_3, out, sem,
):
    step = pl.program_id(0)
    rows = jnp.concatenate([normed[0], normed[1]], axis=0)
    own = jnp.concatenate([normed[0, 0:256, :], normed[1, 0:256, :]], axis=0)
    keys = jnp.concatenate(
        [
            jnp.concatenate([gk[0], gk[1]], axis=0),
            jnp.concatenate([gv[0], gv[1]], axis=0),
        ],
        axis=1,
    )
    queries = jnp.concatenate([gq[0], gq[1]], axis=0)
    branch = jnp.concatenate(
        [branch_m[0:128], branch_o[0:128], branch_m[128:256], branch_o[128:256]], axis=0
    )
    heads = jnp.concatenate([mixed[0], mixed[1]], axis=0)
    at = lax.broadcasted_iota(jnp.int32, (256, 256), 1)
    share = 4 * (at // HD + 4 * step) + at % HD
    spread = (lax.broadcasted_iota(jnp.int32, (256, 256), 0) % HD == share) & (at % HD < 4)
    spread = jnp.where(spread, 1.0, 0.0).astype(BF)
    high, low = split(head_gains[...])
    spread = dot(high, spread) + dot(low, spread)
    row = lax.broadcasted_iota(jnp.int32, (8, 256), 0)
    last = jnp.where(row == 0, gain[...], 0.0)
    last = last + jnp.where(row == 1, spread[0:1], 0.0) + jnp.where(row == 2, spread[1:2], 0.0)
    small = jnp.concatenate([router[...], last, jnp.zeros((88, 256), F32)], axis=0)
    parts = (
        (0, 512, dot_tn(own, queries).astype(BF)),
        (512, 1024, dot_tn(rows, keys).astype(BF)),
        (1024, 1536, dot_tn(branch, heads).astype(BF)),
        (1536, 1664, small.T.astype(BF)),
    )
    for i in range(4):
        to = place[4 * step + i]
        for low, high, value in parts:
            out[to, :, low:high] = value[i * 64 : i * 64 + 64]

    @pl.when(step == 3)
    def _():
        sends = [
            pltpu.make_async_copy(out.at[4 * i : 4 * i + 4], to, sem.at[i])
            for i, to in enumerate((out_0, out_1, out_2, out_3))
        ]
        for send in sends:
            send.start()
        for send in sends:
            send.wait()


def weight_grads(place, *args):
    fixed = lambda i, r: (0, 0, 0)
    column = pl.BlockSpec((HALF, 256), lambda i, r: (0, i))
    return pl.pallas_call(
        past(weight_grads_kernel, 11, len(args) - 10),
        grid_spec=pltpu.PrefetchScalarGridSpec(
            num_scalar_prefetch=1,
            grid=(4,),
            in_specs=[
                pl.BlockSpec((2, SEQ, 256), lambda i, r: (0, 0, i)),
                pl.BlockSpec((2, HALF, 512), fixed),
                pl.BlockSpec((2, SEQ, 256), fixed),
                pl.BlockSpec((2, SEQ, 256), fixed),
                column,
                column,
                pl.BlockSpec((2, HALF, 512), fixed),
                pl.BlockSpec((EXPERTS, 256), lambda i, r: (0, i)),
                pl.BlockSpec((1, 256), lambda i, r: (0, i)),
                pl.BlockSpec((8, 256), lambda i, r: (0, 0)),
            ]
            + [HBM] * (len(args) - 10),
            out_specs=[HBM] * 4,
            scratch_shapes=[pltpu.VMEM((N_FSDP, 64, 1664), BF), pltpu.SemaphoreType.DMA((4,))],
        ),
        out_shape=[jax.ShapeDtypeStruct((4, 64, 1664), BF)] * 4,
        compiler_params=params(1),
        cost_estimate=cost(9 * 10**9, 16 * 10**6),
        name="weight_grads",
    )(place, *args)


def input_grads_kernel(gq, gk, gv, w, mine, other):
    part = dot_nt(jnp.concatenate([gk[0], gv[0]], axis=1), w[:, 512:1024])
    own = dot_nt(gq[0], w[:, 0:512])
    for c in range(4):
        for parity, out in enumerate((mine, other)):
            at = slice(c * 256 + parity * 128, c * 256 + parity * 128 + 128)
            value = part[at] + own[at] if c == 0 else part[at]
            out[c] = value.astype(BF)


def input_grads(gq, gk, gv, weights, *others):
    by = lambda s: (s, 0, 0)
    half = pl.BlockSpec((4, 128, D), lambda s: (0, s, 0))
    return pl.pallas_call(
        past(input_grads_kernel, 4, len(others)),
        grid=(2,),
        in_specs=[
            pl.BlockSpec((1, HALF, 512), by),
            pl.BlockSpec((1, SEQ, 256), by),
            pl.BlockSpec((1, SEQ, 256), by),
            pl.BlockSpec((D, 1024), lambda s: (0, 0)),
        ]
        + [HBM] * len(others),
        out_specs=[half, half],
        out_shape=[jax.ShapeDtypeStruct((4, HALF, D), BF)] * 2,
        compiler_params=params(1),
        cost_estimate=cost(6 * 10**9, 12 * 10**6),
        name="input_grads",
    )(gq, gk, gv, weights, *others)


def finish_kernel(own, first, second, third, tokens, grad_hidden, small, out):
    values = tokens[...].astype(F32)
    factor = lax.rsqrt(jnp.mean(values * values, axis=1, keepdims=True) + EPS)
    summed = own[...].astype(F32) + first[...].astype(F32)
    summed = summed + (second[...].astype(F32) + third[...].astype(F32))
    weighted = summed * small[32:33, :]
    mean = jnp.mean(weighted * values, axis=1, keepdims=True)
    out[...] = grad_hidden[...] + factor * weighted - values * (factor * factor * factor * mean)


def finish(*args):
    return pl.pallas_call(
        past(finish_kernel, 7, len(args) - 7),
        in_specs=[pl.BlockSpec(memory_space=pltpu.VMEM)] * 7 + [HBM] * (len(args) - 7),
        out_shape=jax.ShapeDtypeStruct((HALF, D), F32),
        compiler_params=pltpu.CompilerParams(vmem_limit_bytes=VMEM),
        cost_estimate=cost(10**7, 6 * 10**6),
        name="finish",
    )(*args)


def settle_kernel(
    own, first, second, third, w_query, w_key, w_value, gain, g_query, g_key, g_value, g_out, sums
):
    summed = own[...].astype(F32) + first[...].astype(F32)
    summed = summed + (second[...].astype(F32) + third[...].astype(F32))
    g_query[...] = summed[:, 0:512]
    g_key[...] = summed[:, 512:768]
    g_value[...] = summed[:, 768:1024]
    g_out[...] = summed[:, 1024:1536]
    part = jnp.sum(w_query[...].astype(F32) * summed[:, 0:512], axis=1, keepdims=True)
    part = part + jnp.sum(w_key[...].astype(F32) * summed[:, 512:768], axis=1, keepdims=True)
    part = part + jnp.sum(w_value[...].astype(F32) * summed[:, 768:1024], axis=1, keepdims=True)
    diagonal = lax.broadcasted_iota(jnp.int32, (64, 64), 0) == lax.broadcasted_iota(
        jnp.int32, (64, 64), 1
    )
    column = jnp.sum(jnp.where(diagonal, gain[...].astype(F32), 0.0), axis=1, keepdims=True)
    lane = lax.broadcasted_iota(jnp.int32, (64, 128), 1)
    sums[...] = jnp.where(lane == 35, part / column, summed[:, 1536:1664])


def settle(*args):
    return pl.pallas_call(
        past(settle_kernel, 8, len(args) - 8),
        in_specs=[pl.BlockSpec(memory_space=pltpu.VMEM)] * 8 + [HBM] * (len(args) - 8),
        out_shape=[jax.ShapeDtypeStruct((64, n), F32) for n in (512, 256, 256, 512, 128)],
        compiler_params=pltpu.CompilerParams(vmem_limit_bytes=VMEM),
        cost_estimate=cost(10**6, 2 * 10**6),
        name="settle",
    )(*args)


def join_kernel(where, mine, far, out):
    @pl.when(pl.program_id(0) == 0)
    def _():
        out[...] = mine[...].reshape(2, 4, 1, 32, D)

    @pl.when(pl.program_id(0) == 1)
    def _():
        out[...] = far[...].reshape(2, 4, 1, 32, D)


def join(where, mine, far, *others):
    whole = pl.BlockSpec((HALF, D), lambda i, r: (0, 0))
    return pl.pallas_call(
        past(join_kernel, 3, len(others)),
        grid_spec=pltpu.PrefetchScalarGridSpec(
            num_scalar_prefetch=1,
            grid=(2,),
            in_specs=[whole, whole] + [HBM] * len(others),
            out_specs=pl.BlockSpec(
                (2, 4, 1, 32, D), lambda i, r: (0, 0, jnp.where(i == 0, r[0], 1 - r[0]), 0, 0)
            ),
        ),
        out_shape=jax.ShapeDtypeStruct((2, 4, 2, 32, D), mine.dtype),
        compiler_params=params(1),
        cost_estimate=cost(10**6, 4 * 10**6),
        name="join",
    )(where, mine, far, *others).reshape(2, 256, D)


def ring_pairs(stage, step):
    pairs = []
    for x in range(4):
        for z in range(4):
            for t in range(2):
                if (stage == 0) == (t == 0):
                    far = ((x + step) % 4) * 4 + z
                else:
                    far = x * 4 + (z + step) % 4
                pairs.append(((x * 4 + z) * 2 + t, far * 2 + t))
    return pairs


def ring(value, stage, step):
    return lax.ppermute(value, ("fsdp", "tensor"), ring_pairs(stage, step))


def shift(value, step):
    return lax.ppermute(value, "context", [(i, (i + step) % 4) for i in range(4)])


def swap_cores(value):
    return lax.ppermute(value, "tensor", [(0, 1), (1, 0)])


def gather_row(block, stage=0):
    return block, ring(block, stage, -1), ring(block, stage, 1), ring(block, stage, 2)


def gather_chunks(low, high):
    behind_low, ahead_high = ring(low, 1, 1), ring(high, 1, -1)
    behind_high, ahead_low = ring(high, 1, 1), ring(low, 1, -1)
    far = ring(behind_low, 1, 1), ring(ahead_high, 1, -1)
    return (low, high), (ahead_low, ahead_high), (behind_low, behind_high), far


def scatter_parts(parts, move):
    own, ahead, behind, far = parts
    return own, move(ahead, 1), move(behind, -1), move(far, 2)


def total_of(parts):
    first, second, third, fourth = (p.astype(F32) for p in parts)
    return (first + second) + (third + fourth)


def along(stage):
    return lambda v, n: ring(v, stage, n)


def local(
    tokens, segments, routes, attention_gain, w_query, w_key, w_value, w_out, query_gain,
    key_gain, feedforward_gain, router, w_gate, w_up, w_down, cotangent,
):
    f, c, t = lax.axis_index("fsdp"), lax.axis_index("context"), lax.axis_index("tensor")
    x_at, z_at = f // 4, f % 4
    steps = jnp.array([0, 1, 3, 2], jnp.int32)
    as_row = lambda *v: jnp.stack([jnp.asarray(i, jnp.int32) for i in v])
    all_x, all_z = (x_at + steps) % 4, (z_at + steps) % 4
    order = jnp.where(
        t == 0, all_x[None, :] * 4 + all_z[:, None], all_x[:, None] * 4 + all_z[None, :]
    ).astype(jnp.int32)
    far_x, far_z = steps[(jnp.arange(4) - x_at) % 4], steps[(jnp.arange(4) - z_at) % 4]
    place = jnp.where(
        t == 0, far_x[:, None] + 4 * far_z[None, :], 4 * far_x[:, None] + far_z[None, :]
    )
    place = place.reshape(-1).astype(jnp.int32)
    near = ((c + steps) % 4)[:, None] * 2 + jnp.stack([t, 1 - t])[None, :]
    near = near.reshape(8)

    shard = pack(
        as_row(f), w_query, w_key, w_value, w_out, router, attention_gain[None, :],
        feedforward_gain[None, :], query_gain[None, :], key_gain[None, :],
    )
    shards = jnp.stack(gather_row(shard))
    shards = gather_row(shards, 1)

    parity = lambda v, p: lax.dynamic_index_in_dim(
        v.reshape(2, 4, 2, 32, D), p, 2, keepdims=False
    ).reshape(HALF, D)
    tokens_m = parity(tokens, t)
    tokens_all = lax.all_gather(tokens_m, ("context", "tensor"), axis=0)
    picked = routes.reshape(ROWS, TOPK).T
    experts = jnp.arange(EXPERTS, dtype=jnp.int32)
    match = jnp.any(picked[:, None, :] == experts[None, :, None], axis=0)
    before = lambda n: (jnp.arange(n)[:, None] < jnp.arange(n)[None, :]).astype(BF)
    kept = match & (dot(match.astype(BF), before(ROWS)) < CAP)
    half = lambda v: lax.dynamic_index_in_dim(
        v.astype(F32).reshape(EXPERTS, 2, 4, 2, 32), t, 3, keepdims=False
    ).reshape(EXPERTS, HALF)
    match_half, kept_half = half(match), half(kept)
    local_place = dot(kept_half.astype(BF), before(HALF))
    table = experts_to_rows(jnp.where(kept_half > 0, local_place, -1.0).astype(BF))
    cot_payload = pack_cotangent(as_row(t), cotangent, table, *shards[1:])
    cot_row = gather_row(cot_payload)

    experts_w = [lax.all_gather(w, "tensor", axis=0) for w in (w_gate, w_up, w_down)]
    seg = segments.reshape(2, 4, 4, 2, 32).transpose(0, 1, 3, 2, 4).reshape(2, 8, 128)
    seg = jnp.take(seg, near, axis=1).reshape(2, 1, SEQ).astype(F32)

    cosine, sine = (jnp.asarray(v) for v in rotary_tables())
    weights, small, heads, cosine, sine, normed1, k_proj, k_b, v_b, q_proj, q_b = project(
        order.reshape(-1), near.astype(jnp.int32), tokens_all, shards, cosine, sine, seg
    )
    cot_chunks = gather_chunks(*stack_pairs(cot_row, small))
    attended, branch_m, branch_o = attend(q_b, k_b, v_b, seg, weights, cot_chunks[0][0])
    hidden1, payload, probs, totals = route(
        tokens_m, branch_m, swap_cores(branch_o), small, match_half, kept_half,
        *cot_chunks[1], *cot_chunks[2],
    )

    chunks = gather_chunks(*stack_pairs(gather_row(payload), *cot_chunks[3]))
    outs_x, more, counts, carried = {}, [], [], ()
    for slot, i in enumerate((0, 1, 3, 2)):
        where_at = as_row(f // 4, 2 * (f % 4), slot)
        result = expert_chunk(
            order[i], where_at, chunks[i], cot_chunks[i], experts_w, carried
        )
        carried = result[0], *result[2:5]
        outs_x[i] = result[1]
        more += result[5:8]
        counts.append(result[8])
    parts = scatter_parts([outs_x[i] for i in range(4)], along(1))
    grads_e = expert_weights(as_row(t), carried[1:], more, counts, parts[1], parts[3])
    back, grads_e = add_blocks(parts, (grads_e,))
    back = scatter_parts(back, along(0))

    grads_e = lax.psum_scatter(
        grads_e.reshape(8, 2, 256, 768), ("context", "tensor"), scatter_dimension=0
    )
    mixed, grad_hidden, grad_branch, grad_router, grad_gain2 = route_back(
        [carried[0]], *back, cot_payload, hidden1, small, payload, probs, totals, match_half
    )
    mixed = lax.psum_scatter(mixed, "fsdp", scatter_dimension=0)
    branch_far = swap_cores(grad_branch)
    gq, gk, gv, gains = attend_back(
        q_b, q_proj, k_b, k_proj, v_b, seg,
        grad_branch, branch_far, weights, attended, cosine, sine, heads,
    )
    grads_w = weight_grads(
        place, normed1, gq, gk, gv, grad_branch, branch_far, attended, grad_router, grad_gain2, gains,
    )
    gin_m, gin_o = input_grads(gq, gk, gv, weights, grads_w[0])
    (sent,) = add_blocks((gin_m, swap_cores(gin_o)))
    gin = scatter_parts(sent, shift)
    both = lambda v, *others: join(as_row(t), v, swap_cores(v), *others)
    grad_tokens = both(finish(*gin, tokens_m, grad_hidden, small, grads_e))

    grads_w = scatter_parts(grads_w, along(1))
    (grads_w,) = add_blocks(grads_w, (), *sent[1:])
    grads_w = [v[None] for v in scatter_parts(grads_w, along(0))]
    ((grads_w,),) = add_blocks(grads_w, (), *gin[1:])
    g_query, g_key, g_value, g_out, sums = settle(
        *scatter_parts([grads_w] * 4, shift), w_query, w_key, w_value, attention_gain[None, :],
        grad_tokens,
    )
    sums = sums + swap_cores(sums)

    block_half = (hidden1 + mixed.astype(F32)).astype(BF)
    grads_e = grads_e.astype(F32)
    return (
        both(block_half, sums),
        grad_tokens,
        sums[:, 35],
        g_query,
        g_key,
        g_value,
        g_out,
        sums[0:4, 33],
        sums[0:4, 34],
        sums[:, 32],
        sums[:, 0:32],
        grads_e[:, :, 0:256],
        grads_e[:, :, 256:512],
        grads_e[:, :, 512:768],
    )


def solution(mesh):
    in_specs = (
        P("fsdp", "context", None),
        P("fsdp", None),
        P("fsdp", "context", None),
        P("fsdp"),
        P("fsdp", "tensor"),
        P("fsdp", "tensor"),
        P("fsdp", "tensor"),
        P("fsdp", "tensor"),
        P("fsdp"),
        P("fsdp"),
        P("fsdp"),
        P("fsdp", None),
        P("fsdp", None, "tensor"),
        P("fsdp", None, "tensor"),
        P("fsdp", None, "tensor"),
        P("fsdp", "context", None),
    )
    out_specs = (
        P("fsdp", "context", None),
        P("fsdp", "context", None),
        P("fsdp"),
        P("fsdp", "tensor"),
        P("fsdp", "tensor"),
        P("fsdp", "tensor"),
        P("fsdp", "tensor"),
        P("fsdp"),
        P("fsdp"),
        P("fsdp"),
        P("fsdp", None),
        P("fsdp", "context", "tensor"),
        P("fsdp", "context", "tensor"),
        P("fsdp", "context", "tensor"),
    )
    return jax.shard_map(local, mesh=mesh, in_specs=in_specs, out_specs=out_specs, check_vma=False)
```

```python
import functools

import jax
import jax.numpy as jnp
import numpy as np
from jax import lax
from jax.experimental import pallas as pl
from jax.experimental.pallas import tpu as pltpu
from jax.sharding import PartitionSpec as P

HD = 64
EXPERTS = 32
TOPK = 8
SEQ = 1024
D = 1024
ROWS = 512
HALF = 256
CAP = 160
MAIN = 96
TILES = -(-CAP // MAIN)
PAD = 272
N_FSDP = 16
N_CONTEXT = 4
EPS = 1e-06
NEGATIVE = -1e30
VMEM = 62 * 1024 * 1024
BF = jnp.bfloat16
F32 = jnp.float32
NT = (((1,), (1,)), ((), ()))
TN = (((0,), (0,)), ((), ()))


def dot(a, b):
    return jnp.dot(a, b, preferred_element_type=F32)


def dot_nt(a, b):
    return lax.dot_general(a, b, NT, preferred_element_type=F32)


def dot_tn(a, b):
    return lax.dot_general(a, b, TN, preferred_element_type=F32)


def split(v):
    high = v.astype(BF)
    return high, (v - high.astype(F32)).astype(BF)


def params(grid_dims):
    return pltpu.CompilerParams(
        dimension_semantics=("arbitrary",) * grid_dims, vmem_limit_bytes=VMEM
    )


def cost(flops, moved):
    return pl.CostEstimate(flops=flops, bytes_accessed=moved, transcendentals=0)


HBM = pl.BlockSpec(memory_space=pltpu.HBM)


def past(kernel, inputs, others):
    return lambda *refs: kernel(*refs[:inputs], *refs[inputs + others :])


def head_mean(v):
    rows = lax.broadcasted_iota(jnp.int32, (512, 256), 0) % 256 // HD
    cols = lax.broadcasted_iota(jnp.int32, (512, 256), 1) // HD
    block = jnp.where(rows == cols, 1.0, 0.0).astype(BF)
    return dot(jnp.concatenate(split(v), axis=1), block) * (1.0 / HD)


def swap_halves(v):
    lane = lax.broadcasted_iota(jnp.int32, v.shape, 1) % HD
    width = v.shape[1]
    return jnp.where(lane < HD // 2, pltpu.roll(v, width - 32, 1), pltpu.roll(v, 32, 1))


def twice(v):
    return jnp.concatenate([v, v], axis=1)


def rotary_tables():
    middle = HD // 2
    inverse = 10000.0 ** (-(2.0 * np.arange(middle, dtype=np.float64) / HD))
    inverse = inverse.astype(np.float32)
    angles = np.arange(SEQ, dtype=np.float32)[:, None] * inverse[None, :]
    angles = angles.astype(np.float64)
    cosine, sine = np.cos(angles).astype(np.float32), np.sin(angles).astype(np.float32)
    cosine = np.concatenate([cosine] * 4, axis=1)
    sine = np.concatenate([-sine, sine, -sine, sine], axis=1)
    order = lambda v: v.reshape(4, 4, 2, 32, 128).transpose(0, 2, 1, 3, 4).reshape(8, 128, 128)
    return order(cosine), order(sine)


def pack_kernel(where, w_query, w_key, w_value, w_out, router, gain1, gain2, q_gain, k_gain, out):
    out[:, 0:512] = w_query[...]
    out[:, 512:768] = w_key[...]
    out[:, 768:1024] = w_value[...]
    out[:, 1024:1536] = w_out[...]
    diagonal = lax.broadcasted_iota(jnp.int32, (64, 64), 0) == lax.broadcasted_iota(
        jnp.int32, (64, 64), 1
    )
    column = lambda v: jnp.sum(
        jnp.where(diagonal, v[...].astype(F32), 0.0), axis=1, keepdims=True
    )
    row = lax.broadcasted_iota(jnp.int32, (64, 128), 0)
    lane = lax.broadcasted_iota(jnp.int32, (64, 128), 1)
    small = jnp.where(lane == 32, column(gain1), 0.0) + jnp.where(lane == 33, column(gain2), 0.0)
    for i in range(4):
        here = lane == HD + 4 * where[0] + i
        for r, v in enumerate((q_gain, k_gain)):
            small = small + jnp.where(here & (row == r), v[0:1, i : i + 1].astype(F32), 0.0)
    lanes = lax.broadcasted_iota(jnp.int32, (EXPERTS, 128), 1)
    rows = lax.broadcasted_iota(jnp.int32, (EXPERTS, 128), 0)
    small = small + dot_tn(router[...], jnp.where(lanes == rows, 1.0, 0.0).astype(BF))
    out[:, 1536:1664] = small.astype(BF)


def pack(where, *arrays):
    whole = lambda v: pl.BlockSpec(v.shape, lambda i, r: (0, 0))
    return pl.pallas_call(
        pack_kernel,
        grid_spec=pltpu.PrefetchScalarGridSpec(
            num_scalar_prefetch=1,
            grid=(1,),
            in_specs=[whole(v) for v in arrays],
            out_specs=pl.BlockSpec((64, 1664), lambda i, r: (0, 0)),
        ),
        out_shape=jax.ShapeDtypeStruct((64, 1664), BF),
        compiler_params=params(1),
        cost_estimate=cost(10**6, 10**6),
        name="pack",
    )(where, *arrays)


def stack_pairs(blocks, *others):
    rows, width = blocks[0].shape

    def kernel(*refs):
        low, high, held, load_sem, send_sem = refs[4 + len(others) :]
        loads = [
            pltpu.make_async_copy(refs[i], held.at[i], load_sem.at[i]) for i in range(4)
        ]
        sends = [
            pltpu.make_async_copy(held.at[2 * i : 2 * i + 2], out, send_sem.at[i])
            for i, out in enumerate((low, high))
        ]
        for load in loads:
            load.start()
        for i in range(2):
            loads[2 * i].wait()
            loads[2 * i + 1].wait()
            sends[i].start()
        for send in sends:
            send.wait()

    return pl.pallas_call(
        kernel,
        in_specs=[HBM] * (4 + len(others)),
        out_specs=[HBM] * 2,
        out_shape=[jax.ShapeDtypeStruct((2, rows, width), BF)] * 2,
        scratch_shapes=[
            pltpu.VMEM((4, rows, width), BF),
            pltpu.SemaphoreType.DMA((4,)),
            pltpu.SemaphoreType.DMA((2,)),
        ],
        compiler_params=pltpu.CompilerParams(vmem_limit_bytes=VMEM),
        cost_estimate=cost(10**6, 10**6),
        name="stack_pairs",
    )(*blocks, *others)


def add_blocks(arrays, handed=(), *others):
    blocks, n, k = arrays[0].shape[0], len(arrays), len(handed)
    shape = arrays[0].shape[1:]

    def kernel(*refs):
        outs = refs[n + k + len(others) :][:blocks]
        held, total, load_sem, send_sem = refs[-4:]
        load = lambda i, j: pltpu.make_async_copy(
            refs[j].at[i], held.at[i * n + j], load_sem.at[i * n + j]
        )
        send = lambda i: pltpu.make_async_copy(total.at[i], outs[i], send_sem.at[i])
        for i in range(blocks):
            for j in range(n):
                load(i, j).start()
        for i in range(blocks):
            for j in range(n):
                load(i, j).wait()
            summed = held[i * n].astype(F32)
            for j in range(1, n):
                summed = summed + held[i * n + j].astype(F32)
            total[i] = summed.astype(BF)
            send(i).start()
        for i in range(blocks):
            send(i).wait()

    out = pl.pallas_call(
        kernel,
        in_specs=[HBM] * (n + k + len(others)),
        out_specs=[HBM] * (blocks + k),
        out_shape=[jax.ShapeDtypeStruct(shape, BF)] * blocks
        + [jax.ShapeDtypeStruct(v.shape, v.dtype) for v in handed],
        input_output_aliases={n + i: blocks + i for i in range(k)},
        scratch_shapes=[
            pltpu.VMEM((n * blocks, *shape), BF),
            pltpu.VMEM((blocks, *shape), BF),
            pltpu.SemaphoreType.DMA((n * blocks,)),
            pltpu.SemaphoreType.DMA((blocks,)),
        ],
        compiler_params=pltpu.CompilerParams(vmem_limit_bytes=VMEM),
        cost_estimate=cost(10**9, 10**7),
        name="add_blocks",
    )(*arrays, *handed, *others)
    return out[:blocks], *out[blocks:]


def pack_cotangent(where, cotangent, table, *others):
    def kernel(where, rows, table, out):
        out[0:HALF, :] = rows[...].reshape(HALF, D)
        out[HALF:PAD, :] = jnp.concatenate([table[...], jnp.zeros((8, D), BF)], axis=0)

    return pl.pallas_call(
        past(kernel, 3, len(others)),
        grid_spec=pltpu.PrefetchScalarGridSpec(
            num_scalar_prefetch=1,
            grid=(1,),
            in_specs=[
                pl.BlockSpec((2, 4, 1, 32, D), lambda i, r: (0, 0, r[0], 0, 0)),
                pl.BlockSpec((8, D), lambda i, r: (0, 0)),
            ]
            + [HBM] * len(others),
            out_specs=pl.BlockSpec((PAD, D), lambda i, r: (0, 0)),
        ),
        out_shape=jax.ShapeDtypeStruct((PAD, D), BF),
        compiler_params=params(1),
        cost_estimate=cost(10**6, 10**6),
        name="pack_cotangent",
    )(where, cotangent.reshape(2, 4, 2, 32, D), table, *others)


def project_kernel(
    order, near, x0, x1, x2, x3, x4, x5, x6, x7, w0, w1, w2, w3, cos_all, sin_all,
    w, small, heads, cosine, sine, normed, k_proj, k_b, v_b, q_proj, q_b,
):
    @pl.when(pl.program_id(0) == 0)
    def _():
        for i, shards in enumerate((w0, w1, w2, w3)):
            for j in range(4):
                to = pl.ds(pl.multiple_of(order[4 * i + j] * 64, 64), 64)
                w[to, :] = shards[j]
        for i in range(8):
            cosine[i * 128 : i * 128 + 128, :] = cos_all[near[i]]
            sine[i * 128 : i * 128 + 128, :] = sin_all[near[i]]
        last = w[:, 1536:1664].astype(F32)
        small[...] = last.T
        summed = last[0:64]
        for i in range(1, N_FSDP):
            summed = summed + last[i * 64 : i * 64 + 64]
        lane = lax.broadcasted_iota(jnp.int32, (8, 128), 1)
        gains = jnp.where(lane >= HD, summed[0:8], 0.0)
        heads[...] = gains + pltpu.roll(gains, HD, 1)

    gain = small[32:33, :]
    for i, x in enumerate((x0, x1, x2, x3, x4, x5, x6, x7)):
        values = x[0].astype(F32)
        factor = lax.rsqrt(jnp.mean(values * values, axis=1, keepdims=True) + EPS)
        normed[0, i * 128 : i * 128 + 128, :] = (values * factor * gain).astype(BF)
    both = dot(normed[0], w[:, 512:1024])
    keys = both[:, 0:256]
    k_proj[0] = keys
    v_b[0] = both[:, 256:512].astype(BF)
    cos, sin = twice(cosine[...]), twice(sine[...])
    scaled = keys * lax.rsqrt(head_mean(keys * keys) + EPS) * twice(heads[1:2, :])
    k_b[0] = (scaled * cos + swap_halves(scaled) * sin).astype(BF)
    queries = dot(normed[0, 0:256, :], w[:, 0:512])
    q_proj[0] = queries
    for block in range(2):
        at = slice(block * 256, block * 256 + 256)
        head = queries[:, at]
        scaled = head * lax.rsqrt(head_mean(head * head) + EPS) * twice(heads[0:1, :])
        turned = scaled * cos[0:256] + swap_halves(scaled) * sin[0:256]
        q_b[0, :, at] = (turned.astype(BF).astype(F32) * 0.125).astype(BF)


def project(order, near, tokens, shards, cosine, sine, *others):
    row = lambda s, r, n: (0, 0)
    of = lambda s, r, n: (s, 0, 0)
    block = lambda i: pl.BlockSpec((1, 128, D), lambda s, r, n: (n[i], s, 0))
    fixed = ((D, 1664, BF), (128, D, F32), (8, 128, F32), (SEQ, 128, F32), (SEQ, 128, F32))
    shapes = ((SEQ, D, BF), (SEQ, 256, F32), (SEQ, 256, BF), (SEQ, 256, BF), (256, 512, F32), (256, 512, BF))
    return pl.pallas_call(
        past(project_kernel, 16, len(others)),
        grid_spec=pltpu.PrefetchScalarGridSpec(
            num_scalar_prefetch=2,
            grid=(2,),
            in_specs=[block(i) for i in range(8)]
            + [pl.BlockSpec((4, 64, 1664), lambda s, r, n: (0, 0, 0))] * 4
            + [pl.BlockSpec((8, 128, 128), lambda s, r, n: (0, 0, 0))] * 2
            + [HBM] * len(others),
            out_specs=[pl.BlockSpec((r, n), row) for r, n, _ in fixed]
            + [pl.BlockSpec((1, r, n), of) for r, n, _ in shapes],
        ),
        out_shape=[jax.ShapeDtypeStruct((r, n), dt) for r, n, dt in fixed]
        + [jax.ShapeDtypeStruct((2, r, n), dt) for r, n, dt in shapes],
        compiler_params=params(1),
        cost_estimate=cost(10 * 10**9, 20 * 10**6),
        name="project",
    )(order, near, *([tokens] * 8), *shards, cosine, sine, *others)


def as_column(row):
    return jnp.broadcast_to(row, (8, row.shape[1])).T[:, 0:1]


def place_head(v, target, source):
    moved = v if target == source else pltpu.roll(v, HD, 1)
    lane = lax.broadcasted_iota(jnp.int32, v.shape, 1) // HD
    return jnp.where(lane == target, moved, jnp.zeros_like(moved))


def stack_heads(v):
    parts = []
    for block in range(2):
        for j in range(2):
            parts.append(place_head(v[:, block * 128 : block * 128 + 128], block, j))
    return jnp.concatenate(parts, axis=0)


def unstack_heads(v):
    blocks = []
    for block in range(2):
        pair = [v[(2 * block + j) * 256 : (2 * block + j + 1) * 256] for j in range(2)]
        blocks.append(place_head(pair[0], 0, block) + place_head(pair[1], 1, block))
    return jnp.concatenate(blocks, axis=1)


def attend_kernel(q, k, v, seg, w_out, attended, mine, other):
    row = seg[0]
    mask = jnp.where(as_column(row[:, 0:HALF]) == row, 0.0, NEGATIVE)
    queries = stack_heads(q[0].astype(F32)).astype(BF)
    scores = dot_nt(queries, k[0])
    weights = jnp.concatenate(
        [jnp.exp(scores[i * 256 : i * 256 + 256] + mask).astype(BF) for i in range(4)], axis=0
    )
    summed = dot(weights, jnp.concatenate([v[0], jnp.ones((SEQ, 128), BF)], axis=1))
    mixed = unstack_heads(summed[:, :128] / summed[:, 128:]).astype(BF)
    attended[0] = mixed
    part = dot_nt(mixed, w_out[...])

    @pl.when(pl.program_id(1) == 0)
    def _():
        mine[...] = part[0:128]
        other[...] = part[128:256]

    @pl.when(pl.program_id(1) != 0)
    def _():
        mine[...] += part[0:128]
        other[...] += part[128:256]


def attend(q_b, k_b, v_b, seg, w_out, *others):
    half = pl.BlockSpec((128, D), lambda s, p: (s, 0))
    return pl.pallas_call(
        past(attend_kernel, 5, len(others)),
        grid=(2, 2),
        in_specs=[
            pl.BlockSpec((1, HALF, 256), lambda s, p: (s, 0, p)),
            pl.BlockSpec((1, SEQ, 128), lambda s, p: (s, 0, p)),
            pl.BlockSpec((1, SEQ, 128), lambda s, p: (s, 0, p)),
            pl.BlockSpec((1, 1, SEQ), lambda s, p: (s, 0, 0)),
            pl.BlockSpec((D, 256), lambda s, p: (0, 4 + p)),
        ]
        + [HBM] * len(others),
        out_specs=[pl.BlockSpec((1, HALF, 256), lambda s, p: (s, 0, p)), half, half],
        out_shape=[
            jax.ShapeDtypeStruct((2, HALF, 512), BF),
            jax.ShapeDtypeStruct((HALF, D), F32),
            jax.ShapeDtypeStruct((HALF, D), F32),
        ],
        compiler_params=params(2),
        cost_estimate=cost(10 * 10**9, 8 * 10**6),
        name="attend",
    )(q_b, k_b, v_b, seg, w_out, *others)


def experts_to_rows(table):
    return jnp.concatenate([table[8 * k : 8 * k + 8] for k in range(4)], axis=1)


def rows_to_experts(rows):
    return jnp.concatenate([rows[:, 256 * k : 256 * k + 256] for k in range(4)], axis=0)


def route_kernel(tokens, mine, other, small, match, kept, hidden, payload, probs, totals):
    values = tokens[...].astype(F32) + mine[...] + other[...]
    hidden[...] = values
    factor = lax.rsqrt(jnp.mean(values * values, axis=1, keepdims=True) + EPS)
    rows = (values * factor * small[33:34, :]).astype(BF)
    payload[0:HALF, :] = rows
    logits = dot_nt(small[0:32, :].astype(BF), rows)
    raised = jnp.exp(logits - jnp.max(logits, axis=0, keepdims=True))
    prob = raised / jnp.sum(raised, axis=0, keepdims=True)
    probs[...] = prob
    chosen = prob * match[...]
    total = jnp.sum(chosen, axis=0, keepdims=True)
    totals[...] = total
    high, low = split(experts_to_rows(chosen / total * kept[...]))
    payload[HALF:PAD, :] = jnp.concatenate([high, low], axis=0)


def route(*args):
    return pl.pallas_call(
        past(route_kernel, 6, len(args) - 6),
        in_specs=[pl.BlockSpec(memory_space=pltpu.VMEM)] * 6 + [HBM] * (len(args) - 6),
        out_shape=[
            jax.ShapeDtypeStruct((HALF, D), F32),
            jax.ShapeDtypeStruct((PAD, D), BF),
            jax.ShapeDtypeStruct((EXPERTS, HALF), F32),
            jax.ShapeDtypeStruct((1, HALF), F32),
        ],
        compiler_params=pltpu.CompilerParams(vmem_limit_bytes=VMEM),
        cost_estimate=cost(10**8, 5 * 10**6),
        name="route",
    )(*args)


def own_row(table, lane_block, row):
    picked = jnp.zeros((8, 256), F32)
    for k in range(4):
        picked = picked + jnp.where(lane_block == k, table[:, 256 * k : 256 * k + 256], 0.0)
    number = lax.broadcasted_iota(jnp.int32, (8, 256), 0)
    return jnp.sum(jnp.where(number == row, picked, 0.0), axis=0, keepdims=True)


def expert_math(x, g, gate, w):
    pre = dot(x, w[:, 0:1024])
    grad_all = dot(g, w[:, 1024:1536])
    acts, grads, gate_dot = [], [], 0.0
    for part in range(2):
        gate_pre = pre[:, part * 512 : part * 512 + 256]
        up_pre = pre[:, part * 512 + 256 : part * 512 + 512]
        grad = grad_all[:, part * 256 : part * 256 + 256]
        sig = jax.nn.sigmoid(gate_pre)
        swish = gate_pre * sig
        act = (swish * up_pre).astype(BF).astype(F32)
        gate_dot = gate_dot + jnp.sum(act * grad, axis=1, keepdims=True)
        acts.append((act * gate).astype(BF))
        grad = grad * gate
        grads.append((grad * up_pre * sig * (1.0 + gate_pre * (1.0 - sig))).astype(BF))
        grads.append((grad * swish).astype(BF))
    act = jnp.concatenate(acts, axis=1)
    grad = jnp.concatenate(grads, axis=1)
    y = dot_nt(act, w[:, 1024:1536]).astype(BF)
    back = dot_nt(grad, w[:, 0:1024]).astype(BF)
    return y, back, act, grad, gate_dot


def pick_rows(places, first, rows):
    number = lax.broadcasted_iota(jnp.int32, (rows, 256), 0) + first
    return number == places.astype(jnp.int32)


def expert_kernel(order, where_at, x_low, x_high, c_low, c_high, w_gate, w_up, w_down, *refs):
    refs = refs[len(refs) - 25 :]
    out_y, out_x, kept_x, kept_g, kept_h, more_x, more_g, more_h, tiles = refs[:9]
    x_all, c_all, wv, xs, gs, hs, picks, sums, ys, bs, total, places, gate_rows, dots = refs[9:23]
    in_sem, out_sem = refs[23:]
    slot = where_at[2]
    lane_block, row_at = where_at[0], where_at[1]
    copy = pltpu.make_async_copy
    loads = [
        copy(x_low, x_all.at[0:2], in_sem.at[0]),
        copy(c_low, c_all.at[0:2], in_sem.at[1]),
        copy(x_high, x_all.at[2:4], in_sem.at[2]),
        copy(c_high, c_all.at[2:4], in_sem.at[3]),
    ]

    def load_w(e):
        copies = []
        for part in range(2):
            for w, at in ((w_gate, 512 * part), (w_up, 512 * part + 256), (w_down, 1024 + 256 * part)):
                sem = in_sem.at[4 + 2 * len(copies) + e]
                copies.append(copy(w.at[part, e], wv.at[e, :, at : at + 256], sem))
        return copies

    for load in loads + load_w(0) + load_w(1):
        load.start()
    for load in loads:
        load.wait()

    def read(h, carry):
        table = c_all[h, HALF : HALF + 8, :].astype(F32)
        gate_table = x_all[h, HALF:PAD, :].astype(F32)
        gate_table = gate_table[0:8] + gate_table[8:16]
        for e in range(2):
            places[pl.ds(4 * e + h, 1), :] = own_row(table, lane_block, row_at + e)
            gate_rows[pl.ds(4 * e + h, 1), :] = own_row(gate_table, lane_block, row_at + e)
        return carry

    lax.fori_loop(0, 4, read, 0)
    most = jnp.max(places[...]).astype(jnp.int32)
    count = jnp.maximum(most, 0) // MAIN + 1
    tiles[...] = jnp.zeros((8, 128), F32) + count.astype(F32)

    rows = pl.ds(pl.multiple_of(slot * (4 * MAIN), 4 * MAIN), 4 * MAIN)

    def tile(i, carry):
        first = i * MAIN
        more = pl.ds(pl.multiple_of(jnp.maximum(i - 1, 0) * (4 * MAIN), 4 * MAIN), 4 * MAIN)
        sends = lambda e: (
            (xs, kept_x, more_x, e),
            (gs, kept_g, more_g, 2 + e),
            (hs, kept_h, more_h, 4 + e),
        )

        def start(v, kept, other, e, n):
            @pl.when(i == 0)
            def _():
                copy(v.at[e], kept.at[e, rows], out_sem.at[n]).start()

            @pl.when(i > 0)
            def _():
                copy(v.at[e], other.at[e, more], out_sem.at[n]).start()

        def gather(h, carry):
            pick = [
                jnp.where(pick_rows(places[pl.ds(4 * e + h, 1), :], first, MAIN), 1.0, 0.0)
                for e in range(2)
            ]
            pick = jnp.concatenate(pick, axis=0).astype(BF)
            picks[h] = pick
            x = dot(pick, x_all[h, 0:HALF, :]).astype(BF)
            g = dot(pick, c_all[h, 0:HALF, :]).astype(BF)
            to = pl.ds(pl.multiple_of(h * MAIN, MAIN), MAIN)
            for e in range(2):
                xs[e, to, :] = x[e * MAIN : e * MAIN + MAIN]
                gs[e, to, :] = g[e * MAIN : e * MAIN + MAIN]
            return carry

        lax.fori_loop(0, 4, gather, 0)
        for e in range(2):
            start(xs, kept_x, more_x, e, e)
            start(gs, kept_g, more_g, e, 2 + e)

        def math(e, carry):
            here = [pick_rows(places[pl.ds(4 * e + h, 1), :], first, MAIN) for h in range(4)]
            gate = [
                jnp.sum(
                    jnp.where(here[h], gate_rows[pl.ds(4 * e + h, 1), :], 0.0),
                    axis=1,
                    keepdims=True,
                )
                for h in range(4)
            ]

            @pl.when(i == 0)
            def _():
                for load in load_w(e):
                    load.wait()

            y, back, act, grad, gate_dot = expert_math(
                xs[e], gs[e], jnp.concatenate(gate, axis=0), wv.at[e]
            )
            hs[e, :, 0:512] = act
            hs[e, :, 512:1536] = grad
            start(hs, kept_h, more_h, e, 4 + e)
            to = pl.ds(pl.multiple_of(e * MAIN, MAIN), MAIN)
            for h in range(4):
                at = slice(h * MAIN, h * MAIN + MAIN)
                sums[h, to, 0:D] = y[at]
                sums[h, to, D : 2 * D] = back[at]
                spread = jnp.sum(jnp.where(here[h], gate_dot[at], 0.0), axis=0, keepdims=True)
                row = pl.ds(4 * e + h, 1)
                dots[row, :] = jnp.where(i == 0, 0.0, dots[row, :]) + spread
            return carry

        lax.fori_loop(0, 2, math, 0)
        last = i == count - 1

        def scatter(h, carry):
            out = dot_tn(picks[h], sums[h])
            at = pl.ds(pl.multiple_of(h * HALF, HALF), HALF)

            @pl.when(i > 0)
            def _():
                total[at, :] += out

            @pl.when((i == 0) & jnp.logical_not(last))
            def _():
                total[at, :] = out

            @pl.when(last)
            def _():
                @pl.when(i == 0)
                def _():
                    ys[h] = out[:, 0:D].astype(BF)
                    bs[h, 0:HALF, :] = out[:, D : 2 * D].astype(BF)

                @pl.when(i > 0)
                def _():
                    ys[h] = total[at, 0:D].astype(BF)
                    bs[h, 0:HALF, :] = total[at, D : 2 * D].astype(BF)

                row = lax.broadcasted_iota(jnp.int32, (8, 256), 0)
                table = jnp.where(row == row_at, dots[pl.ds(h, 1), :], 0.0)
                table = table + jnp.where(row == row_at + 1, dots[pl.ds(4 + h, 1), :], 0.0)
                table = [jnp.where(lane_block == k, table, 0.0) for k in range(4)]
                high, low = split(jnp.concatenate(table, axis=1))
                bs[h, HALF:PAD, :] = jnp.concatenate([high, low], axis=0)
                copy(bs.at[h], out_x.at[h], out_sem.at[6 + h]).start()
                copy(ys.at[h], out_y.at[order[h]], out_sem.at[10 + h]).start()

            return carry

        lax.fori_loop(0, 4, scatter, 0)
        for e in range(2):
            for v, kept, _, n in sends(e):
                copy(v.at[e], kept.at[e, rows], out_sem.at[n]).wait()
        return carry

    lax.fori_loop(0, count, tile, 0)
    for h in range(4):
        copy(bs.at[h], out_x.at[h], out_sem.at[6 + h]).wait()
        copy(ys.at[h], out_y.at[order[h]], out_sem.at[10 + h]).wait()


def expert_chunk(order, where_at, x, cotangents, weights, kept):
    rows = 4 * MAIN
    widths = (D, D, 1536)
    shape = lambda *v: jax.ShapeDtypeStruct(v, BF)
    vmem = lambda *v: pltpu.VMEM(v, BF)
    aliases = {9: 0, 10: 2, 11: 3, 12: 4} if kept else {}
    return pl.pallas_call(
        expert_kernel,
        grid_spec=pltpu.PrefetchScalarGridSpec(
            num_scalar_prefetch=2,
            grid=(1,),
            in_specs=[HBM] * (7 + len(kept)),
            out_specs=[HBM] * 8 + [pl.BlockSpec((8, 128), lambda i, r, w: (0, 0))],
            scratch_shapes=[
                vmem(4, PAD, D),
                vmem(4, PAD, D),
                vmem(2, D, 1536),
                vmem(2, rows, D),
                vmem(2, rows, D),
                vmem(2, rows, 1536),
                vmem(4, 2 * MAIN, 256),
                vmem(4, 2 * MAIN, 2 * D),
                vmem(4, HALF, D),
                vmem(4, PAD, D),
                pltpu.VMEM((1024, 2 * D), F32),
                pltpu.VMEM((8, 256), F32),
                pltpu.VMEM((8, 256), F32),
                pltpu.VMEM((8, 256), F32),
                pltpu.SemaphoreType.DMA((16,)),
                pltpu.SemaphoreType.DMA((14,)),
            ],
        ),
        out_shape=[shape(N_FSDP, HALF, D), shape(4, PAD, D)]
        + [shape(2, 4 * rows, n) for n in widths]
        + [shape(2, (TILES - 1) * rows, n) for n in widths]
        + [jax.ShapeDtypeStruct((8, 128), F32)],
        input_output_aliases=aliases,
        compiler_params=params(1),
        cost_estimate=cost(14 * 10**9, 30 * 10**6),
        name="experts",
    )(order, where_at, *x, *cotangents, *weights, *kept)


def expert_weight_kernel(place, x, g, act, grad, *refs):
    more, counts, (down, gate_up), (mx, mg, mh) = refs[:12], refs[12:16], refs[-5:-3], refs[-3:]
    out = refs[-6]
    expert, part = pl.program_id(0), pl.program_id(1)
    down[...] = dot_tn(g[0], act[0])
    gate_up[...] = dot_tn(x[0], grad[0])
    for chunk in range(4):
        count = jnp.max(counts[chunk][...]).astype(jnp.int32) - 1

        @pl.when(count > 0)
        def _(chunk=chunk, count=count):
            def piece(i, carry):
                rows = pl.ds(pl.multiple_of(i * 4 * MAIN, 4 * MAIN), 4 * MAIN)
                for ref, to in zip(more[3 * chunk : 3 * chunk + 3], (mx, mg, mh)):
                    pltpu.sync_copy(ref.at[expert, rows], to)
                for p in range(2):

                    @pl.when(part == p)
                    def _(p=p):
                        at = p * 256
                        down[...] += dot_tn(mg[...], mh[:, at : at + 256])
                        at = 512 + p * 512
                        gate_up[...] += dot_tn(mx[...], mh[:, at : at + 512])

                return carry

            lax.fori_loop(0, count, piece, 0)

    for c in range(4):
        at = slice(c * 256, c * 256 + 256)
        out[c, 0, 0, :, 0:512] = gate_up[at, :].astype(BF)
        out[c, 0, 0, :, 512:768] = down[at, :].astype(BF)


def expert_weights(place, kept, more, counts, *others):
    rows = 16 * MAIN
    by_expert = lambda e, p, r: (e, 0, 0)
    return pl.pallas_call(
        expert_weight_kernel,
        grid_spec=pltpu.PrefetchScalarGridSpec(
            num_scalar_prefetch=1,
            grid=(2, 2),
            in_specs=[
                pl.BlockSpec((1, rows, D), by_expert),
                pl.BlockSpec((1, rows, D), by_expert),
                pl.BlockSpec((1, rows, 256), lambda e, p, r: (e, 0, p)),
                pl.BlockSpec((1, rows, 512), lambda e, p, r: (e, 0, 1 + p)),
            ]
            + [HBM] * 12
            + [pl.BlockSpec((8, 128), lambda e, p, r: (0, 0))] * 4
            + [HBM] * len(others),
            out_specs=pl.BlockSpec(
                (4, 1, 1, 256, 768),
                lambda e, p, r: (0, p, e, 0, 0),
            ),
            scratch_shapes=[
                pltpu.VMEM((D, 256), F32),
                pltpu.VMEM((D, 512), F32),
                pltpu.VMEM((4 * MAIN, D), BF),
                pltpu.VMEM((4 * MAIN, D), BF),
                pltpu.VMEM((4 * MAIN, 1536), BF),
            ],
        ),
        out_shape=jax.ShapeDtypeStruct((4, 2, 2, 256, 768), BF),
        compiler_params=params(2),
        cost_estimate=cost(20 * 10**9, 30 * 10**6),
        name="expert_weights",
    )(place, kept[0], kept[1], kept[2], kept[2], *more, *counts, *others)


def route_back_kernel(
    own, first, second, third, cotangent, hidden, small, normed, probs, totals, match,
    grad_hidden, grad_branch, grad_router, grad_gain,
):
    summed = own[...].astype(F32) + first[...].astype(F32)
    summed = summed + (second[...].astype(F32) + third[...].astype(F32))
    tables = summed[HALF:PAD, :]
    grad_gates = rows_to_experts(tables[0:8] + tables[8:16])
    prob, total = probs[...], totals[...]
    chosen = prob * match[...]
    shared = jnp.sum(grad_gates * chosen, axis=0, keepdims=True) / (total * total)
    grad_prob = (grad_gates / total - shared) * match[...]
    grad_logits = prob * (grad_prob - jnp.sum(prob * grad_prob, axis=0, keepdims=True))
    high, low = split(grad_logits)
    grad_router[...] = dot(high, normed[0:HALF, :]) + dot(low, normed[0:HALF, :])
    router = small[0:32, :].astype(BF)
    grad_normed = summed[0:HALF, :] + dot_tn(high, router) + dot_tn(low, router)
    values = hidden[...]
    factor = lax.rsqrt(jnp.mean(values * values, axis=1, keepdims=True) + EPS)
    grad_gain[...] = jnp.sum(grad_normed * values * factor, axis=0, keepdims=True)
    weighted = grad_normed * small[33:34, :]
    mean = jnp.mean(weighted * values, axis=1, keepdims=True)
    grad = cotangent[0:HALF, :].astype(F32) + factor * weighted - values * (factor * factor * factor * mean)
    grad_hidden[...] = grad
    grad_branch[...] = grad.astype(BF)


def route_back(handed, *args):
    n, others, shapes = len(handed), len(args) - 11, [jax.ShapeDtypeStruct(v.shape, v.dtype) for v in handed]
    vmem = pl.BlockSpec(memory_space=pltpu.VMEM)
    kernel = past(route_back_kernel, 11, others + n)
    return pl.pallas_call(
        lambda *refs: kernel(*refs[n:]),
        in_specs=[HBM] * n + [vmem] * 11 + [HBM] * others,
        out_specs=[HBM] * n + [vmem] * 4,
        input_output_aliases={i: i for i in range(n)},
        out_shape=shapes
        + [
            jax.ShapeDtypeStruct((HALF, D), F32),
            jax.ShapeDtypeStruct((HALF, D), BF),
            jax.ShapeDtypeStruct((EXPERTS, D), F32),
            jax.ShapeDtypeStruct((1, D), F32),
        ],
        compiler_params=pltpu.CompilerParams(vmem_limit_bytes=VMEM),
        cost_estimate=cost(4 * 10**9, 6 * 10**6),
        name="route_back",
    )(*handed, *args)


def norm_back_heads(grad, proj, gain, cosine, sine):
    turned = grad * cosine - swap_halves(grad) * sine
    factor = lax.rsqrt(head_mean(proj * proj) + EPS)
    weighted = turned * gain
    mean = head_mean(weighted * proj)
    back = factor * weighted - proj * (factor * factor * factor * mean)
    return back, jnp.sum(turned * proj * factor, axis=0, keepdims=True)


def attend_back_kernel(
    q, q_proj, k, k_proj, v, seg, branch_m, branch_o, w_out, attended,
    cosine, sine, heads, grad_q, grad_k, grad_v, gains,
):
    row = seg[0]
    mask = jnp.where(as_column(row) == row[:, 0:HALF], 0.0, NEGATIVE)
    keys, values = k[0], v[0]
    grad_branch = jnp.concatenate([branch_m[...], branch_o[...]], axis=0)
    grad_mixed = dot(grad_branch, w_out[...]).astype(BF).astype(F32)
    queries = stack_heads(q[0].astype(F32)).astype(BF)
    grads = stack_heads(grad_mixed).astype(BF)
    high, low = split(stack_heads(attended[0].astype(F32) * grad_mixed))
    ones = jnp.ones((8, 256), BF)
    row_dot = dot_nt(ones, jnp.concatenate([high, low], axis=1))[0:1]
    scores = dot_nt(keys, queries)
    grad_probs = dot_nt(values, grads)
    probs_b, grad_scores = [], []
    for i in range(4):
        at = slice(i * 256, i * 256 + 256)
        raised = jnp.exp(scores[:, at] + mask)
        probs = raised * (1.0 / jnp.sum(raised, axis=0, keepdims=True))
        probs_b.append(probs.astype(BF))
        grad_scores.append((probs * (grad_probs[:, at] - row_dot[:, at])).astype(BF))
    probs_b = jnp.concatenate(probs_b, axis=1)
    grad_scores = jnp.concatenate(grad_scores, axis=1)
    grad_v[0] = dot(probs_b, grads).astype(BF)
    sum_k = dot(grad_scores, queries)
    sum_q = unstack_heads(dot_tn(grad_scores, keys) * 0.125)
    cos, sin = cosine[...], sine[...]
    back, gain_q = norm_back_heads(
        sum_q, q_proj[0], twice(heads[0:1, :]), twice(cos[0:256]), twice(sin[0:256])
    )
    grad_q[0] = back.astype(BF)
    wide = lambda value: jnp.concatenate([value[0:512], value[512:1024]], axis=1)
    back, gain_k = norm_back_heads(
        wide(sum_k), wide(k_proj[0]), twice(heads[1:2, :]), wide(cos), wide(sin)
    )
    grad_k[0, 0:512, :] = back[:, 0:128].astype(BF)
    grad_k[0, 512:1024, :] = back[:, 128:256].astype(BF)
    part = jnp.concatenate([gain_q, gain_k, jnp.zeros((6, 256), F32)], axis=0)

    @pl.when((pl.program_id(0) == 0) & (pl.program_id(1) == 0))
    def _():
        gains[...] = part

    @pl.when((pl.program_id(0) != 0) | (pl.program_id(1) != 0))
    def _():
        gains[...] += part


def attend_back(
    q_b, q_proj, k_b, k_proj, v_b, seg, branch_m, branch_o, w_out, attended,
    cosine, sine, heads,
):
    queries = pl.BlockSpec((1, HALF, 256), lambda s, p: (s, 0, p))
    keys = pl.BlockSpec((1, SEQ, 128), lambda s, p: (s, 0, p))
    table = pl.BlockSpec((SEQ, 128), lambda s, p: (0, 0))
    gain = pl.BlockSpec((8, 128), lambda s, p: (0, 0))
    half = pl.BlockSpec((128, D), lambda s, p: (s, 0))
    return pl.pallas_call(
        attend_back_kernel,
        grid=(2, 2),
        in_specs=[
            queries, queries, keys, keys, keys,
            pl.BlockSpec((1, 1, SEQ), lambda s, p: (s, 0, 0)),
            half, half,
            pl.BlockSpec((D, 256), lambda s, p: (0, 4 + p)),
            queries, table, table, gain,
        ],
        out_specs=[queries, keys, keys, pl.BlockSpec((8, 256), lambda s, p: (0, 0))],
        out_shape=[
            jax.ShapeDtypeStruct((2, HALF, 512), BF),
            jax.ShapeDtypeStruct((2, SEQ, 256), BF),
            jax.ShapeDtypeStruct((2, SEQ, 256), BF),
            jax.ShapeDtypeStruct((8, 256), F32),
        ],
        compiler_params=params(2),
        cost_estimate=cost(18 * 10**9, 16 * 10**6),
        name="attend_back",
    )(
        q_b, q_proj, k_b, k_proj, v_b, seg, branch_m, branch_o, w_out, attended,
        cosine, sine, heads,
    )


def weight_grads_kernel(
    place, normed, gq, gk, gv, branch_m, branch_o, mixed, router, gain, head_gains,
    out_0, out_1, out_2, out_3, out, sem,
):
    step = pl.program_id(0)
    rows = jnp.concatenate([normed[0], normed[1]], axis=0)
    own = jnp.concatenate([normed[0, 0:256, :], normed[1, 0:256, :]], axis=0)
    keys = jnp.concatenate(
        [
            jnp.concatenate([gk[0], gk[1]], axis=0),
            jnp.concatenate([gv[0], gv[1]], axis=0),
        ],
        axis=1,
    )
    queries = jnp.concatenate([gq[0], gq[1]], axis=0)
    branch = jnp.concatenate(
        [branch_m[0:128], branch_o[0:128], branch_m[128:256], branch_o[128:256]], axis=0
    )
    heads = jnp.concatenate([mixed[0], mixed[1]], axis=0)
    at = lax.broadcasted_iota(jnp.int32, (256, 256), 1)
    share = 4 * (at // HD + 4 * step) + at % HD
    spread = (lax.broadcasted_iota(jnp.int32, (256, 256), 0) % HD == share) & (at % HD < 4)
    spread = jnp.where(spread, 1.0, 0.0).astype(BF)
    high, low = split(head_gains[...])
    spread = dot(high, spread) + dot(low, spread)
    row = lax.broadcasted_iota(jnp.int32, (8, 256), 0)
    last = jnp.where(row == 0, gain[...], 0.0)
    last = last + jnp.where(row == 1, spread[0:1], 0.0) + jnp.where(row == 2, spread[1:2], 0.0)
    small = jnp.concatenate([router[...], last, jnp.zeros((88, 256), F32)], axis=0)
    parts = (
        (0, 512, dot_tn(own, queries).astype(BF)),
        (512, 1024, dot_tn(rows, keys).astype(BF)),
        (1024, 1536, dot_tn(branch, heads).astype(BF)),
        (1536, 1664, small.T.astype(BF)),
    )
    for i in range(4):
        to = place[4 * step + i]
        for low, high, value in parts:
            out[to, :, low:high] = value[i * 64 : i * 64 + 64]

    @pl.when(step == 3)
    def _():
        sends = [
            pltpu.make_async_copy(out.at[4 * i : 4 * i + 4], to, sem.at[i])
            for i, to in enumerate((out_0, out_1, out_2, out_3))
        ]
        for send in sends:
            send.start()
        for send in sends:
            send.wait()


def weight_grads(place, *args):
    fixed = lambda i, r: (0, 0, 0)
    column = pl.BlockSpec((HALF, 256), lambda i, r: (0, i))
    return pl.pallas_call(
        past(weight_grads_kernel, 11, len(args) - 10),
        grid_spec=pltpu.PrefetchScalarGridSpec(
            num_scalar_prefetch=1,
            grid=(4,),
            in_specs=[
                pl.BlockSpec((2, SEQ, 256), lambda i, r: (0, 0, i)),
                pl.BlockSpec((2, HALF, 512), fixed),
                pl.BlockSpec((2, SEQ, 256), fixed),
                pl.BlockSpec((2, SEQ, 256), fixed),
                column,
                column,
                pl.BlockSpec((2, HALF, 512), fixed),
                pl.BlockSpec((EXPERTS, 256), lambda i, r: (0, i)),
                pl.BlockSpec((1, 256), lambda i, r: (0, i)),
                pl.BlockSpec((8, 256), lambda i, r: (0, 0)),
            ]
            + [HBM] * (len(args) - 10),
            out_specs=[HBM] * 4,
            scratch_shapes=[pltpu.VMEM((N_FSDP, 64, 1664), BF), pltpu.SemaphoreType.DMA((4,))],
        ),
        out_shape=[jax.ShapeDtypeStruct((4, 64, 1664), BF)] * 4,
        compiler_params=params(1),
        cost_estimate=cost(9 * 10**9, 16 * 10**6),
        name="weight_grads",
    )(place, *args)


def input_grads_kernel(gq, gk, gv, w, mine, other):
    part = dot_nt(jnp.concatenate([gk[0], gv[0]], axis=1), w[:, 512:1024])
    own = dot_nt(gq[0], w[:, 0:512])
    for c in range(4):
        for parity, out in enumerate((mine, other)):
            at = slice(c * 256 + parity * 128, c * 256 + parity * 128 + 128)
            value = part[at] + own[at] if c == 0 else part[at]
            out[c] = value.astype(BF)


def input_grads(gq, gk, gv, weights, *others):
    by = lambda s: (s, 0, 0)
    half = pl.BlockSpec((4, 128, D), lambda s: (0, s, 0))
    return pl.pallas_call(
        past(input_grads_kernel, 4, len(others)),
        grid=(2,),
        in_specs=[
            pl.BlockSpec((1, HALF, 512), by),
            pl.BlockSpec((1, SEQ, 256), by),
            pl.BlockSpec((1, SEQ, 256), by),
            pl.BlockSpec((D, 1024), lambda s: (0, 0)),
        ]
        + [HBM] * len(others),
        out_specs=[half, half],
        out_shape=[jax.ShapeDtypeStruct((4, HALF, D), BF)] * 2,
        compiler_params=params(1),
        cost_estimate=cost(6 * 10**9, 12 * 10**6),
        name="input_grads",
    )(gq, gk, gv, weights, *others)


def finish_kernel(own, first, second, third, tokens, grad_hidden, small, out):
    values = tokens[...].astype(F32)
    factor = lax.rsqrt(jnp.mean(values * values, axis=1, keepdims=True) + EPS)
    summed = own[...].astype(F32) + first[...].astype(F32)
    summed = summed + (second[...].astype(F32) + third[...].astype(F32))
    weighted = summed * small[32:33, :]
    mean = jnp.mean(weighted * values, axis=1, keepdims=True)
    out[...] = grad_hidden[...] + factor * weighted - values * (factor * factor * factor * mean)


def finish(*args):
    return pl.pallas_call(
        past(finish_kernel, 7, len(args) - 7),
        in_specs=[pl.BlockSpec(memory_space=pltpu.VMEM)] * 7 + [HBM] * (len(args) - 7),
        out_shape=jax.ShapeDtypeStruct((HALF, D), F32),
        compiler_params=pltpu.CompilerParams(vmem_limit_bytes=VMEM),
        cost_estimate=cost(10**7, 6 * 10**6),
        name="finish",
    )(*args)


def settle_kernel(
    own, first, second, third, w_query, w_key, w_value, gain, g_query, g_key, g_value, g_out, sums
):
    summed = own[...].astype(F32) + first[...].astype(F32)
    summed = summed + (second[...].astype(F32) + third[...].astype(F32))
    g_query[...] = summed[:, 0:512]
    g_key[...] = summed[:, 512:768]
    g_value[...] = summed[:, 768:1024]
    g_out[...] = summed[:, 1024:1536]
    part = jnp.sum(w_query[...].astype(F32) * summed[:, 0:512], axis=1, keepdims=True)
    part = part + jnp.sum(w_key[...].astype(F32) * summed[:, 512:768], axis=1, keepdims=True)
    part = part + jnp.sum(w_value[...].astype(F32) * summed[:, 768:1024], axis=1, keepdims=True)
    diagonal = lax.broadcasted_iota(jnp.int32, (64, 64), 0) == lax.broadcasted_iota(
        jnp.int32, (64, 64), 1
    )
    column = jnp.sum(jnp.where(diagonal, gain[...].astype(F32), 0.0), axis=1, keepdims=True)
    lane = lax.broadcasted_iota(jnp.int32, (64, 128), 1)
    sums[...] = jnp.where(lane == 35, part / column, summed[:, 1536:1664])


def settle(*args):
    return pl.pallas_call(
        past(settle_kernel, 8, len(args) - 8),
        in_specs=[pl.BlockSpec(memory_space=pltpu.VMEM)] * 8 + [HBM] * (len(args) - 8),
        out_shape=[jax.ShapeDtypeStruct((64, n), F32) for n in (512, 256, 256, 512, 128)],
        compiler_params=pltpu.CompilerParams(vmem_limit_bytes=VMEM),
        cost_estimate=cost(10**6, 2 * 10**6),
        name="settle",
    )(*args)


def join_kernel(where, mine, far, out):
    @pl.when(pl.program_id(0) == 0)
    def _():
        out[...] = mine[...].reshape(2, 4, 1, 32, D)

    @pl.when(pl.program_id(0) == 1)
    def _():
        out[...] = far[...].reshape(2, 4, 1, 32, D)


def join(where, mine, far, *others):
    whole = pl.BlockSpec((HALF, D), lambda i, r: (0, 0))
    return pl.pallas_call(
        past(join_kernel, 3, len(others)),
        grid_spec=pltpu.PrefetchScalarGridSpec(
            num_scalar_prefetch=1,
            grid=(2,),
            in_specs=[whole, whole] + [HBM] * len(others),
            out_specs=pl.BlockSpec(
                (2, 4, 1, 32, D), lambda i, r: (0, 0, jnp.where(i == 0, r[0], 1 - r[0]), 0, 0)
            ),
        ),
        out_shape=jax.ShapeDtypeStruct((2, 4, 2, 32, D), mine.dtype),
        compiler_params=params(1),
        cost_estimate=cost(10**6, 4 * 10**6),
        name="join",
    )(where, mine, far, *others).reshape(2, 256, D)


def ring_pairs(stage, step):
    pairs = []
    for x in range(4):
        for z in range(4):
            for t in range(2):
                if (stage == 0) == (t == 0):
                    far = ((x + step) % 4) * 4 + z
                else:
                    far = x * 4 + (z + step) % 4
                pairs.append(((x * 4 + z) * 2 + t, far * 2 + t))
    return pairs


def ring(value, stage, step):
    return lax.ppermute(value, ("fsdp", "tensor"), ring_pairs(stage, step))


def shift(value, step):
    return lax.ppermute(value, "context", [(i, (i + step) % 4) for i in range(4)])


def swap_cores(value):
    return lax.ppermute(value, "tensor", [(0, 1), (1, 0)])


def gather_row(block, stage=0):
    return block, ring(block, stage, -1), ring(block, stage, 1), ring(block, stage, 2)


def gather_chunks(low, high):
    behind_low, ahead_high = ring(low, 1, 1), ring(high, 1, -1)
    behind_high, ahead_low = ring(high, 1, 1), ring(low, 1, -1)
    far = ring(behind_low, 1, 1), ring(ahead_high, 1, -1)
    return (low, high), (ahead_low, ahead_high), (behind_low, behind_high), far


def scatter_parts(parts, move):
    own, ahead, behind, far = parts
    return own, move(ahead, 1), move(behind, -1), move(far, 2)


def total_of(parts):
    first, second, third, fourth = (p.astype(F32) for p in parts)
    return (first + second) + (third + fourth)


def along(stage):
    return lambda v, n: ring(v, stage, n)


def local(
    tokens, segments, routes, attention_gain, w_query, w_key, w_value, w_out, query_gain,
    key_gain, feedforward_gain, router, w_gate, w_up, w_down, cotangent,
):
    f, c, t = lax.axis_index("fsdp"), lax.axis_index("context"), lax.axis_index("tensor")
    x_at, z_at = f // 4, f % 4
    steps = jnp.array([0, 1, 3, 2], jnp.int32)
    as_row = lambda *v: jnp.stack([jnp.asarray(i, jnp.int32) for i in v])
    all_x, all_z = (x_at + steps) % 4, (z_at + steps) % 4
    order = jnp.where(
        t == 0, all_x[None, :] * 4 + all_z[:, None], all_x[:, None] * 4 + all_z[None, :]
    ).astype(jnp.int32)
    far_x, far_z = steps[(jnp.arange(4) - x_at) % 4], steps[(jnp.arange(4) - z_at) % 4]
    place = jnp.where(
        t == 0, far_x[:, None] + 4 * far_z[None, :], 4 * far_x[:, None] + far_z[None, :]
    )
    place = place.reshape(-1).astype(jnp.int32)
    near = ((c + steps) % 4)[:, None] * 2 + jnp.stack([t, 1 - t])[None, :]
    near = near.reshape(8)

    shard = pack(
        as_row(f), w_query, w_key, w_value, w_out, router.T, attention_gain[None, :],
        feedforward_gain[None, :], query_gain[None, :], key_gain[None, :],
    )
    shards = jnp.stack(gather_row(shard))
    shards = gather_row(shards, 1)

    parity = lambda v, p: lax.dynamic_index_in_dim(
        v.reshape(2, 4, 2, 32, D), p, 2, keepdims=False
    ).reshape(HALF, D)
    tokens_m = parity(tokens, t)
    tokens_all = lax.all_gather(tokens_m, ("context", "tensor"), axis=0)
    picked = routes.reshape(ROWS, TOPK).T
    experts = jnp.arange(EXPERTS, dtype=jnp.int32)
    match = jnp.any(picked[:, None, :] == experts[None, :, None], axis=0)
    before = lambda n: (jnp.arange(n)[:, None] < jnp.arange(n)[None, :]).astype(BF)
    kept = match & (dot(match.astype(BF), before(ROWS)) < CAP)
    half = lambda v: lax.dynamic_index_in_dim(
        v.astype(F32).reshape(EXPERTS, 2, 4, 2, 32), t, 3, keepdims=False
    ).reshape(EXPERTS, HALF)
    match_half, kept_half = half(match), half(kept)
    local_place = dot(kept_half.astype(BF), before(HALF))
    table = experts_to_rows(jnp.where(kept_half > 0, local_place, -1.0).astype(BF))
    cot_payload = pack_cotangent(as_row(t), cotangent, table, *shards[1:])
    cot_row = gather_row(cot_payload)

    experts_w = [lax.all_gather(w, "tensor", axis=0) for w in (w_gate, w_up, w_down)]
    seg = segments.reshape(2, 4, 4, 2, 32).transpose(0, 1, 3, 2, 4).reshape(2, 8, 128)
    seg = jnp.take(seg, near, axis=1).reshape(2, 1, SEQ).astype(F32)

    cosine, sine = (jnp.asarray(v) for v in rotary_tables())
    weights, small, heads, cosine, sine, normed1, k_proj, k_b, v_b, q_proj, q_b = project(
        order.reshape(-1), near.astype(jnp.int32), tokens_all, shards, cosine, sine, seg
    )
    cot_chunks = gather_chunks(*stack_pairs(cot_row, small))
    attended, branch_m, branch_o = attend(q_b, k_b, v_b, seg, weights, cot_chunks[0][0])
    hidden1, payload, probs, totals = route(
        tokens_m, branch_m, swap_cores(branch_o), small, match_half, kept_half,
        *cot_chunks[1], *cot_chunks[2],
    )

    chunks = gather_chunks(*stack_pairs(gather_row(payload), *cot_chunks[3]))
    outs_x, more, counts, carried = {}, [], [], ()
    for slot, i in enumerate((0, 1, 3, 2)):
        where_at = as_row(f // 4, 2 * (f % 4), slot)
        result = expert_chunk(
            order[i], where_at, chunks[i], cot_chunks[i], experts_w, carried
        )
        carried = result[0], *result[2:5]
        outs_x[i] = result[1]
        more += result[5:8]
        counts.append(result[8])
    parts = scatter_parts([outs_x[i] for i in range(4)], along(1))
    grads_e = expert_weights(as_row(t), carried[1:], more, counts, parts[1], parts[3])
    back, grads_e = add_blocks(parts, (grads_e,))
    back = scatter_parts(back, along(0))

    grads_e = lax.psum_scatter(
        grads_e.reshape(8, 2, 256, 768), ("context", "tensor"), scatter_dimension=0
    )
    mixed, grad_hidden, grad_branch, grad_router, grad_gain2 = route_back(
        [carried[0]], *back, cot_payload, hidden1, small, payload, probs, totals, match_half
    )
    mixed = lax.psum_scatter(mixed, "fsdp", scatter_dimension=0)
    branch_far = swap_cores(grad_branch)
    gq, gk, gv, gains = attend_back(
        q_b, q_proj, k_b, k_proj, v_b, seg,
        grad_branch, branch_far, weights, attended, cosine, sine, heads,
    )
    grads_w = weight_grads(
        place, normed1, gq, gk, gv, grad_branch, branch_far, attended, grad_router, grad_gain2, gains,
    )
    gin_m, gin_o = input_grads(gq, gk, gv, weights, grads_w[0])
    (sent,) = add_blocks((gin_m, swap_cores(gin_o)))
    gin = scatter_parts(sent, shift)
    both = lambda v, *others: join(as_row(t), v, swap_cores(v), *others)
    grad_tokens = both(finish(*gin, tokens_m, grad_hidden, small, grads_e))

    grads_w = scatter_parts(grads_w, along(1))
    (grads_w,) = add_blocks(grads_w, (), *sent[1:])
    grads_w = [v[None] for v in scatter_parts(grads_w, along(0))]
    ((grads_w,),) = add_blocks(grads_w, (), *gin[1:])
    summed_w = grads_w
    block_output = both((hidden1 + mixed.astype(F32)).astype(BF), summed_w)
    g_query, g_key, g_value, g_out, sums = settle(
        *scatter_parts([grads_w] * 4, shift), w_query, w_key, w_value, attention_gain[None, :],
        grad_tokens,
    )
    sums = sums + swap_cores(sums)

    grads_e = grads_e.astype(F32)
    return (
        block_output,
        grad_tokens,
        sums[:, 35],
        g_query,
        g_key,
        g_value,
        g_out,
        sums[0:4, 33],
        sums[0:4, 34],
        sums[:, 32],
        sums[:, 0:32],
        grads_e[:, :, 0:256],
        grads_e[:, :, 256:512],
        grads_e[:, :, 512:768],
    )


def solution(mesh):
    in_specs = (
        P("fsdp", "context", None),
        P("fsdp", None),
        P("fsdp", "context", None),
        P("fsdp"),
        P("fsdp", "tensor"),
        P("fsdp", "tensor"),
        P("fsdp", "tensor"),
        P("fsdp", "tensor"),
        P("fsdp"),
        P("fsdp"),
        P("fsdp"),
        P("fsdp", None),
        P("fsdp", None, "tensor"),
        P("fsdp", None, "tensor"),
        P("fsdp", None, "tensor"),
        P("fsdp", "context", None),
    )
    out_specs = (
        P("fsdp", "context", None),
        P("fsdp", "context", None),
        P("fsdp"),
        P("fsdp", "tensor"),
        P("fsdp", "tensor"),
        P("fsdp", "tensor"),
        P("fsdp", "tensor"),
        P("fsdp"),
        P("fsdp"),
        P("fsdp"),
        P("fsdp", None),
        P("fsdp", "context", "tensor"),
        P("fsdp", "context", "tensor"),
        P("fsdp", "context", "tensor"),
    )
    return jax.shard_map(local, mesh=mesh, in_specs=in_specs, out_specs=out_specs, check_vma=False)
```

```python
import functools

import jax
import jax.numpy as jnp
import numpy as np
from jax import lax
from jax.experimental import pallas as pl
from jax.experimental.pallas import tpu as pltpu
from jax.sharding import PartitionSpec as P

HD = 64
EXPERTS = 32
TOPK = 8
SEQ = 1024
D = 1024
ROWS = 512
HALF = 256
CAP = 160
MAIN = 96
TILES = -(-CAP // MAIN)
PAD = 272
N_FSDP = 16
N_CONTEXT = 4
EPS = 1e-06
NEGATIVE = -1e30
VMEM = 62 * 1024 * 1024
BF = jnp.bfloat16
F32 = jnp.float32
NT = (((1,), (1,)), ((), ()))
TN = (((0,), (0,)), ((), ()))


def dot(a, b):
    return jnp.dot(a, b, preferred_element_type=F32)


def dot_nt(a, b):
    return lax.dot_general(a, b, NT, preferred_element_type=F32)


def dot_tn(a, b):
    return lax.dot_general(a, b, TN, preferred_element_type=F32)


def split(v):
    high = v.astype(BF)
    return high, (v - high.astype(F32)).astype(BF)


def params(grid_dims):
    return pltpu.CompilerParams(
        dimension_semantics=("arbitrary",) * grid_dims, vmem_limit_bytes=VMEM
    )


def cost(flops, moved):
    return pl.CostEstimate(flops=flops, bytes_accessed=moved, transcendentals=0)


HBM = pl.BlockSpec(memory_space=pltpu.HBM)


def past(kernel, inputs, others):
    return lambda *refs: kernel(*refs[:inputs], *refs[inputs + others :])


def head_mean(v):
    rows = lax.broadcasted_iota(jnp.int32, (512, 256), 0) % 256 // HD
    cols = lax.broadcasted_iota(jnp.int32, (512, 256), 1) // HD
    block = jnp.where(rows == cols, 1.0, 0.0).astype(BF)
    return dot(jnp.concatenate(split(v), axis=1), block) * (1.0 / HD)


def swap_halves(v):
    lane = lax.broadcasted_iota(jnp.int32, v.shape, 1) % HD
    width = v.shape[1]
    return jnp.where(lane < HD // 2, pltpu.roll(v, width - 32, 1), pltpu.roll(v, 32, 1))


def twice(v):
    return jnp.concatenate([v, v], axis=1)


def rotary_tables():
    middle = HD // 2
    inverse = 10000.0 ** (-(2.0 * np.arange(middle, dtype=np.float64) / HD))
    inverse = inverse.astype(np.float32)
    angles = np.arange(SEQ, dtype=np.float32)[:, None] * inverse[None, :]
    angles = angles.astype(np.float64)
    cosine, sine = np.cos(angles).astype(np.float32), np.sin(angles).astype(np.float32)
    cosine = np.concatenate([cosine] * 4, axis=1)
    sine = np.concatenate([-sine, sine, -sine, sine], axis=1)
    order = lambda v: v.reshape(4, 4, 2, 32, 128).transpose(0, 2, 1, 3, 4).reshape(8, 128, 128)
    return order(cosine), order(sine)


def pack_kernel(where, w_query, w_key, w_value, w_out, router, gain1, gain2, q_gain, k_gain, out):
    out[:, 0:512] = w_query[...]
    out[:, 512:768] = w_key[...]
    out[:, 768:1024] = w_value[...]
    out[:, 1024:1536] = w_out[...]
    diagonal = lax.broadcasted_iota(jnp.int32, (64, 64), 0) == lax.broadcasted_iota(
        jnp.int32, (64, 64), 1
    )
    column = lambda v: jnp.sum(
        jnp.where(diagonal, v[...].astype(F32), 0.0), axis=1, keepdims=True
    )
    row = lax.broadcasted_iota(jnp.int32, (64, 128), 0)
    lane = lax.broadcasted_iota(jnp.int32, (64, 128), 1)
    small = jnp.where(lane == 32, column(gain1), 0.0) + jnp.where(lane == 33, column(gain2), 0.0)
    for i in range(4):
        here = lane == HD + 4 * where[0] + i
        for r, v in enumerate((q_gain, k_gain)):
            small = small + jnp.where(here & (row == r), v[0:1, i : i + 1].astype(F32), 0.0)
    out[:, 1536:1664] = small.astype(BF)
    out[:, 1536:1568] = router[...]


def pack(where, *arrays):
    whole = lambda v: pl.BlockSpec(v.shape, lambda i, r: (0, 0))
    return pl.pallas_call(
        pack_kernel,
        grid_spec=pltpu.PrefetchScalarGridSpec(
            num_scalar_prefetch=1,
            grid=(1,),
            in_specs=[whole(v) for v in arrays],
            out_specs=pl.BlockSpec((64, 1664), lambda i, r: (0, 0)),
        ),
        out_shape=jax.ShapeDtypeStruct((64, 1664), BF),
        compiler_params=params(1),
        cost_estimate=cost(10**6, 10**6),
        name="pack",
    )(where, *arrays)


def stack_pairs(blocks, *others):
    rows, width = blocks[0].shape

    def kernel(a, b, c, d, low, high):
        low[0], low[1] = a[...], b[...]
        high[0], high[1] = c[...], d[...]

    return pl.pallas_call(
        past(kernel, 4, len(others)),
        in_specs=[pl.BlockSpec(memory_space=pltpu.VMEM)] * 4 + [HBM] * len(others),
        out_shape=[jax.ShapeDtypeStruct((2, rows, width), BF)] * 2,
        compiler_params=pltpu.CompilerParams(vmem_limit_bytes=VMEM),
        cost_estimate=cost(10**6, 10**6),
        name="stack_pairs",
    )(*blocks, *others)


def add_blocks(arrays, handed=(), *others):
    blocks, n, k = arrays[0].shape[0], len(arrays), len(handed)

    def kernel(*refs):
        for i, out in enumerate(refs[n + k + len(others) :][:blocks]):
            total = refs[0][i].astype(F32)
            for ref in refs[1:n]:
                total = total + ref[i].astype(F32)
            out[...] = total.astype(BF)

    vmem = pl.BlockSpec(memory_space=pltpu.VMEM)
    out = pl.pallas_call(
        kernel,
        in_specs=[vmem] * n + [HBM] * (k + len(others)),
        out_specs=[vmem] * blocks + [HBM] * k,
        out_shape=[jax.ShapeDtypeStruct(arrays[0].shape[1:], BF)] * blocks
        + [jax.ShapeDtypeStruct(v.shape, v.dtype) for v in handed],
        input_output_aliases={n + i: blocks + i for i in range(k)},
        compiler_params=pltpu.CompilerParams(vmem_limit_bytes=VMEM),
        cost_estimate=cost(10**9, 10**7),
        name="add_blocks",
    )(*arrays, *handed, *others)
    return out[:blocks], *out[blocks:]


def pack_cotangent(where, cotangent, table, *others):
    def kernel(where, rows, table, out):
        out[0:HALF, :] = rows[...].reshape(HALF, D)
        out[HALF:PAD, :] = jnp.concatenate([table[...], jnp.zeros((8, D), BF)], axis=0)

    return pl.pallas_call(
        past(kernel, 3, len(others)),
        grid_spec=pltpu.PrefetchScalarGridSpec(
            num_scalar_prefetch=1,
            grid=(1,),
            in_specs=[
                pl.BlockSpec((2, 4, 1, 32, D), lambda i, r: (0, 0, r[0], 0, 0)),
                pl.BlockSpec((8, D), lambda i, r: (0, 0)),
            ]
            + [HBM] * len(others),
            out_specs=pl.BlockSpec((PAD, D), lambda i, r: (0, 0)),
        ),
        out_shape=jax.ShapeDtypeStruct((PAD, D), BF),
        compiler_params=params(1),
        cost_estimate=cost(10**6, 10**6),
        name="pack_cotangent",
    )(where, cotangent.reshape(2, 4, 2, 32, D), table, *others)


def project_kernel(
    order, near, x0, x1, x2, x3, x4, x5, x6, x7, w0, w1, w2, w3, cos_all, sin_all,
    w, small, heads, cosine, sine, normed, k_proj, k_b, v_b, q_proj, q_b,
):
    @pl.when(pl.program_id(0) == 0)
    def _():
        for i, shards in enumerate((w0, w1, w2, w3)):
            for j in range(4):
                to = pl.ds(pl.multiple_of(order[4 * i + j] * 64, 64), 64)
                w[to, :] = shards[j]
        for i in range(8):
            cosine[i * 128 : i * 128 + 128, :] = cos_all[near[i]]
            sine[i * 128 : i * 128 + 128, :] = sin_all[near[i]]
        last = w[:, 1536:1664].astype(F32)
        small[...] = last.T
        summed = last[0:64]
        for i in range(1, N_FSDP):
            summed = summed + last[i * 64 : i * 64 + 64]
        lane = lax.broadcasted_iota(jnp.int32, (8, 128), 1)
        gains = jnp.where(lane >= HD, summed[0:8], 0.0)
        heads[...] = gains + pltpu.roll(gains, HD, 1)

    gain = small[32:33, :]
    for i, x in enumerate((x0, x1, x2, x3, x4, x5, x6, x7)):
        values = x[0].astype(F32)
        factor = lax.rsqrt(jnp.mean(values * values, axis=1, keepdims=True) + EPS)
        normed[0, i * 128 : i * 128 + 128, :] = (values * factor * gain).astype(BF)
    both = dot(normed[0], w[:, 512:1024])
    keys = both[:, 0:256]
    k_proj[0] = keys
    v_b[0] = both[:, 256:512].astype(BF)
    cos, sin = twice(cosine[...]), twice(sine[...])
    scaled = keys * lax.rsqrt(head_mean(keys * keys) + EPS) * twice(heads[1:2, :])
    k_b[0] = (scaled * cos + swap_halves(scaled) * sin).astype(BF)
    queries = dot(normed[0, 0:256, :], w[:, 0:512])
    q_proj[0] = queries
    for block in range(2):
        at = slice(block * 256, block * 256 + 256)
        head = queries[:, at]
        scaled = head * lax.rsqrt(head_mean(head * head) + EPS) * twice(heads[0:1, :])
        turned = scaled * cos[0:256] + swap_halves(scaled) * sin[0:256]
        q_b[0, :, at] = (turned.astype(BF).astype(F32) * 0.125).astype(BF)


def project(order, near, tokens, shards, cosine, sine, *others):
    row = lambda s, r, n: (0, 0)
    of = lambda s, r, n: (s, 0, 0)
    block = lambda i: pl.BlockSpec((1, 128, D), lambda s, r, n: (n[i], s, 0))
    fixed = ((D, 1664, BF), (128, D, F32), (8, 128, F32), (SEQ, 128, F32), (SEQ, 128, F32))
    shapes = ((SEQ, D, BF), (SEQ, 256, F32), (SEQ, 256, BF), (SEQ, 256, BF), (256, 512, F32), (256, 512, BF))
    return pl.pallas_call(
        past(project_kernel, 16, len(others)),
        grid_spec=pltpu.PrefetchScalarGridSpec(
            num_scalar_prefetch=2,
            grid=(2,),
            in_specs=[block(i) for i in range(8)]
            + [pl.BlockSpec((4, 64, 1664), lambda s, r, n: (0, 0, 0))] * 4
            + [pl.BlockSpec((8, 128, 128), lambda s, r, n: (0, 0, 0))] * 2
            + [HBM] * len(others),
            out_specs=[pl.BlockSpec((r, n), row) for r, n, _ in fixed]
            + [pl.BlockSpec((1, r, n), of) for r, n, _ in shapes],
        ),
        out_shape=[jax.ShapeDtypeStruct((r, n), dt) for r, n, dt in fixed]
        + [jax.ShapeDtypeStruct((2, r, n), dt) for r, n, dt in shapes],
        compiler_params=params(1),
        cost_estimate=cost(10 * 10**9, 20 * 10**6),
        name="project",
    )(order, near, *([tokens] * 8), *shards, cosine, sine, *others)


def as_column(row):
    return jnp.broadcast_to(row, (8, row.shape[1])).T[:, 0:1]


def place_head(v, target, source):
    moved = v if target == source else pltpu.roll(v, HD, 1)
    lane = lax.broadcasted_iota(jnp.int32, v.shape, 1) // HD
    return jnp.where(lane == target, moved, jnp.zeros_like(moved))


def stack_heads(v):
    parts = []
    for block in range(2):
        for j in range(2):
            parts.append(place_head(v[:, block * 128 : block * 128 + 128], block, j))
    return jnp.concatenate(parts, axis=0)


def unstack_heads(v):
    blocks = []
    for block in range(2):
        pair = [v[(2 * block + j) * 256 : (2 * block + j + 1) * 256] for j in range(2)]
        blocks.append(place_head(pair[0], 0, block) + place_head(pair[1], 1, block))
    return jnp.concatenate(blocks, axis=1)


def attend_kernel(q, k, v, seg, w_out, attended, mine, other):
    row = seg[0]
    mask = jnp.where(as_column(row[:, 0:HALF]) == row, 0.0, NEGATIVE)
    queries = stack_heads(q[0].astype(F32)).astype(BF)
    scores = dot_nt(queries, k[0])
    weights = jnp.concatenate(
        [jnp.exp(scores[i * 256 : i * 256 + 256] + mask).astype(BF) for i in range(4)], axis=0
    )
    summed = dot(weights, jnp.concatenate([v[0], jnp.ones((SEQ, 128), BF)], axis=1))
    mixed = unstack_heads(summed[:, :128] / summed[:, 128:]).astype(BF)
    attended[0] = mixed
    part = dot_nt(mixed, w_out[...])

    @pl.when(pl.program_id(1) == 0)
    def _():
        mine[...] = part[0:128]
        other[...] = part[128:256]

    @pl.when(pl.program_id(1) != 0)
    def _():
        mine[...] += part[0:128]
        other[...] += part[128:256]


def attend(q_b, k_b, v_b, seg, w_out, *others):
    half = pl.BlockSpec((128, D), lambda s, p: (s, 0))
    return pl.pallas_call(
        past(attend_kernel, 5, len(others)),
        grid=(2, 2),
        in_specs=[
            pl.BlockSpec((1, HALF, 256), lambda s, p: (s, 0, p)),
            pl.BlockSpec((1, SEQ, 128), lambda s, p: (s, 0, p)),
            pl.BlockSpec((1, SEQ, 128), lambda s, p: (s, 0, p)),
            pl.BlockSpec((1, 1, SEQ), lambda s, p: (s, 0, 0)),
            pl.BlockSpec((D, 256), lambda s, p: (0, 4 + p)),
        ]
        + [HBM] * len(others),
        out_specs=[pl.BlockSpec((1, HALF, 256), lambda s, p: (s, 0, p)), half, half],
        out_shape=[
            jax.ShapeDtypeStruct((2, HALF, 512), BF),
            jax.ShapeDtypeStruct((HALF, D), F32),
            jax.ShapeDtypeStruct((HALF, D), F32),
        ],
        compiler_params=params(2),
        cost_estimate=cost(10 * 10**9, 8 * 10**6),
        name="attend",
    )(q_b, k_b, v_b, seg, w_out, *others)


def experts_to_rows(table):
    return jnp.concatenate([table[8 * k : 8 * k + 8] for k in range(4)], axis=1)


def rows_to_experts(rows):
    return jnp.concatenate([rows[:, 256 * k : 256 * k + 256] for k in range(4)], axis=0)


def route_kernel(tokens, mine, other, small, match, kept, hidden, payload, probs, totals):
    values = tokens[...].astype(F32) + mine[...] + other[...]
    hidden[...] = values
    factor = lax.rsqrt(jnp.mean(values * values, axis=1, keepdims=True) + EPS)
    rows = (values * factor * small[33:34, :]).astype(BF)
    payload[0:HALF, :] = rows
    logits = dot_nt(small[0:32, :].astype(BF), rows)
    raised = jnp.exp(logits - jnp.max(logits, axis=0, keepdims=True))
    prob = raised / jnp.sum(raised, axis=0, keepdims=True)
    probs[...] = prob
    chosen = prob * match[...]
    total = jnp.sum(chosen, axis=0, keepdims=True)
    totals[...] = total
    high, low = split(experts_to_rows(chosen / total * kept[...]))
    payload[HALF:PAD, :] = jnp.concatenate([high, low], axis=0)


def route(*args):
    return pl.pallas_call(
        past(route_kernel, 6, len(args) - 6),
        in_specs=[pl.BlockSpec(memory_space=pltpu.VMEM)] * 6 + [HBM] * (len(args) - 6),
        out_shape=[
            jax.ShapeDtypeStruct((HALF, D), F32),
            jax.ShapeDtypeStruct((PAD, D), BF),
            jax.ShapeDtypeStruct((EXPERTS, HALF), F32),
            jax.ShapeDtypeStruct((1, HALF), F32),
        ],
        compiler_params=pltpu.CompilerParams(vmem_limit_bytes=VMEM),
        cost_estimate=cost(10**8, 5 * 10**6),
        name="route",
    )(*args)


def own_row(table, lane_block, row):
    picked = jnp.zeros((8, 256), F32)
    for k in range(4):
        picked = picked + jnp.where(lane_block == k, table[:, 256 * k : 256 * k + 256], 0.0)
    number = lax.broadcasted_iota(jnp.int32, (8, 256), 0)
    return jnp.sum(jnp.where(number == row, picked, 0.0), axis=0, keepdims=True)


def expert_math(x, g, gate, w):
    pre = dot(x, w[:, 0:1024])
    grad_all = dot(g, w[:, 1024:1536])
    acts, grads, gate_dot = [], [], 0.0
    for part in range(2):
        gate_pre = pre[:, part * 512 : part * 512 + 256]
        up_pre = pre[:, part * 512 + 256 : part * 512 + 512]
        grad = grad_all[:, part * 256 : part * 256 + 256]
        sig = jax.nn.sigmoid(gate_pre)
        swish = gate_pre * sig
        act = (swish * up_pre).astype(BF).astype(F32)
        gate_dot = gate_dot + jnp.sum(act * grad, axis=1, keepdims=True)
        acts.append((act * gate).astype(BF))
        grad = grad * gate
        grads.append((grad * up_pre * sig * (1.0 + gate_pre * (1.0 - sig))).astype(BF))
        grads.append((grad * swish).astype(BF))
    act = jnp.concatenate(acts, axis=1)
    grad = jnp.concatenate(grads, axis=1)
    y = dot_nt(act, w[:, 1024:1536]).astype(BF)
    back = dot_nt(grad, w[:, 0:1024]).astype(BF)
    return y, back, act, grad, gate_dot


def pick_rows(places, first, rows):
    number = lax.broadcasted_iota(jnp.int32, (rows, 256), 0) + first
    return number == places.astype(jnp.int32)


def expert_kernel(order, where_at, x_low, x_high, c_low, c_high, w_gate, w_up, w_down, *refs):
    refs = refs[len(refs) - 25 :]
    out_y, out_x, kept_x, kept_g, kept_h, more_x, more_g, more_h, tiles = refs[:9]
    x_all, c_all, wv, xs, gs, hs, picks, sums, ys, bs, total, places, gate_rows, dots = refs[9:23]
    in_sem, out_sem = refs[23:]
    slot = where_at[2]
    lane_block, row_at = where_at[0], where_at[1]
    copy = pltpu.make_async_copy
    loads = [
        copy(x_low, x_all.at[0:2], in_sem.at[0]),
        copy(c_low, c_all.at[0:2], in_sem.at[1]),
        copy(x_high, x_all.at[2:4], in_sem.at[2]),
        copy(c_high, c_all.at[2:4], in_sem.at[3]),
    ]

    def load_w(e):
        copies = []
        for part in range(2):
            for w, at in ((w_gate, 512 * part), (w_up, 512 * part + 256), (w_down, 1024 + 256 * part)):
                sem = in_sem.at[4 + 2 * len(copies) + e]
                copies.append(copy(w.at[part, e], wv.at[e, :, at : at + 256], sem))
        return copies

    for load in loads + load_w(0) + load_w(1):
        load.start()
    for load in loads:
        load.wait()

    def read(h, carry):
        table = c_all[h, HALF : HALF + 8, :].astype(F32)
        gate_table = x_all[h, HALF:PAD, :].astype(F32)
        gate_table = gate_table[0:8] + gate_table[8:16]
        for e in range(2):
            places[pl.ds(4 * e + h, 1), :] = own_row(table, lane_block, row_at + e)
            gate_rows[pl.ds(4 * e + h, 1), :] = own_row(gate_table, lane_block, row_at + e)
        return carry

    lax.fori_loop(0, 4, read, 0)
    most = jnp.max(places[...]).astype(jnp.int32)
    count = jnp.maximum(most, 0) // MAIN + 1
    tiles[...] = jnp.zeros((8, 128), F32) + count.astype(F32)

    rows = pl.ds(pl.multiple_of(slot * (4 * MAIN), 4 * MAIN), 4 * MAIN)

    def tile(i, carry):
        first = i * MAIN
        more = pl.ds(pl.multiple_of(jnp.maximum(i - 1, 0) * (4 * MAIN), 4 * MAIN), 4 * MAIN)
        sends = lambda e: (
            (xs, kept_x, more_x, e),
            (gs, kept_g, more_g, 2 + e),
            (hs, kept_h, more_h, 4 + e),
        )

        def start(v, kept, other, e, n):
            @pl.when(i == 0)
            def _():
                copy(v.at[e], kept.at[e, rows], out_sem.at[n]).start()

            @pl.when(i > 0)
            def _():
                copy(v.at[e], other.at[e, more], out_sem.at[n]).start()

        def gather(h, carry):
            pick = [
                jnp.where(pick_rows(places[pl.ds(4 * e + h, 1), :], first, MAIN), 1.0, 0.0)
                for e in range(2)
            ]
            pick = jnp.concatenate(pick, axis=0).astype(BF)
            picks[h] = pick
            x = dot(pick, x_all[h, 0:HALF, :]).astype(BF)
            g = dot(pick, c_all[h, 0:HALF, :]).astype(BF)
            to = pl.ds(pl.multiple_of(h * MAIN, MAIN), MAIN)
            for e in range(2):
                xs[e, to, :] = x[e * MAIN : e * MAIN + MAIN]
                gs[e, to, :] = g[e * MAIN : e * MAIN + MAIN]
            return carry

        lax.fori_loop(0, 4, gather, 0)
        for e in range(2):
            start(xs, kept_x, more_x, e, e)
            start(gs, kept_g, more_g, e, 2 + e)

        def math(e, carry):
            here = [pick_rows(places[pl.ds(4 * e + h, 1), :], first, MAIN) for h in range(4)]
            gate = [
                jnp.sum(
                    jnp.where(here[h], gate_rows[pl.ds(4 * e + h, 1), :], 0.0),
                    axis=1,
                    keepdims=True,
                )
                for h in range(4)
            ]

            @pl.when(i == 0)
            def _():
                for load in load_w(e):
                    load.wait()

            y, back, act, grad, gate_dot = expert_math(
                xs[e], gs[e], jnp.concatenate(gate, axis=0), wv.at[e]
            )
            hs[e, :, 0:512] = act
            hs[e, :, 512:1536] = grad
            start(hs, kept_h, more_h, e, 4 + e)
            to = pl.ds(pl.multiple_of(e * MAIN, MAIN), MAIN)
            for h in range(4):
                at = slice(h * MAIN, h * MAIN + MAIN)
                sums[h, to, 0:D] = y[at]
                sums[h, to, D : 2 * D] = back[at]
                spread = jnp.sum(jnp.where(here[h], gate_dot[at], 0.0), axis=0, keepdims=True)
                row = pl.ds(4 * e + h, 1)
                dots[row, :] = jnp.where(i == 0, 0.0, dots[row, :]) + spread
            return carry

        lax.fori_loop(0, 2, math, 0)
        last = i == count - 1

        def scatter(h, carry):
            out = dot_tn(picks[h], sums[h])
            at = pl.ds(pl.multiple_of(h * HALF, HALF), HALF)

            @pl.when(i > 0)
            def _():
                total[at, :] += out

            @pl.when((i == 0) & jnp.logical_not(last))
            def _():
                total[at, :] = out

            @pl.when(last)
            def _():
                @pl.when(i == 0)
                def _():
                    ys[h] = out[:, 0:D].astype(BF)
                    bs[h, 0:HALF, :] = out[:, D : 2 * D].astype(BF)

                @pl.when(i > 0)
                def _():
                    ys[h] = total[at, 0:D].astype(BF)
                    bs[h, 0:HALF, :] = total[at, D : 2 * D].astype(BF)

                row = lax.broadcasted_iota(jnp.int32, (8, 256), 0)
                table = jnp.where(row == row_at, dots[pl.ds(h, 1), :], 0.0)
                table = table + jnp.where(row == row_at + 1, dots[pl.ds(4 + h, 1), :], 0.0)
                table = [jnp.where(lane_block == k, table, 0.0) for k in range(4)]
                high, low = split(jnp.concatenate(table, axis=1))
                bs[h, HALF:PAD, :] = jnp.concatenate([high, low], axis=0)
                copy(bs.at[h], out_x.at[h], out_sem.at[6 + h]).start()
                copy(ys.at[h], out_y.at[order[h]], out_sem.at[10 + h]).start()

            return carry

        lax.fori_loop(0, 4, scatter, 0)
        for e in range(2):
            for v, kept, _, n in sends(e):
                copy(v.at[e], kept.at[e, rows], out_sem.at[n]).wait()
        return carry

    lax.fori_loop(0, count, tile, 0)
    for h in range(4):
        copy(bs.at[h], out_x.at[h], out_sem.at[6 + h]).wait()
        copy(ys.at[h], out_y.at[order[h]], out_sem.at[10 + h]).wait()


def expert_chunk(order, where_at, x, cotangents, weights, kept):
    rows = 4 * MAIN
    widths = (D, D, 1536)
    shape = lambda *v: jax.ShapeDtypeStruct(v, BF)
    vmem = lambda *v: pltpu.VMEM(v, BF)
    aliases = {9: 0, 10: 2, 11: 3, 12: 4} if kept else {}
    return pl.pallas_call(
        expert_kernel,
        grid_spec=pltpu.PrefetchScalarGridSpec(
            num_scalar_prefetch=2,
            grid=(1,),
            in_specs=[HBM] * (7 + len(kept)),
            out_specs=[HBM] * 8 + [pl.BlockSpec((8, 128), lambda i, r, w: (0, 0))],
            scratch_shapes=[
                vmem(4, PAD, D),
                vmem(4, PAD, D),
                vmem(2, D, 1536),
                vmem(2, rows, D),
                vmem(2, rows, D),
                vmem(2, rows, 1536),
                vmem(4, 2 * MAIN, 256),
                vmem(4, 2 * MAIN, 2 * D),
                vmem(4, HALF, D),
                vmem(4, PAD, D),
                pltpu.VMEM((1024, 2 * D), F32),
                pltpu.VMEM((8, 256), F32),
                pltpu.VMEM((8, 256), F32),
                pltpu.VMEM((8, 256), F32),
                pltpu.SemaphoreType.DMA((16,)),
                pltpu.SemaphoreType.DMA((14,)),
            ],
        ),
        out_shape=[shape(N_FSDP, HALF, D), shape(4, PAD, D)]
        + [shape(2, 4 * rows, n) for n in widths]
        + [shape(2, (TILES - 1) * rows, n) for n in widths]
        + [jax.ShapeDtypeStruct((8, 128), F32)],
        input_output_aliases=aliases,
        compiler_params=params(1),
        cost_estimate=cost(14 * 10**9, 30 * 10**6),
        name="experts",
    )(order, where_at, *x, *cotangents, *weights, *kept)


def expert_weight_kernel(place, x, g, act, grad, *refs):
    more, counts, (down, gate_up), (mx, mg, mh) = refs[:12], refs[12:16], refs[-5:-3], refs[-3:]
    out = refs[-6]
    expert, part = pl.program_id(0), pl.program_id(1)
    down[...] = dot_tn(g[0], act[0])
    gate_up[...] = dot_tn(x[0], grad[0])
    for chunk in range(4):
        count = jnp.max(counts[chunk][...]).astype(jnp.int32) - 1

        @pl.when(count > 0)
        def _(chunk=chunk, count=count):
            def piece(i, carry):
                rows = pl.ds(pl.multiple_of(i * 4 * MAIN, 4 * MAIN), 4 * MAIN)
                for ref, to in zip(more[3 * chunk : 3 * chunk + 3], (mx, mg, mh)):
                    pltpu.sync_copy(ref.at[expert, rows], to)
                for p in range(2):

                    @pl.when(part == p)
                    def _(p=p):
                        at = p * 256
                        down[...] += dot_tn(mg[...], mh[:, at : at + 256])
                        at = 512 + p * 512
                        gate_up[...] += dot_tn(mx[...], mh[:, at : at + 512])

                return carry

            lax.fori_loop(0, count, piece, 0)

    for c in range(4):
        at = slice(c * 256, c * 256 + 256)
        out[c, 0, 0, :, 0:512] = gate_up[at, :].astype(BF)
        out[c, 0, 0, :, 512:768] = down[at, :].astype(BF)


def expert_weights(place, kept, more, counts, *others):
    rows = 16 * MAIN
    by_expert = lambda e, p, r: (e, 0, 0)
    return pl.pallas_call(
        expert_weight_kernel,
        grid_spec=pltpu.PrefetchScalarGridSpec(
            num_scalar_prefetch=1,
            grid=(2, 2),
            in_specs=[
                pl.BlockSpec((1, rows, D), by_expert),
                pl.BlockSpec((1, rows, D), by_expert),
                pl.BlockSpec((1, rows, 256), lambda e, p, r: (e, 0, p)),
                pl.BlockSpec((1, rows, 512), lambda e, p, r: (e, 0, 1 + p)),
            ]
            + [HBM] * 12
            + [pl.BlockSpec((8, 128), lambda e, p, r: (0, 0))] * 4
            + [HBM] * len(others),
            out_specs=pl.BlockSpec(
                (4, 1, 1, 256, 768),
                lambda e, p, r: (0, p, e, 0, 0),
            ),
            scratch_shapes=[
                pltpu.VMEM((D, 256), F32),
                pltpu.VMEM((D, 512), F32),
                pltpu.VMEM((4 * MAIN, D), BF),
                pltpu.VMEM((4 * MAIN, D), BF),
                pltpu.VMEM((4 * MAIN, 1536), BF),
            ],
        ),
        out_shape=jax.ShapeDtypeStruct((4, 2, 2, 256, 768), BF),
        compiler_params=params(2),
        cost_estimate=cost(20 * 10**9, 30 * 10**6),
        name="expert_weights",
    )(place, kept[0], kept[1], kept[2], kept[2], *more, *counts, *others)


def route_back_kernel(
    own, first, second, third, cotangent, hidden, small, normed, probs, totals, match,
    grad_hidden, grad_branch, grad_router, grad_gain,
):
    summed = own[...].astype(F32) + first[...].astype(F32)
    summed = summed + (second[...].astype(F32) + third[...].astype(F32))
    tables = summed[HALF:PAD, :]
    grad_gates = rows_to_experts(tables[0:8] + tables[8:16])
    prob, total = probs[...], totals[...]
    chosen = prob * match[...]
    shared = jnp.sum(grad_gates * chosen, axis=0, keepdims=True) / (total * total)
    grad_prob = (grad_gates / total - shared) * match[...]
    grad_logits = prob * (grad_prob - jnp.sum(prob * grad_prob, axis=0, keepdims=True))
    high, low = split(grad_logits)
    grad_router[...] = dot(high, normed[0:HALF, :]) + dot(low, normed[0:HALF, :])
    router = small[0:32, :].astype(BF)
    grad_normed = summed[0:HALF, :] + dot_tn(high, router) + dot_tn(low, router)
    values = hidden[...]
    factor = lax.rsqrt(jnp.mean(values * values, axis=1, keepdims=True) + EPS)
    grad_gain[...] = jnp.sum(grad_normed * values * factor, axis=0, keepdims=True)
    weighted = grad_normed * small[33:34, :]
    mean = jnp.mean(weighted * values, axis=1, keepdims=True)
    grad = cotangent[0:HALF, :].astype(F32) + factor * weighted - values * (factor * factor * factor * mean)
    grad_hidden[...] = grad
    grad_branch[...] = grad.astype(BF)


def route_back(handed, *args):
    n, others, shapes = len(handed), len(args) - 11, [jax.ShapeDtypeStruct(v.shape, v.dtype) for v in handed]
    vmem = pl.BlockSpec(memory_space=pltpu.VMEM)
    kernel = past(route_back_kernel, 11, others + n)
    return pl.pallas_call(
        lambda *refs: kernel(*refs[n:]),
        in_specs=[HBM] * n + [vmem] * 11 + [HBM] * others,
        out_specs=[HBM] * n + [vmem] * 4,
        input_output_aliases={i: i for i in range(n)},
        out_shape=shapes
        + [
            jax.ShapeDtypeStruct((HALF, D), F32),
            jax.ShapeDtypeStruct((HALF, D), BF),
            jax.ShapeDtypeStruct((EXPERTS, D), F32),
            jax.ShapeDtypeStruct((1, D), F32),
        ],
        compiler_params=pltpu.CompilerParams(vmem_limit_bytes=VMEM),
        cost_estimate=cost(10**6, 10**6),
        name="route_back",
    )(*handed, *args)


def norm_back_heads(grad, proj, gain, cosine, sine):
    turned = grad * cosine - swap_halves(grad) * sine
    factor = lax.rsqrt(head_mean(proj * proj) + EPS)
    weighted = turned * gain
    mean = head_mean(weighted * proj)
    back = factor * weighted - proj * (factor * factor * factor * mean)
    return back, jnp.sum(turned * proj * factor, axis=0, keepdims=True)


def attend_back_kernel(
    q, q_proj, k, k_proj, v, seg, branch_m, branch_o, w_out, attended,
    cosine, sine, heads, grad_q, grad_k, grad_v, gains,
):
    row = seg[0]
    mask = jnp.where(as_column(row) == row[:, 0:HALF], 0.0, NEGATIVE)
    keys, values = k[0], v[0]
    grad_branch = jnp.concatenate([branch_m[...], branch_o[...]], axis=0)
    grad_mixed = dot(grad_branch, w_out[...]).astype(BF).astype(F32)
    queries = stack_heads(q[0].astype(F32)).astype(BF)
    grads = stack_heads(grad_mixed).astype(BF)
    high, low = split(stack_heads(attended[0].astype(F32) * grad_mixed))
    ones = jnp.ones((8, 256), BF)
    row_dot = dot_nt(ones, jnp.concatenate([high, low], axis=1))[0:1]
    scores = dot_nt(keys, queries)
    grad_probs = dot_nt(values, grads)
    probs_b, grad_scores = [], []
    for i in range(4):
        at = slice(i * 256, i * 256 + 256)
        raised = jnp.exp(scores[:, at] + mask)
        probs = raised * (1.0 / jnp.sum(raised, axis=0, keepdims=True))
        probs_b.append(probs.astype(BF))
        grad_scores.append((probs * (grad_probs[:, at] - row_dot[:, at])).astype(BF))
    probs_b = jnp.concatenate(probs_b, axis=1)
    grad_scores = jnp.concatenate(grad_scores, axis=1)
    grad_v[0] = dot(probs_b, grads).astype(BF)
    sum_k = dot(grad_scores, queries)
    sum_q = unstack_heads(dot_tn(grad_scores, keys) * 0.125)
    cos, sin = cosine[...], sine[...]
    back, gain_q = norm_back_heads(
        sum_q, q_proj[0], twice(heads[0:1, :]), twice(cos[0:256]), twice(sin[0:256])
    )
    grad_q[0] = back.astype(BF)
    wide = lambda value: jnp.concatenate([value[0:512], value[512:1024]], axis=1)
    back, gain_k = norm_back_heads(
        wide(sum_k), wide(k_proj[0]), twice(heads[1:2, :]), wide(cos), wide(sin)
    )
    grad_k[0, 0:512, :] = back[:, 0:128].astype(BF)
    grad_k[0, 512:1024, :] = back[:, 128:256].astype(BF)
    part = jnp.concatenate([gain_q, gain_k, jnp.zeros((6, 256), F32)], axis=0)

    @pl.when((pl.program_id(0) == 0) & (pl.program_id(1) == 0))
    def _():
        gains[...] = part

    @pl.when((pl.program_id(0) != 0) | (pl.program_id(1) != 0))
    def _():
        gains[...] += part


def attend_back(
    q_b, q_proj, k_b, k_proj, v_b, seg, branch_m, branch_o, w_out, attended,
    cosine, sine, heads,
):
    queries = pl.BlockSpec((1, HALF, 256), lambda s, p: (s, 0, p))
    keys = pl.BlockSpec((1, SEQ, 128), lambda s, p: (s, 0, p))
    table = pl.BlockSpec((SEQ, 128), lambda s, p: (0, 0))
    gain = pl.BlockSpec((8, 128), lambda s, p: (0, 0))
    half = pl.BlockSpec((128, D), lambda s, p: (s, 0))
    return pl.pallas_call(
        attend_back_kernel,
        grid=(2, 2),
        in_specs=[
            queries, queries, keys, keys, keys,
            pl.BlockSpec((1, 1, SEQ), lambda s, p: (s, 0, 0)),
            half, half,
            pl.BlockSpec((D, 256), lambda s, p: (0, 4 + p)),
            queries, table, table, gain,
        ],
        out_specs=[queries, keys, keys, pl.BlockSpec((8, 256), lambda s, p: (0, 0))],
        out_shape=[
            jax.ShapeDtypeStruct((2, HALF, 512), BF),
            jax.ShapeDtypeStruct((2, SEQ, 256), BF),
            jax.ShapeDtypeStruct((2, SEQ, 256), BF),
            jax.ShapeDtypeStruct((8, 256), F32),
        ],
        compiler_params=params(2),
        cost_estimate=cost(10**6, 10**6),
        name="attend_back",
    )(
        q_b, q_proj, k_b, k_proj, v_b, seg, branch_m, branch_o, w_out, attended,
        cosine, sine, heads,
    )


def weight_grads_kernel(
    place, normed, gq, gk, gv, branch_m, branch_o, mixed, router, gain, head_gains,
    out_0, out_1, out_2, out_3, out, sem,
):
    step = pl.program_id(0)
    rows = jnp.concatenate([normed[0], normed[1]], axis=0)
    own = jnp.concatenate([normed[0, 0:256, :], normed[1, 0:256, :]], axis=0)
    keys = jnp.concatenate(
        [
            jnp.concatenate([gk[0], gk[1]], axis=0),
            jnp.concatenate([gv[0], gv[1]], axis=0),
        ],
        axis=1,
    )
    queries = jnp.concatenate([gq[0], gq[1]], axis=0)
    branch = jnp.concatenate(
        [branch_m[0:128], branch_o[0:128], branch_m[128:256], branch_o[128:256]], axis=0
    )
    heads = jnp.concatenate([mixed[0], mixed[1]], axis=0)
    at = lax.broadcasted_iota(jnp.int32, (256, 256), 1)
    share = 4 * (at // HD + 4 * step) + at % HD
    spread = (lax.broadcasted_iota(jnp.int32, (256, 256), 0) % HD == share) & (at % HD < 4)
    spread = jnp.where(spread, 1.0, 0.0).astype(BF)
    high, low = split(head_gains[...])
    spread = dot(high, spread) + dot(low, spread)
    row = lax.broadcasted_iota(jnp.int32, (8, 256), 0)
    last = jnp.where(row == 0, gain[...], 0.0)
    last = last + jnp.where(row == 1, spread[0:1], 0.0) + jnp.where(row == 2, spread[1:2], 0.0)
    small = jnp.concatenate([router[...], last, jnp.zeros((88, 256), F32)], axis=0)
    parts = (
        (0, 512, dot_tn(own, queries).astype(BF)),
        (512, 1024, dot_tn(rows, keys).astype(BF)),
        (1024, 1536, dot_tn(branch, heads).astype(BF)),
        (1536, 1664, small.T.astype(BF)),
    )
    for i in range(4):
        to = place[4 * step + i]
        for low, high, value in parts:
            out[to, :, low:high] = value[i * 64 : i * 64 + 64]

    @pl.when(step == 3)
    def _():
        sends = [
            pltpu.make_async_copy(out.at[4 * i : 4 * i + 4], to, sem.at[i])
            for i, to in enumerate((out_0, out_1, out_2, out_3))
        ]
        for send in sends:
            send.start()
        for send in sends:
            send.wait()


def weight_grads(place, *args):
    fixed = lambda i, r: (0, 0, 0)
    column = pl.BlockSpec((HALF, 256), lambda i, r: (0, i))
    return pl.pallas_call(
        past(weight_grads_kernel, 11, len(args) - 10),
        grid_spec=pltpu.PrefetchScalarGridSpec(
            num_scalar_prefetch=1,
            grid=(4,),
            in_specs=[
                pl.BlockSpec((2, SEQ, 256), lambda i, r: (0, 0, i)),
                pl.BlockSpec((2, HALF, 512), fixed),
                pl.BlockSpec((2, SEQ, 256), fixed),
                pl.BlockSpec((2, SEQ, 256), fixed),
                column,
                column,
                pl.BlockSpec((2, HALF, 512), fixed),
                pl.BlockSpec((EXPERTS, 256), lambda i, r: (0, i)),
                pl.BlockSpec((1, 256), lambda i, r: (0, i)),
                pl.BlockSpec((8, 256), lambda i, r: (0, 0)),
            ]
            + [HBM] * (len(args) - 10),
            out_specs=[HBM] * 4,
            scratch_shapes=[pltpu.VMEM((N_FSDP, 64, 1664), BF), pltpu.SemaphoreType.DMA((4,))],
        ),
        out_shape=[jax.ShapeDtypeStruct((4, 64, 1664), BF)] * 4,
        compiler_params=params(1),
        cost_estimate=cost(10**6, 10**6),
        name="weight_grads",
    )(place, *args)


def input_grads_kernel(gq, gk, gv, w, mine, other):
    part = dot_nt(jnp.concatenate([gk[0], gv[0]], axis=1), w[:, 512:1024])
    own = dot_nt(gq[0], w[:, 0:512])
    for c in range(4):
        for parity, out in enumerate((mine, other)):
            at = slice(c * 256 + parity * 128, c * 256 + parity * 128 + 128)
            value = part[at] + own[at] if c == 0 else part[at]
            out[c] = value.astype(BF)


def input_grads(gq, gk, gv, weights, *others):
    by = lambda s: (s, 0, 0)
    half = pl.BlockSpec((4, 128, D), lambda s: (0, s, 0))
    return pl.pallas_call(
        past(input_grads_kernel, 4, len(others)),
        grid=(2,),
        in_specs=[
            pl.BlockSpec((1, HALF, 512), by),
            pl.BlockSpec((1, SEQ, 256), by),
            pl.BlockSpec((1, SEQ, 256), by),
            pl.BlockSpec((D, 1024), lambda s: (0, 0)),
        ]
        + [HBM] * len(others),
        out_specs=[half, half],
        out_shape=[jax.ShapeDtypeStruct((4, HALF, D), BF)] * 2,
        compiler_params=params(1),
        cost_estimate=cost(10**6, 10**6),
        name="input_grads",
    )(gq, gk, gv, weights, *others)


def finish_kernel(own, first, second, third, tokens, grad_hidden, small, out):
    values = tokens[...].astype(F32)
    factor = lax.rsqrt(jnp.mean(values * values, axis=1, keepdims=True) + EPS)
    summed = own[...].astype(F32) + first[...].astype(F32)
    summed = summed + (second[...].astype(F32) + third[...].astype(F32))
    weighted = summed * small[32:33, :]
    mean = jnp.mean(weighted * values, axis=1, keepdims=True)
    out[...] = grad_hidden[...] + factor * weighted - values * (factor * factor * factor * mean)


def finish(*args):
    return pl.pallas_call(
        past(finish_kernel, 7, len(args) - 7),
        in_specs=[pl.BlockSpec(memory_space=pltpu.VMEM)] * 7 + [HBM] * (len(args) - 7),
        out_shape=jax.ShapeDtypeStruct((HALF, D), F32),
        compiler_params=pltpu.CompilerParams(vmem_limit_bytes=VMEM),
        cost_estimate=cost(10**7, 6 * 10**6),
        name="finish",
    )(*args)


def settle_kernel(
    own, first, second, third, w_query, w_key, w_value, gain, g_query, g_key, g_value, g_out, sums
):
    summed = own[...].astype(F32) + first[...].astype(F32)
    summed = summed + (second[...].astype(F32) + third[...].astype(F32))
    g_query[...] = summed[:, 0:512]
    g_key[...] = summed[:, 512:768]
    g_value[...] = summed[:, 768:1024]
    g_out[...] = summed[:, 1024:1536]
    part = jnp.sum(w_query[...].astype(F32) * summed[:, 0:512], axis=1, keepdims=True)
    part = part + jnp.sum(w_key[...].astype(F32) * summed[:, 512:768], axis=1, keepdims=True)
    part = part + jnp.sum(w_value[...].astype(F32) * summed[:, 768:1024], axis=1, keepdims=True)
    diagonal = lax.broadcasted_iota(jnp.int32, (64, 64), 0) == lax.broadcasted_iota(
        jnp.int32, (64, 64), 1
    )
    column = jnp.sum(jnp.where(diagonal, gain[...].astype(F32), 0.0), axis=1, keepdims=True)
    lane = lax.broadcasted_iota(jnp.int32, (64, 128), 1)
    sums[...] = jnp.where(lane == 35, part / column, summed[:, 1536:1664])


def settle(*args):
    return pl.pallas_call(
        past(settle_kernel, 8, len(args) - 8),
        in_specs=[pl.BlockSpec(memory_space=pltpu.VMEM)] * 8 + [HBM] * (len(args) - 8),
        out_shape=[jax.ShapeDtypeStruct((64, n), F32) for n in (512, 256, 256, 512, 128)],
        compiler_params=pltpu.CompilerParams(vmem_limit_bytes=VMEM),
        cost_estimate=cost(10**6, 2 * 10**6),
        name="settle",
    )(*args)


def join_kernel(where, mine, far, out):
    @pl.when(pl.program_id(0) == 0)
    def _():
        out[...] = mine[...].reshape(2, 4, 1, 32, D)

    @pl.when(pl.program_id(0) == 1)
    def _():
        out[...] = far[...].reshape(2, 4, 1, 32, D)


def join(where, mine, far, *others):
    whole = pl.BlockSpec((HALF, D), lambda i, r: (0, 0))
    return pl.pallas_call(
        past(join_kernel, 3, len(others)),
        grid_spec=pltpu.PrefetchScalarGridSpec(
            num_scalar_prefetch=1,
            grid=(2,),
            in_specs=[whole, whole] + [HBM] * len(others),
            out_specs=pl.BlockSpec(
                (2, 4, 1, 32, D), lambda i, r: (0, 0, jnp.where(i == 0, r[0], 1 - r[0]), 0, 0)
            ),
        ),
        out_shape=jax.ShapeDtypeStruct((2, 4, 2, 32, D), mine.dtype),
        compiler_params=params(1),
        cost_estimate=cost(10**6, 4 * 10**6),
        name="join",
    )(where, mine, far, *others).reshape(2, 256, D)


def ring_pairs(stage, step):
    pairs = []
    for x in range(4):
        for z in range(4):
            for t in range(2):
                if (stage == 0) == (t == 0):
                    far = ((x + step) % 4) * 4 + z
                else:
                    far = x * 4 + (z + step) % 4
                pairs.append(((x * 4 + z) * 2 + t, far * 2 + t))
    return pairs


def ring(value, stage, step):
    return lax.ppermute(value, ("fsdp", "tensor"), ring_pairs(stage, step))


def shift(value, step):
    return lax.ppermute(value, "context", [(i, (i + step) % 4) for i in range(4)])


def swap_cores(value):
    return lax.ppermute(value, "tensor", [(0, 1), (1, 0)])


def gather_row(block, stage=0):
    return block, ring(block, stage, -1), ring(block, stage, 1), ring(block, stage, 2)


def gather_chunks(low, high):
    behind_low, ahead_high = ring(low, 1, 1), ring(high, 1, -1)
    behind_high, ahead_low = ring(high, 1, 1), ring(low, 1, -1)
    far = ring(behind_low, 1, 1), ring(ahead_high, 1, -1)
    return (low, high), (ahead_low, ahead_high), (behind_low, behind_high), far


def scatter_parts(parts, move):
    own, ahead, behind, far = parts
    return own, move(ahead, 1), move(behind, -1), move(far, 2)


def total_of(parts):
    first, second, third, fourth = (p.astype(F32) for p in parts)
    return (first + second) + (third + fourth)


def along(stage):
    return lambda v, n: ring(v, stage, n)


def local(
    tokens, segments, routes, attention_gain, w_query, w_key, w_value, w_out, query_gain,
    key_gain, feedforward_gain, router, w_gate, w_up, w_down, cotangent,
):
    f, c, t = lax.axis_index("fsdp"), lax.axis_index("context"), lax.axis_index("tensor")
    x_at, z_at = f // 4, f % 4
    steps = jnp.array([0, 1, 3, 2], jnp.int32)
    as_row = lambda *v: jnp.stack([jnp.asarray(i, jnp.int32) for i in v])
    all_x, all_z = (x_at + steps) % 4, (z_at + steps) % 4
    order = jnp.where(
        t == 0, all_x[None, :] * 4 + all_z[:, None], all_x[:, None] * 4 + all_z[None, :]
    ).astype(jnp.int32)
    far_x, far_z = steps[(jnp.arange(4) - x_at) % 4], steps[(jnp.arange(4) - z_at) % 4]
    place = jnp.where(
        t == 0, far_x[:, None] + 4 * far_z[None, :], 4 * far_x[:, None] + far_z[None, :]
    )
    place = place.reshape(-1).astype(jnp.int32)
    near = ((c + steps) % 4)[:, None] * 2 + jnp.stack([t, 1 - t])[None, :]
    near = near.reshape(8)

    shard = pack(
        as_row(f), w_query, w_key, w_value, w_out, router, attention_gain[None, :],
        feedforward_gain[None, :], query_gain[None, :], key_gain[None, :],
    )
    shards = jnp.stack(gather_row(shard))
    shards = gather_row(shards, 1)

    parity = lambda v, p: lax.dynamic_index_in_dim(
        v.reshape(2, 4, 2, 32, D), p, 2, keepdims=False
    ).reshape(HALF, D)
    tokens_m = parity(tokens, t)
    tokens_all = lax.all_gather(tokens_m, ("context", "tensor"), axis=0)
    picked = routes.reshape(ROWS, TOPK).T
    experts = jnp.arange(EXPERTS, dtype=jnp.int32)
    match = jnp.any(picked[:, None, :] == experts[None, :, None], axis=0)
    before = lambda n: (jnp.arange(n)[:, None] < jnp.arange(n)[None, :]).astype(BF)
    kept = match & (dot(match.astype(BF), before(ROWS)) < CAP)
    half = lambda v: lax.dynamic_index_in_dim(
        v.astype(F32).reshape(EXPERTS, 2, 4, 2, 32), t, 3, keepdims=False
    ).reshape(EXPERTS, HALF)
    match_half, kept_half = half(match), half(kept)
    local_place = dot(kept_half.astype(BF), before(HALF))
    table = experts_to_rows(jnp.where(kept_half > 0, local_place, -1.0).astype(BF))
    cot_payload = pack_cotangent(as_row(t), cotangent, table, *shards[1:])
    cot_row = gather_row(cot_payload)

    experts_w = [lax.all_gather(w, "tensor", axis=0) for w in (w_gate, w_up, w_down)]
    seg = segments.reshape(2, 4, 4, 2, 32).transpose(0, 1, 3, 2, 4).reshape(2, 8, 128)
    seg = jnp.take(seg, near, axis=1).reshape(2, 1, SEQ).astype(F32)

    cosine, sine = (jnp.asarray(v) for v in rotary_tables())
    weights, small, heads, cosine, sine, normed1, k_proj, k_b, v_b, q_proj, q_b = project(
        order.reshape(-1), near.astype(jnp.int32), tokens_all, shards, cosine, sine, seg
    )
    cot_chunks = gather_chunks(*stack_pairs(cot_row, small))
    attended, branch_m, branch_o = attend(q_b, k_b, v_b, seg, weights, cot_chunks[0][0])
    hidden1, payload, probs, totals = route(
        tokens_m, branch_m, swap_cores(branch_o), small, match_half, kept_half,
        *cot_chunks[1], *cot_chunks[2],
    )

    chunks = gather_chunks(*stack_pairs(gather_row(payload), *cot_chunks[3]))
    outs_x, more, counts, carried = {}, [], [], ()
    for slot, i in enumerate((0, 1, 3, 2)):
        where_at = as_row(f // 4, 2 * (f % 4), slot)
        result = expert_chunk(
            order[i], where_at, chunks[i], cot_chunks[i], experts_w, carried
        )
        carried = result[0], *result[2:5]
        outs_x[i] = result[1]
        more += result[5:8]
        counts.append(result[8])
    parts = scatter_parts([outs_x[i] for i in range(4)], along(1))
    grads_e = expert_weights(as_row(t), carried[1:], more, counts, parts[1], parts[3])
    back, grads_e = add_blocks(parts, (grads_e,))
    back = scatter_parts(back, along(0))

    grads_e = lax.psum_scatter(
        grads_e.reshape(8, 2, 256, 768), ("context", "tensor"), scatter_dimension=0
    )
    mixed, grad_hidden, grad_branch, grad_router, grad_gain2 = route_back(
        [carried[0]], *back, cot_payload, hidden1, small, payload, probs, totals, match_half
    )
    mixed = lax.psum_scatter(mixed, "fsdp", scatter_dimension=0)
    branch_far = swap_cores(grad_branch)
    gq, gk, gv, gains = attend_back(
        q_b, q_proj, k_b, k_proj, v_b, seg,
        grad_branch, branch_far, weights, attended, cosine, sine, heads,
    )
    gin_m, gin_o = input_grads(gq, gk, gv, weights)
    grads_w = weight_grads(
        place, normed1, gq, gk, gv, grad_branch, branch_far, attended, grad_router, grad_gain2, gains,
        gin_o, grads_e,
    )
    gin_far = swap_cores(gin_o)
    sent = [(gin_m[i].astype(F32) + gin_far[i].astype(F32)).astype(BF) for i in range(4)]
    gin = scatter_parts(sent, shift)
    both = lambda v, *others: join(as_row(t), v, swap_cores(v), *others)
    grad_tokens = both(finish(*gin, tokens_m, grad_hidden, small))

    grads_w = scatter_parts(grads_w, along(1))
    (grads_w,) = add_blocks(grads_w)
    grads_w = [v[None] for v in scatter_parts(grads_w, along(0))]
    ((grads_w,),) = add_blocks(grads_w)
    g_query, g_key, g_value, g_out, sums = settle(
        *scatter_parts([grads_w] * 4, shift), w_query, w_key, w_value, attention_gain[None, :],
    )
    sums = sums + swap_cores(sums)

    block_half = (hidden1 + mixed.astype(F32)).astype(BF)
    grads_e = grads_e.astype(F32)
    return (
        both(block_half),
        grad_tokens,
        sums[:, 35],
        g_query,
        g_key,
        g_value,
        g_out,
        sums[0:4, 33],
        sums[0:4, 34],
        sums[:, 32],
        sums[:, 0:32],
        grads_e[:, :, 0:256],
        grads_e[:, :, 256:512],
        grads_e[:, :, 512:768],
    )


def solution(mesh):
    in_specs = (
        P("fsdp", "context", None),
        P("fsdp", None),
        P("fsdp", "context", None),
        P("fsdp"),
        P("fsdp", "tensor"),
        P("fsdp", "tensor"),
        P("fsdp", "tensor"),
        P("fsdp", "tensor"),
        P("fsdp"),
        P("fsdp"),
        P("fsdp"),
        P("fsdp", None),
        P("fsdp", None, "tensor"),
        P("fsdp", None, "tensor"),
        P("fsdp", None, "tensor"),
        P("fsdp", "context", None),
    )
    out_specs = (
        P("fsdp", "context", None),
        P("fsdp", "context", None),
        P("fsdp"),
        P("fsdp", "tensor"),
        P("fsdp", "tensor"),
        P("fsdp", "tensor"),
        P("fsdp", "tensor"),
        P("fsdp"),
        P("fsdp"),
        P("fsdp"),
        P("fsdp", None),
        P("fsdp", "context", "tensor"),
        P("fsdp", "context", "tensor"),
        P("fsdp", "context", "tensor"),
    )
    return jax.shard_map(local, mesh=mesh, in_specs=in_specs, out_specs=out_specs, check_vma=False)
```

```python
import functools

import jax
import jax.numpy as jnp
import numpy as np
from jax import lax
from jax.experimental import pallas as pl
from jax.experimental.pallas import tpu as pltpu
from jax.sharding import PartitionSpec as P

HD = 64
EXPERTS = 32
TOPK = 8
SEQ = 1024
D = 1024
ROWS = 512
HALF = 256
CAP = 160
MAIN = 96
TILES = -(-CAP // MAIN)
PAD = 272
N_FSDP = 16
N_CONTEXT = 4
EPS = 1e-06
NEGATIVE = -1e30
VMEM = 62 * 1024 * 1024
BF = jnp.bfloat16
F32 = jnp.float32
NT = (((1,), (1,)), ((), ()))
TN = (((0,), (0,)), ((), ()))


def dot(a, b):
    return jnp.dot(a, b, preferred_element_type=F32)


def dot_nt(a, b):
    return lax.dot_general(a, b, NT, preferred_element_type=F32)


def dot_tn(a, b):
    return lax.dot_general(a, b, TN, preferred_element_type=F32)


def split(v):
    high = v.astype(BF)
    return high, (v - high.astype(F32)).astype(BF)


def params(grid_dims):
    return pltpu.CompilerParams(
        dimension_semantics=("arbitrary",) * grid_dims, vmem_limit_bytes=VMEM
    )


def cost(flops, moved):
    return pl.CostEstimate(flops=flops, bytes_accessed=moved, transcendentals=0)


HBM = pl.BlockSpec(memory_space=pltpu.HBM)


def past(kernel, inputs, others):
    return lambda *refs: kernel(*refs[:inputs], *refs[inputs + others :])


def head_mean(v):
    rows = lax.broadcasted_iota(jnp.int32, (512, 256), 0) % 256 // HD
    cols = lax.broadcasted_iota(jnp.int32, (512, 256), 1) // HD
    block = jnp.where(rows == cols, 1.0, 0.0).astype(BF)
    return dot(jnp.concatenate(split(v), axis=1), block) * (1.0 / HD)


def swap_halves(v):
    lane = lax.broadcasted_iota(jnp.int32, v.shape, 1) % HD
    width = v.shape[1]
    return jnp.where(lane < HD // 2, pltpu.roll(v, width - 32, 1), pltpu.roll(v, 32, 1))


def twice(v):
    return jnp.concatenate([v, v], axis=1)


def rotary_tables():
    middle = HD // 2
    inverse = 10000.0 ** (-(2.0 * np.arange(middle, dtype=np.float64) / HD))
    inverse = inverse.astype(np.float32)
    angles = np.arange(SEQ, dtype=np.float32)[:, None] * inverse[None, :]
    angles = angles.astype(np.float64)
    cosine, sine = np.cos(angles).astype(np.float32), np.sin(angles).astype(np.float32)
    cosine = np.concatenate([cosine] * 4, axis=1)
    sine = np.concatenate([-sine, sine, -sine, sine], axis=1)
    order = lambda v: v.reshape(4, 4, 2, 32, 128).transpose(0, 2, 1, 3, 4).reshape(8, 128, 128)
    return order(cosine), order(sine)


def pack_kernel(where, w_query, w_key, w_value, w_out, router, gain1, gain2, q_gain, k_gain, out):
    out[:, 0:512] = w_query[...]
    out[:, 512:768] = w_key[...]
    out[:, 768:1024] = w_value[...]
    out[:, 1024:1536] = w_out[...]
    diagonal = lax.broadcasted_iota(jnp.int32, (64, 64), 0) == lax.broadcasted_iota(
        jnp.int32, (64, 64), 1
    )
    column = lambda v: jnp.sum(
        jnp.where(diagonal, v[...].astype(F32), 0.0), axis=1, keepdims=True
    )
    row = lax.broadcasted_iota(jnp.int32, (64, 128), 0)
    lane = lax.broadcasted_iota(jnp.int32, (64, 128), 1)
    small = jnp.where(lane == 32, column(gain1), 0.0) + jnp.where(lane == 33, column(gain2), 0.0)
    for i in range(4):
        here = lane == HD + 4 * where[0] + i
        for r, v in enumerate((q_gain, k_gain)):
            small = small + jnp.where(here & (row == r), v[0:1, i : i + 1].astype(F32), 0.0)
    lanes = lax.broadcasted_iota(jnp.int32, (EXPERTS, 128), 1)
    rows = lax.broadcasted_iota(jnp.int32, (EXPERTS, 128), 0)
    small = small + dot_tn(router[...], jnp.where(lanes == rows, 1.0, 0.0).astype(BF))
    out[:, 1536:1664] = small.astype(BF)


def pack(where, *arrays):
    whole = lambda v: pl.BlockSpec(v.shape, lambda i, r: (0, 0))
    return pl.pallas_call(
        pack_kernel,
        grid_spec=pltpu.PrefetchScalarGridSpec(
            num_scalar_prefetch=1,
            grid=(1,),
            in_specs=[whole(v) for v in arrays],
            out_specs=pl.BlockSpec((64, 1664), lambda i, r: (0, 0)),
        ),
        out_shape=jax.ShapeDtypeStruct((64, 1664), BF),
        compiler_params=params(1),
        cost_estimate=cost(10**6, 10**6),
        name="pack",
    )(where, *arrays)


def stack_pairs(blocks, *others):
    rows, width = blocks[0].shape

    def kernel(*refs):
        low, high, held, load_sem, send_sem = refs[4 + len(others) :]
        loads = [
            pltpu.make_async_copy(refs[i], held.at[i], load_sem.at[i]) for i in range(4)
        ]
        sends = [
            pltpu.make_async_copy(held.at[2 * i : 2 * i + 2], out, send_sem.at[i])
            for i, out in enumerate((low, high))
        ]
        for load in loads:
            load.start()
        for i in range(2):
            loads[2 * i].wait()
            loads[2 * i + 1].wait()
            sends[i].start()
        for send in sends:
            send.wait()

    return pl.pallas_call(
        kernel,
        in_specs=[HBM] * (4 + len(others)),
        out_specs=[HBM] * 2,
        out_shape=[jax.ShapeDtypeStruct((2, rows, width), BF)] * 2,
        scratch_shapes=[
            pltpu.VMEM((4, rows, width), BF),
            pltpu.SemaphoreType.DMA((4,)),
            pltpu.SemaphoreType.DMA((2,)),
        ],
        compiler_params=pltpu.CompilerParams(vmem_limit_bytes=VMEM),
        cost_estimate=cost(10**6, 10**6),
        name="stack_pairs",
    )(*blocks, *others)


def add_blocks(arrays, handed=(), *others):
    blocks, n, k = arrays[0].shape[0], len(arrays), len(handed)

    def kernel(*refs):
        for i, out in enumerate(refs[n + k + len(others) :][:blocks]):
            total = refs[0][i].astype(F32)
            for ref in refs[1:n]:
                total = total + ref[i].astype(F32)
            out[...] = total.astype(BF)

    vmem = pl.BlockSpec(memory_space=pltpu.VMEM)
    out = pl.pallas_call(
        kernel,
        in_specs=[vmem] * n + [HBM] * (k + len(others)),
        out_specs=[vmem] * blocks + [HBM] * k,
        out_shape=[jax.ShapeDtypeStruct(arrays[0].shape[1:], BF)] * blocks
        + [jax.ShapeDtypeStruct(v.shape, v.dtype) for v in handed],
        input_output_aliases={n + i: blocks + i for i in range(k)},
        compiler_params=pltpu.CompilerParams(vmem_limit_bytes=VMEM),
        cost_estimate=cost(10**9, 10**7),
        name="add_blocks",
    )(*arrays, *handed, *others)
    return out[:blocks], *out[blocks:]


def pack_cotangent(where, cotangent, table, *others):
    def kernel(where, rows, table, out):
        out[0:HALF, :] = rows[...].reshape(HALF, D)
        out[HALF:PAD, :] = jnp.concatenate([table[...], jnp.zeros((8, D), BF)], axis=0)

    return pl.pallas_call(
        past(kernel, 3, len(others)),
        grid_spec=pltpu.PrefetchScalarGridSpec(
            num_scalar_prefetch=1,
            grid=(1,),
            in_specs=[
                pl.BlockSpec((2, 4, 1, 32, D), lambda i, r: (0, 0, r[0], 0, 0)),
                pl.BlockSpec((8, D), lambda i, r: (0, 0)),
            ]
            + [HBM] * len(others),
            out_specs=pl.BlockSpec((PAD, D), lambda i, r: (0, 0)),
        ),
        out_shape=jax.ShapeDtypeStruct((PAD, D), BF),
        compiler_params=params(1),
        cost_estimate=cost(10**6, 10**6),
        name="pack_cotangent",
    )(where, cotangent.reshape(2, 4, 2, 32, D), table, *others)


def project_kernel(
    order, near, x0, x1, x2, x3, x4, x5, x6, x7, w0, w1, w2, w3, cos_all, sin_all,
    w, small, heads, cosine, sine, normed, k_proj, k_b, v_b, q_proj, q_b,
):
    @pl.when(pl.program_id(0) == 0)
    def _():
        for i, shards in enumerate((w0, w1, w2, w3)):
            for j in range(4):
                to = pl.ds(pl.multiple_of(order[4 * i + j] * 64, 64), 64)
                w[to, :] = shards[j]
        for i in range(8):
            cosine[i * 128 : i * 128 + 128, :] = cos_all[near[i]]
            sine[i * 128 : i * 128 + 128, :] = sin_all[near[i]]
        last = w[:, 1536:1664].astype(F32)
        small[...] = last.T
        summed = last[0:64]
        for i in range(1, N_FSDP):
            summed = summed + last[i * 64 : i * 64 + 64]
        lane = lax.broadcasted_iota(jnp.int32, (8, 128), 1)
        gains = jnp.where(lane >= HD, summed[0:8], 0.0)
        heads[...] = gains + pltpu.roll(gains, HD, 1)

    gain = small[32:33, :]
    for i, x in enumerate((x0, x1, x2, x3, x4, x5, x6, x7)):
        values = x[0].astype(F32)
        factor = lax.rsqrt(jnp.mean(values * values, axis=1, keepdims=True) + EPS)
        normed[0, i * 128 : i * 128 + 128, :] = (values * factor * gain).astype(BF)
    both = dot(normed[0], w[:, 512:1024])
    keys = both[:, 0:256]
    k_proj[0] = keys
    v_b[0] = both[:, 256:512].astype(BF)
    cos, sin = twice(cosine[...]), twice(sine[...])
    scaled = keys * lax.rsqrt(head_mean(keys * keys) + EPS) * twice(heads[1:2, :])
    k_b[0] = (scaled * cos + swap_halves(scaled) * sin).astype(BF)
    queries = dot(normed[0, 0:256, :], w[:, 0:512])
    q_proj[0] = queries
    for block in range(2):
        at = slice(block * 256, block * 256 + 256)
        head = queries[:, at]
        scaled = head * lax.rsqrt(head_mean(head * head) + EPS) * twice(heads[0:1, :])
        turned = scaled * cos[0:256] + swap_halves(scaled) * sin[0:256]
        q_b[0, :, at] = (turned.astype(BF).astype(F32) * 0.125).astype(BF)


def project(order, near, tokens, shards, cosine, sine, *others):
    row = lambda s, r, n: (0, 0)
    of = lambda s, r, n: (s, 0, 0)
    block = lambda i: pl.BlockSpec((1, 128, D), lambda s, r, n: (n[i], s, 0))
    fixed = ((D, 1664, BF), (128, D, F32), (8, 128, F32), (SEQ, 128, F32), (SEQ, 128, F32))
    shapes = ((SEQ, D, BF), (SEQ, 256, F32), (SEQ, 256, BF), (SEQ, 256, BF), (256, 512, F32), (256, 512, BF))
    return pl.pallas_call(
        past(project_kernel, 16, len(others)),
        grid_spec=pltpu.PrefetchScalarGridSpec(
            num_scalar_prefetch=2,
            grid=(2,),
            in_specs=[block(i) for i in range(8)]
            + [pl.BlockSpec((4, 64, 1664), lambda s, r, n: (0, 0, 0))] * 4
            + [pl.BlockSpec((8, 128, 128), lambda s, r, n: (0, 0, 0))] * 2
            + [HBM] * len(others),
            out_specs=[pl.BlockSpec((r, n), row) for r, n, _ in fixed]
            + [pl.BlockSpec((1, r, n), of) for r, n, _ in shapes],
        ),
        out_shape=[jax.ShapeDtypeStruct((r, n), dt) for r, n, dt in fixed]
        + [jax.ShapeDtypeStruct((2, r, n), dt) for r, n, dt in shapes],
        compiler_params=params(1),
        cost_estimate=cost(10 * 10**9, 20 * 10**6),
        name="project",
    )(order, near, *([tokens] * 8), *shards, cosine, sine, *others)


def as_column(row):
    return jnp.broadcast_to(row, (8, row.shape[1])).T[:, 0:1]


def place_head(v, target, source):
    moved = v if target == source else pltpu.roll(v, HD, 1)
    lane = lax.broadcasted_iota(jnp.int32, v.shape, 1) // HD
    return jnp.where(lane == target, moved, jnp.zeros_like(moved))


def stack_heads(v):
    parts = []
    for block in range(2):
        for j in range(2):
            parts.append(place_head(v[:, block * 128 : block * 128 + 128], block, j))
    return jnp.concatenate(parts, axis=0)


def unstack_heads(v):
    blocks = []
    for block in range(2):
        pair = [v[(2 * block + j) * 256 : (2 * block + j + 1) * 256] for j in range(2)]
        blocks.append(place_head(pair[0], 0, block) + place_head(pair[1], 1, block))
    return jnp.concatenate(blocks, axis=1)


def attend_kernel(q, k, v, seg, w_out, attended, mine, other):
    row = seg[0]
    mask = jnp.where(as_column(row[:, 0:HALF]) == row, 0.0, NEGATIVE)
    queries = stack_heads(q[0].astype(F32)).astype(BF)
    scores = dot_nt(queries, k[0])
    weights = jnp.concatenate(
        [jnp.exp(scores[i * 256 : i * 256 + 256] + mask).astype(BF) for i in range(4)], axis=0
    )
    summed = dot(weights, jnp.concatenate([v[0], jnp.ones((SEQ, 128), BF)], axis=1))
    mixed = unstack_heads(summed[:, :128] / summed[:, 128:]).astype(BF)
    attended[0] = mixed
    part = dot_nt(mixed, w_out[...])

    @pl.when(pl.program_id(1) == 0)
    def _():
        mine[...] = part[0:128]
        other[...] = part[128:256]

    @pl.when(pl.program_id(1) != 0)
    def _():
        mine[...] += part[0:128]
        other[...] += part[128:256]


def attend(q_b, k_b, v_b, seg, w_out, *others):
    half = pl.BlockSpec((128, D), lambda s, p: (s, 0))
    return pl.pallas_call(
        past(attend_kernel, 5, len(others)),
        grid=(2, 2),
        in_specs=[
            pl.BlockSpec((1, HALF, 256), lambda s, p: (s, 0, p)),
            pl.BlockSpec((1, SEQ, 128), lambda s, p: (s, 0, p)),
            pl.BlockSpec((1, SEQ, 128), lambda s, p: (s, 0, p)),
            pl.BlockSpec((1, 1, SEQ), lambda s, p: (s, 0, 0)),
            pl.BlockSpec((D, 256), lambda s, p: (0, 4 + p)),
        ]
        + [HBM] * len(others),
        out_specs=[pl.BlockSpec((1, HALF, 256), lambda s, p: (s, 0, p)), half, half],
        out_shape=[
            jax.ShapeDtypeStruct((2, HALF, 512), BF),
            jax.ShapeDtypeStruct((HALF, D), F32),
            jax.ShapeDtypeStruct((HALF, D), F32),
        ],
        compiler_params=params(2),
        cost_estimate=cost(10 * 10**9, 8 * 10**6),
        name="attend",
    )(q_b, k_b, v_b, seg, w_out, *others)


def experts_to_rows(table):
    return jnp.concatenate([table[8 * k : 8 * k + 8] for k in range(4)], axis=1)


def rows_to_experts(rows):
    return jnp.concatenate([rows[:, 256 * k : 256 * k + 256] for k in range(4)], axis=0)


def route_kernel(tokens, mine, other, small, match, kept, hidden, payload, probs, totals):
    values = tokens[...].astype(F32) + mine[...] + other[...]
    hidden[...] = values
    factor = lax.rsqrt(jnp.mean(values * values, axis=1, keepdims=True) + EPS)
    rows = (values * factor * small[33:34, :]).astype(BF)
    payload[0:HALF, :] = rows
    logits = dot_nt(small[0:32, :].astype(BF), rows)
    raised = jnp.exp(logits - jnp.max(logits, axis=0, keepdims=True))
    prob = raised / jnp.sum(raised, axis=0, keepdims=True)
    probs[...] = prob
    chosen = prob * match[...]
    total = jnp.sum(chosen, axis=0, keepdims=True)
    totals[...] = total
    high, low = split(experts_to_rows(chosen / total * kept[...]))
    payload[HALF:PAD, :] = jnp.concatenate([high, low], axis=0)


def route(*args):
    return pl.pallas_call(
        past(route_kernel, 6, len(args) - 6),
        in_specs=[pl.BlockSpec(memory_space=pltpu.VMEM)] * 6 + [HBM] * (len(args) - 6),
        out_shape=[
            jax.ShapeDtypeStruct((HALF, D), F32),
            jax.ShapeDtypeStruct((PAD, D), BF),
            jax.ShapeDtypeStruct((EXPERTS, HALF), F32),
            jax.ShapeDtypeStruct((1, HALF), F32),
        ],
        compiler_params=pltpu.CompilerParams(vmem_limit_bytes=VMEM),
        cost_estimate=cost(10**8, 5 * 10**6),
        name="route",
    )(*args)


def own_row(table, lane_block, row):
    picked = jnp.zeros((8, 256), F32)
    for k in range(4):
        picked = picked + jnp.where(lane_block == k, table[:, 256 * k : 256 * k + 256], 0.0)
    number = lax.broadcasted_iota(jnp.int32, (8, 256), 0)
    return jnp.sum(jnp.where(number == row, picked, 0.0), axis=0, keepdims=True)


def expert_math(x, g, gate, w):
    pre = dot(x, w[:, 0:1024])
    grad_all = dot(g, w[:, 1024:1536])
    acts, grads, gate_dot = [], [], 0.0
    for part in range(2):
        gate_pre = pre[:, part * 512 : part * 512 + 256]
        up_pre = pre[:, part * 512 + 256 : part * 512 + 512]
        grad = grad_all[:, part * 256 : part * 256 + 256]
        sig = jax.nn.sigmoid(gate_pre)
        swish = gate_pre * sig
        act = (swish * up_pre).astype(BF).astype(F32)
        gate_dot = gate_dot + jnp.sum(act * grad, axis=1, keepdims=True)
        acts.append((act * gate).astype(BF))
        grad = grad * gate
        grads.append((grad * up_pre * sig * (1.0 + gate_pre * (1.0 - sig))).astype(BF))
        grads.append((grad * swish).astype(BF))
    act = jnp.concatenate(acts, axis=1)
    grad = jnp.concatenate(grads, axis=1)
    y = dot_nt(act, w[:, 1024:1536]).astype(BF)
    back = dot_nt(grad, w[:, 0:1024]).astype(BF)
    return y, back, act, grad, gate_dot


def pick_rows(places, first, rows):
    number = lax.broadcasted_iota(jnp.int32, (rows, 256), 0) + first
    return number == places.astype(jnp.int32)


def expert_kernel(order, where_at, x_low, x_high, c_low, c_high, w_gate, w_up, w_down, *refs):
    refs = refs[len(refs) - 25 :]
    out_y, out_x, kept_x, kept_g, kept_h, more_x, more_g, more_h, tiles = refs[:9]
    x_all, c_all, wv, xs, gs, hs, picks, sums, ys, bs, total, places, gate_rows, dots = refs[9:23]
    in_sem, out_sem = refs[23:]
    slot = where_at[2]
    lane_block, row_at = where_at[0], where_at[1]
    copy = pltpu.make_async_copy
    loads = [
        copy(x_low, x_all.at[0:2], in_sem.at[0]),
        copy(c_low, c_all.at[0:2], in_sem.at[1]),
        copy(x_high, x_all.at[2:4], in_sem.at[2]),
        copy(c_high, c_all.at[2:4], in_sem.at[3]),
    ]

    def load_w(e):
        copies = []
        for part in range(2):
            for w, at in ((w_gate, 512 * part), (w_up, 512 * part + 256), (w_down, 1024 + 256 * part)):
                sem = in_sem.at[4 + 2 * len(copies) + e]
                copies.append(copy(w.at[part, e], wv.at[e, :, at : at + 256], sem))
        return copies

    for load in loads + load_w(0) + load_w(1):
        load.start()
    for load in loads:
        load.wait()

    def read(h, carry):
        table = c_all[h, HALF : HALF + 8, :].astype(F32)
        gate_table = x_all[h, HALF:PAD, :].astype(F32)
        gate_table = gate_table[0:8] + gate_table[8:16]
        for e in range(2):
            places[pl.ds(4 * e + h, 1), :] = own_row(table, lane_block, row_at + e)
            gate_rows[pl.ds(4 * e + h, 1), :] = own_row(gate_table, lane_block, row_at + e)
        return carry

    lax.fori_loop(0, 4, read, 0)
    most = jnp.max(places[...]).astype(jnp.int32)
    count = jnp.maximum(most, 0) // MAIN + 1
    tiles[...] = jnp.zeros((8, 128), F32) + count.astype(F32)

    rows = pl.ds(pl.multiple_of(slot * (4 * MAIN), 4 * MAIN), 4 * MAIN)

    def tile(i, carry):
        first = i * MAIN
        more = pl.ds(pl.multiple_of(jnp.maximum(i - 1, 0) * (4 * MAIN), 4 * MAIN), 4 * MAIN)
        sends = lambda e: (
            (xs, kept_x, more_x, e),
            (gs, kept_g, more_g, 2 + e),
            (hs, kept_h, more_h, 4 + e),
        )

        def start(v, kept, other, e, n):
            @pl.when(i == 0)
            def _():
                copy(v.at[e], kept.at[e, rows], out_sem.at[n]).start()

            @pl.when(i > 0)
            def _():
                copy(v.at[e], other.at[e, more], out_sem.at[n]).start()

        def gather(h, carry):
            pick = [
                jnp.where(pick_rows(places[pl.ds(4 * e + h, 1), :], first, MAIN), 1.0, 0.0)
                for e in range(2)
            ]
            pick = jnp.concatenate(pick, axis=0).astype(BF)
            picks[h] = pick
            x = dot(pick, x_all[h, 0:HALF, :]).astype(BF)
            g = dot(pick, c_all[h, 0:HALF, :]).astype(BF)
            to = pl.ds(pl.multiple_of(h * MAIN, MAIN), MAIN)
            for e in range(2):
                xs[e, to, :] = x[e * MAIN : e * MAIN + MAIN]
                gs[e, to, :] = g[e * MAIN : e * MAIN + MAIN]
            return carry

        lax.fori_loop(0, 4, gather, 0)
        for e in range(2):
            start(xs, kept_x, more_x, e, e)
            start(gs, kept_g, more_g, e, 2 + e)

        def math(e, carry):
            here = [pick_rows(places[pl.ds(4 * e + h, 1), :], first, MAIN) for h in range(4)]
            gate = [
                jnp.sum(
                    jnp.where(here[h], gate_rows[pl.ds(4 * e + h, 1), :], 0.0),
                    axis=1,
                    keepdims=True,
                )
                for h in range(4)
            ]

            @pl.when(i == 0)
            def _():
                for load in load_w(e):
                    load.wait()

            y, back, act, grad, gate_dot = expert_math(
                xs[e], gs[e], jnp.concatenate(gate, axis=0), wv.at[e]
            )
            hs[e, :, 0:512] = act
            hs[e, :, 512:1536] = grad
            start(hs, kept_h, more_h, e, 4 + e)
            to = pl.ds(pl.multiple_of(e * MAIN, MAIN), MAIN)
            for h in range(4):
                at = slice(h * MAIN, h * MAIN + MAIN)
                sums[h, to, 0:D] = y[at]
                sums[h, to, D : 2 * D] = back[at]
                spread = jnp.sum(jnp.where(here[h], gate_dot[at], 0.0), axis=0, keepdims=True)
                row = pl.ds(4 * e + h, 1)
                dots[row, :] = jnp.where(i == 0, 0.0, dots[row, :]) + spread
            return carry

        lax.fori_loop(0, 2, math, 0)
        last = i == count - 1

        def scatter(h, carry):
            out = dot_tn(picks[h], sums[h])
            at = pl.ds(pl.multiple_of(h * HALF, HALF), HALF)

            @pl.when(i > 0)
            def _():
                total[at, :] += out

            @pl.when((i == 0) & jnp.logical_not(last))
            def _():
                total[at, :] = out

            @pl.when(last)
            def _():
                @pl.when(i == 0)
                def _():
                    ys[h] = out[:, 0:D].astype(BF)
                    bs[h, 0:HALF, :] = out[:, D : 2 * D].astype(BF)

                @pl.when(i > 0)
                def _():
                    ys[h] = total[at, 0:D].astype(BF)
                    bs[h, 0:HALF, :] = total[at, D : 2 * D].astype(BF)

                row = lax.broadcasted_iota(jnp.int32, (8, 256), 0)
                table = jnp.where(row == row_at, dots[pl.ds(h, 1), :], 0.0)
                table = table + jnp.where(row == row_at + 1, dots[pl.ds(4 + h, 1), :], 0.0)
                table = [jnp.where(lane_block == k, table, 0.0) for k in range(4)]
                high, low = split(jnp.concatenate(table, axis=1))
                bs[h, HALF:PAD, :] = jnp.concatenate([high, low], axis=0)
                copy(bs.at[h], out_x.at[h], out_sem.at[6 + h]).start()
                copy(ys.at[h], out_y.at[order[h]], out_sem.at[10 + h]).start()

            return carry

        lax.fori_loop(0, 4, scatter, 0)
        for e in range(2):
            for v, kept, _, n in sends(e):
                copy(v.at[e], kept.at[e, rows], out_sem.at[n]).wait()
        return carry

    lax.fori_loop(0, count, tile, 0)
    for h in range(4):
        copy(bs.at[h], out_x.at[h], out_sem.at[6 + h]).wait()
        copy(ys.at[h], out_y.at[order[h]], out_sem.at[10 + h]).wait()


def expert_chunk(order, where_at, x, cotangents, weights, kept):
    rows = 4 * MAIN
    widths = (D, D, 1536)
    shape = lambda *v: jax.ShapeDtypeStruct(v, BF)
    vmem = lambda *v: pltpu.VMEM(v, BF)
    aliases = {9: 0, 10: 2, 11: 3, 12: 4} if kept else {}
    return pl.pallas_call(
        expert_kernel,
        grid_spec=pltpu.PrefetchScalarGridSpec(
            num_scalar_prefetch=2,
            grid=(1,),
            in_specs=[HBM] * (7 + len(kept)),
            out_specs=[HBM] * 8 + [pl.BlockSpec((8, 128), lambda i, r, w: (0, 0))],
            scratch_shapes=[
                vmem(4, PAD, D),
                vmem(4, PAD, D),
                vmem(2, D, 1536),
                vmem(2, rows, D),
                vmem(2, rows, D),
                vmem(2, rows, 1536),
                vmem(4, 2 * MAIN, 256),
                vmem(4, 2 * MAIN, 2 * D),
                vmem(4, HALF, D),
                vmem(4, PAD, D),
                pltpu.VMEM((1024, 2 * D), F32),
                pltpu.VMEM((8, 256), F32),
                pltpu.VMEM((8, 256), F32),
                pltpu.VMEM((8, 256), F32),
                pltpu.SemaphoreType.DMA((16,)),
                pltpu.SemaphoreType.DMA((14,)),
            ],
        ),
        out_shape=[shape(N_FSDP, HALF, D), shape(4, PAD, D)]
        + [shape(2, 4 * rows, n) for n in widths]
        + [shape(2, (TILES - 1) * rows, n) for n in widths]
        + [jax.ShapeDtypeStruct((8, 128), F32)],
        input_output_aliases=aliases,
        compiler_params=params(1),
        cost_estimate=cost(14 * 10**9, 30 * 10**6),
        name="experts",
    )(order, where_at, *x, *cotangents, *weights, *kept)


def expert_weight_kernel(place, x, g, act, grad, *refs):
    more, counts, (down, gate_up), (mx, mg, mh) = refs[:12], refs[12:16], refs[-5:-3], refs[-3:]
    out = refs[-6]
    expert, part = pl.program_id(0), pl.program_id(1)
    down[...] = dot_tn(g[0], act[0])
    gate_up[...] = dot_tn(x[0], grad[0])
    for chunk in range(4):
        count = jnp.max(counts[chunk][...]).astype(jnp.int32) - 1

        @pl.when(count > 0)
        def _(chunk=chunk, count=count):
            def piece(i, carry):
                rows = pl.ds(pl.multiple_of(i * 4 * MAIN, 4 * MAIN), 4 * MAIN)
                for ref, to in zip(more[3 * chunk : 3 * chunk + 3], (mx, mg, mh)):
                    pltpu.sync_copy(ref.at[expert, rows], to)
                for p in range(2):

                    @pl.when(part == p)
                    def _(p=p):
                        at = p * 256
                        down[...] += dot_tn(mg[...], mh[:, at : at + 256])
                        at = 512 + p * 512
                        gate_up[...] += dot_tn(mx[...], mh[:, at : at + 512])

                return carry

            lax.fori_loop(0, count, piece, 0)

    for c in range(4):
        at = slice(c * 256, c * 256 + 256)
        out[c, 0, 0, :, 0:512] = gate_up[at, :].astype(BF)
        out[c, 0, 0, :, 512:768] = down[at, :].astype(BF)


def expert_weights(place, kept, more, counts, *others):
    rows = 16 * MAIN
    by_expert = lambda e, p, r: (e, 0, 0)
    return pl.pallas_call(
        expert_weight_kernel,
        grid_spec=pltpu.PrefetchScalarGridSpec(
            num_scalar_prefetch=1,
            grid=(2, 2),
            in_specs=[
                pl.BlockSpec((1, rows, D), by_expert),
                pl.BlockSpec((1, rows, D), by_expert),
                pl.BlockSpec((1, rows, 256), lambda e, p, r: (e, 0, p)),
                pl.BlockSpec((1, rows, 512), lambda e, p, r: (e, 0, 1 + p)),
            ]
            + [HBM] * 12
            + [pl.BlockSpec((8, 128), lambda e, p, r: (0, 0))] * 4
            + [HBM] * len(others),
            out_specs=pl.BlockSpec(
                (4, 1, 1, 256, 768),
                lambda e, p, r: (0, p, e, 0, 0),
            ),
            scratch_shapes=[
                pltpu.VMEM((D, 256), F32),
                pltpu.VMEM((D, 512), F32),
                pltpu.VMEM((4 * MAIN, D), BF),
                pltpu.VMEM((4 * MAIN, D), BF),
                pltpu.VMEM((4 * MAIN, 1536), BF),
            ],
        ),
        out_shape=jax.ShapeDtypeStruct((4, 2, 2, 256, 768), BF),
        compiler_params=params(2),
        cost_estimate=cost(20 * 10**9, 30 * 10**6),
        name="expert_weights",
    )(place, kept[0], kept[1], kept[2], kept[2], *more, *counts, *others)


def route_back_kernel(
    own, first, second, third, cotangent, hidden, small, normed, probs, totals, match,
    grad_hidden, grad_branch, grad_router, grad_gain,
):
    summed = own[...].astype(F32) + first[...].astype(F32)
    summed = summed + (second[...].astype(F32) + third[...].astype(F32))
    tables = summed[HALF:PAD, :]
    grad_gates = rows_to_experts(tables[0:8] + tables[8:16])
    prob, total = probs[...], totals[...]
    chosen = prob * match[...]
    shared = jnp.sum(grad_gates * chosen, axis=0, keepdims=True) / (total * total)
    grad_prob = (grad_gates / total - shared) * match[...]
    grad_logits = prob * (grad_prob - jnp.sum(prob * grad_prob, axis=0, keepdims=True))
    high, low = split(grad_logits)
    grad_router[...] = dot(high, normed[0:HALF, :]) + dot(low, normed[0:HALF, :])
    router = small[0:32, :].astype(BF)
    grad_normed = summed[0:HALF, :] + dot_tn(high, router) + dot_tn(low, router)
    values = hidden[...]
    factor = lax.rsqrt(jnp.mean(values * values, axis=1, keepdims=True) + EPS)
    grad_gain[...] = jnp.sum(grad_normed * values * factor, axis=0, keepdims=True)
    weighted = grad_normed * small[33:34, :]
    mean = jnp.mean(weighted * values, axis=1, keepdims=True)
    grad = cotangent[0:HALF, :].astype(F32) + factor * weighted - values * (factor * factor * factor * mean)
    grad_hidden[...] = grad
    grad_branch[...] = grad.astype(BF)


def route_back(handed, *args):
    n, others, shapes = len(handed), len(args) - 11, [jax.ShapeDtypeStruct(v.shape, v.dtype) for v in handed]
    vmem = pl.BlockSpec(memory_space=pltpu.VMEM)
    kernel = past(route_back_kernel, 11, others + n)
    return pl.pallas_call(
        lambda *refs: kernel(*refs[n:]),
        in_specs=[HBM] * n + [vmem] * 11 + [HBM] * others,
        out_specs=[HBM] * n + [vmem] * 4,
        input_output_aliases={i: i for i in range(n)},
        out_shape=shapes
        + [
            jax.ShapeDtypeStruct((HALF, D), F32),
            jax.ShapeDtypeStruct((HALF, D), BF),
            jax.ShapeDtypeStruct((EXPERTS, D), F32),
            jax.ShapeDtypeStruct((1, D), F32),
        ],
        compiler_params=pltpu.CompilerParams(vmem_limit_bytes=VMEM),
        cost_estimate=cost(10**6, 10**6),
        name="route_back",
    )(*handed, *args)


def norm_back_heads(grad, proj, gain, cosine, sine):
    turned = grad * cosine - swap_halves(grad) * sine
    factor = lax.rsqrt(head_mean(proj * proj) + EPS)
    weighted = turned * gain
    mean = head_mean(weighted * proj)
    back = factor * weighted - proj * (factor * factor * factor * mean)
    return back, jnp.sum(turned * proj * factor, axis=0, keepdims=True)


def attend_back_kernel(
    q, q_proj, k, k_proj, v, seg, branch_m, branch_o, w_out, attended,
    cosine, sine, heads, grad_q, grad_k, grad_v, gains,
):
    row = seg[0]
    mask = jnp.where(as_column(row) == row[:, 0:HALF], 0.0, NEGATIVE)
    keys, values = k[0], v[0]
    grad_branch = jnp.concatenate([branch_m[...], branch_o[...]], axis=0)
    grad_mixed = dot(grad_branch, w_out[...]).astype(BF).astype(F32)
    queries = stack_heads(q[0].astype(F32)).astype(BF)
    grads = stack_heads(grad_mixed).astype(BF)
    high, low = split(stack_heads(attended[0].astype(F32) * grad_mixed))
    ones = jnp.ones((8, 256), BF)
    row_dot = dot_nt(ones, jnp.concatenate([high, low], axis=1))[0:1]
    scores = dot_nt(keys, queries)
    grad_probs = dot_nt(values, grads)
    probs_b, grad_scores = [], []
    for i in range(4):
        at = slice(i * 256, i * 256 + 256)
        raised = jnp.exp(scores[:, at] + mask)
        probs = raised * (1.0 / jnp.sum(raised, axis=0, keepdims=True))
        probs_b.append(probs.astype(BF))
        grad_scores.append((probs * (grad_probs[:, at] - row_dot[:, at])).astype(BF))
    probs_b = jnp.concatenate(probs_b, axis=1)
    grad_scores = jnp.concatenate(grad_scores, axis=1)
    grad_v[0] = dot(probs_b, grads).astype(BF)
    sum_k = dot(grad_scores, queries)
    sum_q = unstack_heads(dot_tn(grad_scores, keys) * 0.125)
    cos, sin = cosine[...], sine[...]
    back, gain_q = norm_back_heads(
        sum_q, q_proj[0], twice(heads[0:1, :]), twice(cos[0:256]), twice(sin[0:256])
    )
    grad_q[0] = back.astype(BF)
    wide = lambda value: jnp.concatenate([value[0:512], value[512:1024]], axis=1)
    back, gain_k = norm_back_heads(
        wide(sum_k), wide(k_proj[0]), twice(heads[1:2, :]), wide(cos), wide(sin)
    )
    grad_k[0, 0:512, :] = back[:, 0:128].astype(BF)
    grad_k[0, 512:1024, :] = back[:, 128:256].astype(BF)
    part = jnp.concatenate([gain_q, gain_k, jnp.zeros((6, 256), F32)], axis=0)

    @pl.when((pl.program_id(0) == 0) & (pl.program_id(1) == 0))
    def _():
        gains[...] = part

    @pl.when((pl.program_id(0) != 0) | (pl.program_id(1) != 0))
    def _():
        gains[...] += part


def attend_back(
    q_b, q_proj, k_b, k_proj, v_b, seg, branch_m, branch_o, w_out, attended,
    cosine, sine, heads,
):
    queries = pl.BlockSpec((1, HALF, 256), lambda s, p: (s, 0, p))
    keys = pl.BlockSpec((1, SEQ, 128), lambda s, p: (s, 0, p))
    table = pl.BlockSpec((SEQ, 128), lambda s, p: (0, 0))
    gain = pl.BlockSpec((8, 128), lambda s, p: (0, 0))
    half = pl.BlockSpec((128, D), lambda s, p: (s, 0))
    return pl.pallas_call(
        attend_back_kernel,
        grid=(2, 2),
        in_specs=[
            queries, queries, keys, keys, keys,
            pl.BlockSpec((1, 1, SEQ), lambda s, p: (s, 0, 0)),
            half, half,
            pl.BlockSpec((D, 256), lambda s, p: (0, 4 + p)),
            queries, table, table, gain,
        ],
        out_specs=[queries, keys, keys, pl.BlockSpec((8, 256), lambda s, p: (0, 0))],
        out_shape=[
            jax.ShapeDtypeStruct((2, HALF, 512), BF),
            jax.ShapeDtypeStruct((2, SEQ, 256), BF),
            jax.ShapeDtypeStruct((2, SEQ, 256), BF),
            jax.ShapeDtypeStruct((8, 256), F32),
        ],
        compiler_params=params(2),
        cost_estimate=cost(10**6, 10**6),
        name="attend_back",
    )(
        q_b, q_proj, k_b, k_proj, v_b, seg, branch_m, branch_o, w_out, attended,
        cosine, sine, heads,
    )


def weight_grads_kernel(
    place, normed, gq, gk, gv, branch_m, branch_o, mixed, router, gain, head_gains,
    out_0, out_1, out_2, out_3, out, sem,
):
    step = pl.program_id(0)
    rows = jnp.concatenate([normed[0], normed[1]], axis=0)
    own = jnp.concatenate([normed[0, 0:256, :], normed[1, 0:256, :]], axis=0)
    keys = jnp.concatenate(
        [
            jnp.concatenate([gk[0], gk[1]], axis=0),
            jnp.concatenate([gv[0], gv[1]], axis=0),
        ],
        axis=1,
    )
    queries = jnp.concatenate([gq[0], gq[1]], axis=0)
    branch = jnp.concatenate(
        [branch_m[0:128], branch_o[0:128], branch_m[128:256], branch_o[128:256]], axis=0
    )
    heads = jnp.concatenate([mixed[0], mixed[1]], axis=0)
    at = lax.broadcasted_iota(jnp.int32, (256, 256), 1)
    share = 4 * (at // HD + 4 * step) + at % HD
    spread = (lax.broadcasted_iota(jnp.int32, (256, 256), 0) % HD == share) & (at % HD < 4)
    spread = jnp.where(spread, 1.0, 0.0).astype(BF)
    high, low = split(head_gains[...])
    spread = dot(high, spread) + dot(low, spread)
    row = lax.broadcasted_iota(jnp.int32, (8, 256), 0)
    last = jnp.where(row == 0, gain[...], 0.0)
    last = last + jnp.where(row == 1, spread[0:1], 0.0) + jnp.where(row == 2, spread[1:2], 0.0)
    small = jnp.concatenate([router[...], last, jnp.zeros((88, 256), F32)], axis=0)
    parts = (
        (0, 512, dot_tn(own, queries).astype(BF)),
        (512, 1024, dot_tn(rows, keys).astype(BF)),
        (1024, 1536, dot_tn(branch, heads).astype(BF)),
        (1536, 1664, small.T.astype(BF)),
    )
    for i in range(4):
        to = place[4 * step + i]
        for low, high, value in parts:
            out[to, :, low:high] = value[i * 64 : i * 64 + 64]

    @pl.when(step == 3)
    def _():
        sends = [
            pltpu.make_async_copy(out.at[4 * i : 4 * i + 4], to, sem.at[i])
            for i, to in enumerate((out_0, out_1, out_2, out_3))
        ]
        for send in sends:
            send.start()
        for send in sends:
            send.wait()


def weight_grads(place, *args):
    fixed = lambda i, r: (0, 0, 0)
    column = pl.BlockSpec((HALF, 256), lambda i, r: (0, i))
    return pl.pallas_call(
        past(weight_grads_kernel, 11, len(args) - 10),
        grid_spec=pltpu.PrefetchScalarGridSpec(
            num_scalar_prefetch=1,
            grid=(4,),
            in_specs=[
                pl.BlockSpec((2, SEQ, 256), lambda i, r: (0, 0, i)),
                pl.BlockSpec((2, HALF, 512), fixed),
                pl.BlockSpec((2, SEQ, 256), fixed),
                pl.BlockSpec((2, SEQ, 256), fixed),
                column,
                column,
                pl.BlockSpec((2, HALF, 512), fixed),
                pl.BlockSpec((EXPERTS, 256), lambda i, r: (0, i)),
                pl.BlockSpec((1, 256), lambda i, r: (0, i)),
                pl.BlockSpec((8, 256), lambda i, r: (0, 0)),
            ]
            + [HBM] * (len(args) - 10),
            out_specs=[HBM] * 4,
            scratch_shapes=[pltpu.VMEM((N_FSDP, 64, 1664), BF), pltpu.SemaphoreType.DMA((4,))],
        ),
        out_shape=[jax.ShapeDtypeStruct((4, 64, 1664), BF)] * 4,
        compiler_params=params(1),
        cost_estimate=cost(10**6, 10**6),
        name="weight_grads",
    )(place, *args)


def input_grads_kernel(gq, gk, gv, w, mine, other):
    part = dot_nt(jnp.concatenate([gk[0], gv[0]], axis=1), w[:, 512:1024])
    own = dot_nt(gq[0], w[:, 0:512])
    for c in range(4):
        for parity, out in enumerate((mine, other)):
            at = slice(c * 256 + parity * 128, c * 256 + parity * 128 + 128)
            value = part[at] + own[at] if c == 0 else part[at]
            out[c] = value.astype(BF)


def input_grads(gq, gk, gv, weights, *others):
    by = lambda s: (s, 0, 0)
    half = pl.BlockSpec((4, 128, D), lambda s: (0, s, 0))
    return pl.pallas_call(
        past(input_grads_kernel, 4, len(others)),
        grid=(2,),
        in_specs=[
            pl.BlockSpec((1, HALF, 512), by),
            pl.BlockSpec((1, SEQ, 256), by),
            pl.BlockSpec((1, SEQ, 256), by),
            pl.BlockSpec((D, 1024), lambda s: (0, 0)),
        ]
        + [HBM] * len(others),
        out_specs=[half, half],
        out_shape=[jax.ShapeDtypeStruct((4, HALF, D), BF)] * 2,
        compiler_params=params(1),
        cost_estimate=cost(10**6, 10**6),
        name="input_grads",
    )(gq, gk, gv, weights, *others)


def finish_kernel(own, first, second, third, tokens, grad_hidden, small, out):
    values = tokens[...].astype(F32)
    factor = lax.rsqrt(jnp.mean(values * values, axis=1, keepdims=True) + EPS)
    summed = own[...].astype(F32) + first[...].astype(F32)
    summed = summed + (second[...].astype(F32) + third[...].astype(F32))
    weighted = summed * small[32:33, :]
    mean = jnp.mean(weighted * values, axis=1, keepdims=True)
    out[...] = grad_hidden[...] + factor * weighted - values * (factor * factor * factor * mean)


def finish(*args):
    return pl.pallas_call(
        past(finish_kernel, 7, len(args) - 7),
        in_specs=[pl.BlockSpec(memory_space=pltpu.VMEM)] * 7 + [HBM] * (len(args) - 7),
        out_shape=jax.ShapeDtypeStruct((HALF, D), F32),
        compiler_params=pltpu.CompilerParams(vmem_limit_bytes=VMEM),
        cost_estimate=cost(10**7, 6 * 10**6),
        name="finish",
    )(*args)


def settle_kernel(
    own, first, second, third, w_query, w_key, w_value, gain, g_query, g_key, g_value, g_out, sums
):
    summed = own[...].astype(F32) + first[...].astype(F32)
    summed = summed + (second[...].astype(F32) + third[...].astype(F32))
    g_query[...] = summed[:, 0:512]
    g_key[...] = summed[:, 512:768]
    g_value[...] = summed[:, 768:1024]
    g_out[...] = summed[:, 1024:1536]
    part = jnp.sum(w_query[...].astype(F32) * summed[:, 0:512], axis=1, keepdims=True)
    part = part + jnp.sum(w_key[...].astype(F32) * summed[:, 512:768], axis=1, keepdims=True)
    part = part + jnp.sum(w_value[...].astype(F32) * summed[:, 768:1024], axis=1, keepdims=True)
    diagonal = lax.broadcasted_iota(jnp.int32, (64, 64), 0) == lax.broadcasted_iota(
        jnp.int32, (64, 64), 1
    )
    column = jnp.sum(jnp.where(diagonal, gain[...].astype(F32), 0.0), axis=1, keepdims=True)
    lane = lax.broadcasted_iota(jnp.int32, (64, 128), 1)
    sums[...] = jnp.where(lane == 35, part / column, summed[:, 1536:1664])


def settle(*args):
    return pl.pallas_call(
        past(settle_kernel, 8, len(args) - 8),
        in_specs=[pl.BlockSpec(memory_space=pltpu.VMEM)] * 8 + [HBM] * (len(args) - 8),
        out_shape=[jax.ShapeDtypeStruct((64, n), F32) for n in (512, 256, 256, 512, 128)],
        compiler_params=pltpu.CompilerParams(vmem_limit_bytes=VMEM),
        cost_estimate=cost(10**6, 2 * 10**6),
        name="settle",
    )(*args)


def join_kernel(where, mine, far, out):
    @pl.when(pl.program_id(0) == 0)
    def _():
        out[...] = mine[...].reshape(2, 4, 1, 32, D)

    @pl.when(pl.program_id(0) == 1)
    def _():
        out[...] = far[...].reshape(2, 4, 1, 32, D)


def join(where, mine, far, *others):
    whole = pl.BlockSpec((HALF, D), lambda i, r: (0, 0))
    return pl.pallas_call(
        past(join_kernel, 3, len(others)),
        grid_spec=pltpu.PrefetchScalarGridSpec(
            num_scalar_prefetch=1,
            grid=(2,),
            in_specs=[whole, whole] + [HBM] * len(others),
            out_specs=pl.BlockSpec(
                (2, 4, 1, 32, D), lambda i, r: (0, 0, jnp.where(i == 0, r[0], 1 - r[0]), 0, 0)
            ),
        ),
        out_shape=jax.ShapeDtypeStruct((2, 4, 2, 32, D), mine.dtype),
        compiler_params=params(1),
        cost_estimate=cost(10**6, 4 * 10**6),
        name="join",
    )(where, mine, far, *others).reshape(2, 256, D)


def ring_pairs(stage, step):
    pairs = []
    for x in range(4):
        for z in range(4):
            for t in range(2):
                if (stage == 0) == (t == 0):
                    far = ((x + step) % 4) * 4 + z
                else:
                    far = x * 4 + (z + step) % 4
                pairs.append(((x * 4 + z) * 2 + t, far * 2 + t))
    return pairs


def ring(value, stage, step):
    return lax.ppermute(value, ("fsdp", "tensor"), ring_pairs(stage, step))


def shift(value, step):
    return lax.ppermute(value, "context", [(i, (i + step) % 4) for i in range(4)])


def swap_cores(value):
    return lax.ppermute(value, "tensor", [(0, 1), (1, 0)])


def gather_row(block, stage=0):
    return block, ring(block, stage, -1), ring(block, stage, 1), ring(block, stage, 2)


def gather_chunks(low, high):
    behind_low, ahead_high = ring(low, 1, 1), ring(high, 1, -1)
    behind_high, ahead_low = ring(high, 1, 1), ring(low, 1, -1)
    far = ring(behind_low, 1, 1), ring(ahead_high, 1, -1)
    return (low, high), (ahead_low, ahead_high), (behind_low, behind_high), far


def scatter_parts(parts, move):
    own, ahead, behind, far = parts
    return own, move(ahead, 1), move(behind, -1), move(far, 2)


def total_of(parts):
    first, second, third, fourth = (p.astype(F32) for p in parts)
    return (first + second) + (third + fourth)


def along(stage):
    return lambda v, n: ring(v, stage, n)


def local(
    tokens, segments, routes, attention_gain, w_query, w_key, w_value, w_out, query_gain,
    key_gain, feedforward_gain, router, w_gate, w_up, w_down, cotangent,
):
    f, c, t = lax.axis_index("fsdp"), lax.axis_index("context"), lax.axis_index("tensor")
    x_at, z_at = f // 4, f % 4
    steps = jnp.array([0, 1, 3, 2], jnp.int32)
    as_row = lambda *v: jnp.stack([jnp.asarray(i, jnp.int32) for i in v])
    all_x, all_z = (x_at + steps) % 4, (z_at + steps) % 4
    order = jnp.where(
        t == 0, all_x[None, :] * 4 + all_z[:, None], all_x[:, None] * 4 + all_z[None, :]
    ).astype(jnp.int32)
    far_x, far_z = steps[(jnp.arange(4) - x_at) % 4], steps[(jnp.arange(4) - z_at) % 4]
    place = jnp.where(
        t == 0, far_x[:, None] + 4 * far_z[None, :], 4 * far_x[:, None] + far_z[None, :]
    )
    place = place.reshape(-1).astype(jnp.int32)
    near = ((c + steps) % 4)[:, None] * 2 + jnp.stack([t, 1 - t])[None, :]
    near = near.reshape(8)

    shard = pack(
        as_row(f), w_query, w_key, w_value, w_out, router.T, attention_gain[None, :],
        feedforward_gain[None, :], query_gain[None, :], key_gain[None, :],
    )
    shards = jnp.stack(gather_row(shard))
    shards = gather_row(shards, 1)

    parity = lambda v, p: lax.dynamic_index_in_dim(
        v.reshape(2, 4, 2, 32, D), p, 2, keepdims=False
    ).reshape(HALF, D)
    tokens_m = parity(tokens, t)
    tokens_all = lax.all_gather(tokens_m, ("context", "tensor"), axis=0)
    picked = routes.reshape(ROWS, TOPK).T
    experts = jnp.arange(EXPERTS, dtype=jnp.int32)
    match = jnp.any(picked[:, None, :] == experts[None, :, None], axis=0)
    before = lambda n: (jnp.arange(n)[:, None] < jnp.arange(n)[None, :]).astype(BF)
    kept = match & (dot(match.astype(BF), before(ROWS)) < CAP)
    half = lambda v: lax.dynamic_index_in_dim(
        v.astype(F32).reshape(EXPERTS, 2, 4, 2, 32), t, 3, keepdims=False
    ).reshape(EXPERTS, HALF)
    match_half, kept_half = half(match), half(kept)
    local_place = dot(kept_half.astype(BF), before(HALF))
    table = experts_to_rows(jnp.where(kept_half > 0, local_place, -1.0).astype(BF))
    cot_payload = pack_cotangent(as_row(t), cotangent, table, *shards[1:])
    cot_row = gather_row(cot_payload)

    experts_w = [lax.all_gather(w, "tensor", axis=0) for w in (w_gate, w_up, w_down)]
    seg = segments.reshape(2, 4, 4, 2, 32).transpose(0, 1, 3, 2, 4).reshape(2, 8, 128)
    seg = jnp.take(seg, near, axis=1).reshape(2, 1, SEQ).astype(F32)

    cosine, sine = (jnp.asarray(v) for v in rotary_tables())
    weights, small, heads, cosine, sine, normed1, k_proj, k_b, v_b, q_proj, q_b = project(
        order.reshape(-1), near.astype(jnp.int32), tokens_all, shards, cosine, sine, seg
    )
    cot_chunks = gather_chunks(*stack_pairs(cot_row, small))
    attended, branch_m, branch_o = attend(q_b, k_b, v_b, seg, weights, cot_chunks[0][0])
    hidden1, payload, probs, totals = route(
        tokens_m, branch_m, swap_cores(branch_o), small, match_half, kept_half,
        *cot_chunks[1], *cot_chunks[2],
    )

    chunks = gather_chunks(*stack_pairs(gather_row(payload), *cot_chunks[3]))
    outs_x, more, counts, carried = {}, [], [], ()
    for slot, i in enumerate((0, 1, 3, 2)):
        where_at = as_row(f // 4, 2 * (f % 4), slot)
        result = expert_chunk(
            order[i], where_at, chunks[i], cot_chunks[i], experts_w, carried
        )
        carried = result[0], *result[2:5]
        outs_x[i] = result[1]
        more += result[5:8]
        counts.append(result[8])
    parts = scatter_parts([outs_x[i] for i in range(4)], along(1))
    grads_e = expert_weights(as_row(t), carried[1:], more, counts, parts[1], parts[3])
    back, grads_e = add_blocks(parts, (grads_e,))
    back = scatter_parts(back, along(0))

    grads_e = lax.psum_scatter(
        grads_e.reshape(8, 2, 256, 768), ("context", "tensor"), scatter_dimension=0
    )
    mixed, grad_hidden, grad_branch, grad_router, grad_gain2 = route_back(
        [carried[0]], *back, cot_payload, hidden1, small, payload, probs, totals, match_half
    )
    mixed = lax.psum_scatter(mixed, "fsdp", scatter_dimension=0)
    branch_far = swap_cores(grad_branch)
    gq, gk, gv, gains = attend_back(
        q_b, q_proj, k_b, k_proj, v_b, seg,
        grad_branch, branch_far, weights, attended, cosine, sine, heads,
    )
    gin_m, gin_o = input_grads(gq, gk, gv, weights)
    grads_w = weight_grads(
        place, normed1, gq, gk, gv, grad_branch, branch_far, attended, grad_router, grad_gain2, gains,
        gin_o, grads_e,
    )
    gin_far = swap_cores(gin_o)
    sent = [(gin_m[i].astype(F32) + gin_far[i].astype(F32)).astype(BF) for i in range(4)]
    gin = scatter_parts(sent, shift)
    both = lambda v, *others: join(as_row(t), v, swap_cores(v), *others)
    grad_tokens = both(finish(*gin, tokens_m, grad_hidden, small))

    grads_w = scatter_parts(grads_w, along(1))
    (grads_w,) = add_blocks(grads_w)
    grads_w = [v[None] for v in scatter_parts(grads_w, along(0))]
    ((grads_w,),) = add_blocks(grads_w)
    g_query, g_key, g_value, g_out, sums = settle(
        *scatter_parts([grads_w] * 4, shift), w_query, w_key, w_value, attention_gain[None, :],
    )
    sums = sums + swap_cores(sums)

    block_half = (hidden1 + mixed.astype(F32)).astype(BF)
    grads_e = grads_e.astype(F32)
    return (
        both(block_half),
        grad_tokens,
        sums[:, 35],
        g_query,
        g_key,
        g_value,
        g_out,
        sums[0:4, 33],
        sums[0:4, 34],
        sums[:, 32],
        sums[:, 0:32],
        grads_e[:, :, 0:256],
        grads_e[:, :, 256:512],
        grads_e[:, :, 512:768],
    )


def solution(mesh):
    in_specs = (
        P("fsdp", "context", None),
        P("fsdp", None),
        P("fsdp", "context", None),
        P("fsdp"),
        P("fsdp", "tensor"),
        P("fsdp", "tensor"),
        P("fsdp", "tensor"),
        P("fsdp", "tensor"),
        P("fsdp"),
        P("fsdp"),
        P("fsdp"),
        P("fsdp", None),
        P("fsdp", None, "tensor"),
        P("fsdp", None, "tensor"),
        P("fsdp", None, "tensor"),
        P("fsdp", "context", None),
    )
    out_specs = (
        P("fsdp", "context", None),
        P("fsdp", "context", None),
        P("fsdp"),
        P("fsdp", "tensor"),
        P("fsdp", "tensor"),
        P("fsdp", "tensor"),
        P("fsdp", "tensor"),
        P("fsdp"),
        P("fsdp"),
        P("fsdp"),
        P("fsdp", None),
        P("fsdp", "context", "tensor"),
        P("fsdp", "context", "tensor"),
        P("fsdp", "context", "tensor"),
    )
    return jax.shard_map(local, mesh=mesh, in_specs=in_specs, out_specs=out_specs, check_vma=False)
```
